128 devices in a mesh: fsdp: 128 (over z, x, y, core).
Axes of the slice: x: 4, y: 4, z: 4, core: 2. Of those that a mesh axis runs over, the one named last changes fastest.
Arguments:
- inputs: bfloat16 [30720, 960], P('fsdp'), may hold values from -6 to 6
- cotangent: bfloat16 [30720, 960], P('fsdp'), may hold values from -16 to 16
- flat_weights: bfloat16 [9832320], P('fsdp')
- counts: int32 [384], P('fsdp'), may hold values from 40 to 80, as said below
- segments: int32 [30720], P('fsdp'), may hold values from -1 to 2, as said below
Outputs:
- block_out: bfloat16 [30720, 960], P('fsdp')
- input_grad: bfloat16 [30720, 960], P('fsdp')
- flat_grads: float32 [9832320], P('fsdp')
The draws below stay inside these ranges and needn't reach their ends.
Inputs may be any that keep to these rules, and one draw needn't show every extreme that they name: `counts`: one micro-batch in every draw has all 80 rows live and another has exactly 40. `segments`: within a micro-batch the ids never fall over its live rows, which are its first counts rows; ids 0, 1 and 2 each mark one sequence; rows after the live ones hold -1.
All inputs are finite; a program needn't handle non-finite values.
Results may differ from the reference program's by a relative error of at most 0.011.
Values may be sent and summed in bfloat16 or wider, within the bound.
A program may use at most 256 MiB of HBM per device.

```python
import math
import jax
import jax.numpy as jnp
from jax import lax

D = 960
H = 15
KV = 5
HD = 64
FF = 2560
TOK_MB = 80
MB = 3
TOKENS = 30720
PARAMS = 9832320
N_FSDP = 128


def micro_layout(key):
    block_count = N_FSDP * MB
    key_count, key_full, key_short, key_cut = jax.random.split(key, 4)
    live_counts = jax.random.randint(key_count, (block_count,), TOK_MB // 2, TOK_MB + 1)
    block_index = jnp.arange(block_count, dtype=jnp.int32)
    full_block = jax.random.randint(key_full, (), 0, block_count)
    short_block = (full_block + 1 + jax.random.randint(key_short, (), 0, block_count - 1)) % block_count
    live_counts = jnp.where(block_index == full_block, TOK_MB, live_counts)
    live_counts = jnp.where(block_index == short_block, TOK_MB // 2, live_counts)
    cut_points = jax.random.randint(key_cut, (block_count, 2), 1, TOK_MB // 2)
    row_index = jnp.arange(TOK_MB, dtype=jnp.int32)
    segment_ids = (row_index[None, :] >= cut_points[:, 0:1]).astype(jnp.int32) + (row_index[None, :] >= cut_points[:, 1:2]).astype(jnp.int32)
    segment_ids = jnp.where(row_index[None, :] < live_counts[:, None], segment_ids, -1)
    return (live_counts.astype(jnp.int32), segment_ids.reshape(-1).astype(jnp.int32))


def draw_counts(key, part):
    shared = micro_layout(key)
    return shared[0]


def draw_segments(key, part):
    shared = micro_layout(key)
    return shared[1]


def draw_flat_weights(key, part):
    key = jax.random.fold_in(key, 7)
    flat_index = jnp.arange(PARAMS, dtype=jnp.int32)
    start_qkv = 2 * D
    start_out = start_qkv + D * (H + 2 * KV) * HD
    start_in = start_out + D * D
    start_down = start_in + 2 * D * FF
    random_part = jax.random.normal(key, (PARAMS,), jnp.float32)
    entry_scale = jnp.where(flat_index < start_qkv, 0.2, jnp.where(flat_index < start_out, D ** (-0.5), jnp.where(flat_index < start_in, 2.0 * D ** (-0.5), jnp.where(flat_index < start_down, D ** (-0.5), 2.0 * FF ** (-0.5)))))
    offset = jnp.where(flat_index < start_qkv, 1.0, 0.0)
    return (offset + random_part * entry_scale).astype(jnp.bfloat16)


def strengthened(values, stream_key, source, target, parts, factor):
    owner, partner = [(jnp.arange(values.shape[dim]) // (values.shape[dim] // parts)).reshape([-1 if axis == dim else 1 for axis in range(values.ndim)]) for dim in (source, target)]
    chosen = jax.random.permutation(stream_key, parts)[partner]
    strong = (owner == chosen) | (owner == (partner + parts // 2) % parts)
    return jnp.where(strong, factor * values, values)


def block_scale(key, shape, shards, least, largest):
    def one(dim, shards_of):
        draws = jax.random.uniform(jax.random.fold_in(jax.random.fold_in(key, 6), dim), (shards_of,), jnp.float32, least / len(shards), largest / len(shards))
        return jnp.repeat(jnp.exp(draws), shape[dim] // shards_of).reshape((-1,) + (1,) * (len(shape) - dim - 1))

    loudness = one(*shards[0])
    for cut in shards[1:]:
        loudness = loudness * one(*cut)
    return loudness


def centred(own_key, extent, spread, reach, pieces=(), kind=jnp.bfloat16):
    entries = spread * jax.random.normal(own_key, extent, jnp.float32)
    if pieces:
        entries = entries * block_scale(own_key, extent, pieces, -0.22, 0.18)
    return jnp.clip(entries, -reach, reach).astype(kind)


def bell_draw_with(own_key, shape, width, bound, cuts, heavy, held_as=jnp.bfloat16):
    entries = width * jax.random.normal(own_key, shape, jnp.float32)
    if cuts:
        entries = entries * block_scale(own_key, shape, cuts, -0.22, 0.18)
    return jnp.clip(strengthened(entries, jax.random.fold_in(own_key, 3), *heavy), -bound, bound).astype(held_as)


def setup_inputs(seed: int = 0) -> dict:
    arg_keys = jax.random.split(jax.random.key(seed), 6)
    return {
        "inputs": centred(arg_keys[0], (TOKENS, D), 1.0, 6.0, ((0, 128),)),
        "cotangent": bell_draw_with(arg_keys[1], (TOKENS, D), 1.0, 16.0, ((0, 128),), (0, 1, 64, 4.0)),
        "flat_weights": draw_flat_weights(jax.random.fold_in(arg_keys[5], 71), 0),
        "counts": draw_counts(jax.random.fold_in(arg_keys[5], 71), 0),
        "segments": draw_segments(jax.random.fold_in(arg_keys[5], 71), 0),
    }


@jax.custom_vjp
def low(v):
    return lax.optimization_barrier(v.astype(jnp.bfloat16)).astype(jnp.float32)

@jax.custom_vjp
def low_back(v):
    return v

def low_keep(v):
    return (low(v), None)

def low_pass(kept, grad):
    return (grad,)

def back_keep(v):
    return (v, None)

def back_low(kept, grad):
    return (low(grad),)
low.defvjp(low_keep, low_pass)
low_back.defvjp(back_keep, back_low)
EPSILON = 1e-05
HIGHEST = lax.Precision.HIGHEST

def unpack(flat_vector):
    width_qkv = (H + 2 * KV) * HD
    start_qkv = 2 * D
    start_out = start_qkv + D * width_qkv
    start_in = start_out + D * D
    start_down = start_in + 2 * D * FF
    gain_attn = flat_vector[0:D]
    gain_mlp = flat_vector[D:start_qkv]
    w_qkv = flat_vector[start_qkv:start_out].reshape(D, width_qkv)
    w_out = flat_vector[start_out:start_in].reshape(D, D)
    w_in = flat_vector[start_in:start_down].reshape(D, 2 * FF)
    w_down = flat_vector[start_down:start_down + FF * D].reshape(FF, D)
    return (gain_attn, gain_mlp, w_qkv, w_out, w_in, w_down)

def tables(segment_ids):
    length = segment_ids.shape[0]
    places = jnp.arange(length, dtype=jnp.int32)
    same_doc = segment_ids[:, None] == segment_ids[None, :]
    first_row = lax.optimization_barrier(jnp.min(jnp.where(same_doc, places[None, :], length), axis=1))
    position = (places - first_row).astype(jnp.float32)
    freq = jnp.exp(jnp.arange(HD // 2, dtype=jnp.float32) * (-2.0 * math.log(10000.0) / HD))
    angle = position[:, None] * freq[None, :]
    allowed = same_doc & (places[None, :] <= places[:, None])
    return (jnp.cos(angle), jnp.sin(angle), allowed)

def rotate(heads, cos_table, sin_table):
    half_width = HD // 2
    first_half = heads[..., :half_width]
    second_half = heads[..., half_width:]
    cos_part = cos_table[:, None, :]
    sin_part = sin_table[:, None, :]
    return jnp.concatenate([first_half * cos_part - second_half * sin_part, second_half * cos_part + first_half * sin_part], axis=-1)

def matmul(left, right):
    return jnp.dot(left, right, precision=HIGHEST, preferred_element_type=jnp.float32)

def rms_norm(values, gain):
    return values * lax.rsqrt(lax.optimization_barrier(jnp.mean(values * values, axis=-1, keepdims=True)) + EPSILON) * gain

def forward(flat_vector, residual, segment_ids, live_rows):
    gain_attn, gain_mlp, w_qkv, w_out, w_in, w_down = unpack(flat_vector)
    cos_table, sin_table, allowed = tables(segment_ids)
    length = residual.shape[0]
    group_size = H // KV
    normed = low(rms_norm(residual, gain_attn))
    qkv = low_back(matmul(normed, w_qkv))
    queries = low(rotate(qkv[:, :H * HD].reshape(length, H, HD), cos_table, sin_table))
    queries = queries.reshape(length, KV, group_size, HD)
    key_rows = low(rotate(qkv[:, H * HD:(H + KV) * HD].reshape(length, KV, HD), cos_table, sin_table))
    values = low(qkv[:, (H + KV) * HD:].reshape(length, KV, HD))
    scores = low_back(jnp.einsum('qkgd,pkd->kgqp', queries, key_rows, precision=HIGHEST) * 0.125)
    scores = jnp.where(allowed, scores, -1e+30)
    attention = low(jax.nn.softmax(scores, axis=-1))
    mixed_heads = jnp.einsum('kgqp,pkd->qkgd', attention, values, precision=HIGHEST).reshape(length, D)
    mixed_heads = low_back(low(mixed_heads))
    middle = residual + low_back(matmul(mixed_heads, w_out))
    normed_two = low(rms_norm(middle, gain_mlp))
    gate_up = low_back(matmul(normed_two, w_in))
    hidden = low(jax.nn.silu(gate_up[:, :FF]) * gate_up[:, FF:])
    return (middle + matmul(hidden, w_down)) * live_rows[:, None]

def reference(inputs, cotangent, flat_weights, counts, segments):
    flat_vector = flat_weights.astype(jnp.float32)
    block_count = N_FSDP * MB
    input_blocks = inputs.astype(jnp.float32).reshape(block_count, TOK_MB, D)
    grad_blocks = cotangent.astype(jnp.float32).reshape(block_count, TOK_MB, D)
    segment_blocks = segments.reshape(block_count, TOK_MB)
    places = jnp.arange(TOK_MB, dtype=jnp.int32)

    def step_block(running, item):
        residual, grad_rows, segment_ids, live_count = item
        live_rows = (places < live_count).astype(jnp.float32)
        result, pull_back = jax.vjp(lambda params, rows: forward(params, rows, segment_ids, live_rows), flat_vector, residual)
        grad_flat, grad_input = pull_back(grad_rows)
        return (running + grad_flat, (result.astype(jnp.bfloat16), grad_input.astype(jnp.bfloat16)))
    running = jnp.zeros(flat_vector.shape, jnp.float32)
    running, (results, grads) = lax.scan(step_block, running, (input_blocks, grad_blocks, segment_blocks, counts))
    return (results.reshape(-1, D), grads.reshape(-1, D), running)
```

```python
import functools
import math

import jax
import jax.numpy as jnp
from jax import lax
from jax.experimental import pallas as pl
from jax.experimental.pallas import tpu as pltpu
from jax.sharding import PartitionSpec as P

D = 960
H = 15
KV = 5
HD = 64
FF = 2560
MB = 3
EPSILON = 1e-05
GAINS = 2 * D
BLOCK = 76800
N = 128
BF = jnp.bfloat16
F32 = jnp.float32

MESH = pl.DeviceIdType.MESH
TILES = 40
PARTS = ((0, 7, 14), (14, 20, 27), (27, 33, 40))


def place():
    me = lax.axis_index("fsdp")
    return [me // 32, (me // 8) % 4, (me // 2) % 4], me % 2


def device_at(coords, core):
    return (coords[0] * 32 + coords[1] * 8 + coords[2] * 2 + core,)


def moved(coords, dim, by):
    out = list(coords)
    out[dim] = (out[dim] + by + 4) % 4
    return out


def greet(coords, core):
    barrier = pltpu.get_barrier_semaphore()
    for dim in range(3):
        for by in (1, -1):
            pl.semaphore_signal(barrier, inc=1, device_id=device_at(moved(coords, dim, by), core), device_id_type=MESH)
    pl.semaphore_signal(barrier, inc=1, device_id=device_at(coords, 1 - core), device_id_type=MESH)
    pl.semaphore_wait(barrier, 7)


def gather_kernel(blk, out, send, recv, pair_send, pair_recv, own_sem):
    coords, core = place()
    greet(coords, core)
    sent = []

    def at(whole, fixed, tiles):
        index = [slice(None)] * 3
        for dim, value in fixed.items():
            index[dim] = value
        return whole.at[(*index, core, pl.ds(tiles[0], tiles[1] - tiles[0]))]

    def push(src, dst, device, ssem, rsem):
        copy = pltpu.make_async_remote_copy(src_ref=src, dst_ref=dst, send_sem=ssem, recv_sem=rsem, device_id=device, device_id_type=MESH)
        copy.start()
        sent.append(copy)

    def landed(dst, rsem):
        pltpu.make_async_copy(dst, dst, rsem).wait()

    own = {0: coords[0], 1: coords[1], 2: coords[2]}
    here = out.at[(*coords, core)]
    local = pltpu.make_async_copy(blk, here, own_sem)
    local.start()
    sibling = device_at(coords, 1 - core)
    push(blk, here, sibling, pair_send.at[36], pair_recv.at[36])

    def orders(p):
        return [(p + k) % 3 for k in range(3)]

    def halves(p, sign):
        lo, mid, hi = PARTS[p]
        first, second = (lo, mid), (mid, hi)
        return (first, second) if sign > 0 else (second, first)

    def fixed_at(p, phase, coord):
        fixed = {orders(p)[phase]: coord}
        for later in range(phase + 1, 3):
            fixed[orders(p)[later]] = coords[orders(p)[later]]
        return fixed

    def base(p, phase, sign):
        return ((p * 3 + phase) * 2 + (0 if sign > 0 else 1)) * 3

    def pair_base(p, phase):
        return (p * 3 + phase) * 4

    for phase in range(3):
        for half in range(2):
            for p in range(3):
                dim = orders(p)[phase]
                for sign in (1, -1):
                    tiles = halves(p, sign)[half]
                    ref = at(out, fixed_at(p, phase, coords[dim]), tiles)
                    src = blk.at[pl.ds(tiles[0], tiles[1] - tiles[0])] if phase == 0 else ref
                    k = base(p, phase, sign) + half
                    push(src, ref, device_at(moved(coords, dim, sign), core), send.at[k], recv.at[k])
        for p in range(3):
            dim = orders(p)[phase]
            for sign in (1, -1):
                tiles = halves(p, sign)[0]
                coord = moved(coords, dim, -sign)[dim]
                ref = at(out, fixed_at(p, phase, coord), tiles)
                k = base(p, phase, sign)
                landed(ref, recv.at[k])
                push(ref, ref, device_at(moved(coords, dim, sign), core), send.at[k + 2], recv.at[k + 2])
        for p in range(3):
            dim = orders(p)[phase]
            for n, sign in enumerate((1, -1)):
                tiles = halves(p, sign)[1]
                coord = moved(coords, dim, -sign)[dim]
                landed(at(out, fixed_at(p, phase, coord), tiles), recv.at[base(p, phase, sign) + 1])
                lo, mid, hi = PARTS[p]
                ref = at(out, fixed_at(p, phase, coord), (lo, hi))
                m = pair_base(p, phase) + n
                push(ref, ref, sibling, pair_send.at[m], pair_recv.at[m])
        for p in range(3):
            dim = orders(p)[phase]
            coord = moved(coords, dim, 2)[dim]
            for n, sign in enumerate((1, -1)):
                tiles = halves(p, sign)[0]
                ref = at(out, fixed_at(p, phase, coord), tiles)
                landed(ref, recv.at[base(p, phase, sign) + 2])
                m = pair_base(p, phase) + 2 + n
                push(ref, ref, sibling, pair_send.at[m], pair_recv.at[m])
        if phase == 0:
            local.wait()

    other = 1 - core

    def theirs(whole, fixed, tiles):
        index = [slice(None)] * 3
        for dim, value in fixed.items():
            index[dim] = value
        return whole.at[(*index, other, pl.ds(tiles[0], tiles[1] - tiles[0]))]

    landed(out.at[(*coords, other)], pair_recv.at[36])
    for phase in range(3):
        for p in range(3):
            dim = orders(p)[phase]
            lo, mid, hi = PARTS[p]
            for n, sign in enumerate((1, -1)):
                coord = moved(coords, dim, -sign)[dim]
                landed(theirs(out, fixed_at(p, phase, coord), (lo, hi)), pair_recv.at[pair_base(p, phase) + n])
            coord = moved(coords, dim, 2)[dim]
            for n, sign in enumerate((1, -1)):
                landed(theirs(out, fixed_at(p, phase, coord), halves(p, sign)[0]), pair_recv.at[pair_base(p, phase) + 2 + n])
    for copy in sent:
        copy.wait_send()


def gather(block):
    return pl.pallas_call(
        gather_kernel,
        out_shape=jax.ShapeDtypeStruct((4, 4, 4, 2, TILES, 16, 128), jnp.bfloat16),
        in_specs=[pl.BlockSpec(memory_space=pl.ANY)],
        out_specs=pl.BlockSpec(memory_space=pl.ANY),
        scratch_shapes=[
            pltpu.SemaphoreType.DMA((54,)),
            pltpu.SemaphoreType.DMA((54,)),
            pltpu.SemaphoreType.DMA((37,)),
            pltpu.SemaphoreType.DMA((37,)),
            pltpu.SemaphoreType.DMA,
        ],
        compiler_params=pltpu.CompilerParams(collective_id=0, has_side_effects=True),
    )(block)


def scatter_kernel(grads, out, mine, pair_buf, b1, b2, b3, send, recv, pair_send, pair_recv, own_sem):
    coords, core = place()
    greet(coords, core)
    other = 1 - core
    sibling = device_at(coords, other)
    bufs = (b1, b2, b3)
    sent = []

    def orders(p):
        return [(p + k) % 3 for k in range(3)]

    def index_of(fixed):
        index = [slice(None)] * 3
        for dim, value in fixed.items():
            index[dim] = value
        return tuple(index)

    def rng(tiles):
        return pl.ds(tiles[0], tiles[1] - tiles[0])

    def halves(p, sign):
        lo, mid, hi = PARTS[p]
        first, second = (lo, mid), (mid, hi)
        return (first, second) if sign > 0 else (second, first)

    def push(src, dst, device, ssem, rsem):
        copy = pltpu.make_async_remote_copy(src_ref=src, dst_ref=dst, send_sem=ssem, recv_sem=rsem, device_id=device, device_id_type=MESH)
        copy.start()
        sent.append(copy)

    def landed(dst, rsem):
        pltpu.make_async_copy(dst, dst, rsem).wait()

    order = (2, 1, -1, 0)
    local = {}
    for step in order:
        for p in range(3):
            dim = orders(p)[0]
            lo, mid, hi = PARTS[p]
            fixed = index_of({dim: moved(coords, dim, step)[dim]})
            k = p * 4 + step % 4
            push(grads.at[(*fixed, other, rng((lo, hi)))], pair_buf.at[(*fixed, rng((lo, hi)))], sibling, pair_send.at[k], pair_recv.at[k])
            copy = pltpu.make_async_copy(grads.at[(*fixed, core, rng((lo, hi)))], mine.at[(*fixed, rng((lo, hi)))], own_sem.at[k])
            copy.start()
            local[k] = copy

    def ready(p, step):
        dim = orders(p)[0]
        lo, mid, hi = PARTS[p]
        n = hi - lo
        coord = moved(coords, dim, step)[dim]
        fixed = index_of({dim: coord})
        k = p * 4 + step % 4
        local[k].wait()
        landed(pair_buf.at[(*fixed, rng((lo, hi)))], pair_recv.at[k])

        def body(t, _):
            index = [t // 4, t % 4]
            index.insert(dim, coord)
            where = (*index, rng((lo, hi)))
            mine[where] = mine[where] + pair_buf[where]
            return 0

        lax.fori_loop(0, 16, body, 0)

    def fixed_at(p, phase, coord):
        fixed = {}
        for earlier in range(phase):
            fixed[orders(p)[earlier]] = coords[orders(p)[earlier]]
        fixed[orders(p)[phase]] = coord
        return fixed

    def base(p, phase, sign):
        return ((p * 3 + phase) * 2 + (0 if sign > 0 else 1)) * 3

    def slot(phase, which, tiles):
        return bufs[phase].at[(which, *([slice(None)] * (2 - phase)), rng(tiles))]

    def ship(p, phase, sign, step, half, number):
        dim = orders(p)[phase]
        tiles = halves(p, sign)[half]
        fixed = index_of(fixed_at(p, phase, moved(coords, dim, step)[dim]))
        k = base(p, phase, sign) + number
        side = 0 if sign > 0 else 1
        which = 2 + side if number == 0 else side
        push(mine.at[(*fixed, rng(tiles))], slot(phase, which, tiles), device_at(moved(coords, dim, sign), core), send.at[k], recv.at[k])

    def loop(phase, p, coord, fn):
        dims = orders(p)
        if phase == 2:
            fn((*[coord if d == dims[2] else coords[d] for d in range(3)],), ())
            return
        free = [d for d in range(3) if d in dims[phase + 1:]]

        def body(t, _):
            inner = [t // 4, t % 4] if phase == 0 else [t]
            index = []
            for d in range(3):
                if d in free:
                    index.append(inner[free.index(d)])
                elif d == dims[phase]:
                    index.append(coord)
                else:
                    index.append(coords[d])
            fn(tuple(index), tuple(inner))
            return 0

        lax.fori_loop(0, 16 if phase == 0 else 4, body, 0)

    for phase in range(3):
        for p in range(3):
            if phase == 0:
                ready(p, 2)
            for sign in (1, -1):
                ship(p, phase, sign, 2, 0, 0)
        for p in range(3):
            for sign in (1, -1):
                if phase == 0:
                    ready(p, sign)
                ship(p, phase, sign, sign, 1, 1)
        for p in range(3):
            dim = orders(p)[phase]
            for side, sign in enumerate((1, -1)):
                tiles = halves(p, sign)[0]
                landed(slot(phase, 2 + side, tiles), recv.at[base(p, phase, sign)])
                coord = moved(coords, dim, sign)[dim]

                def fold(where, inner):
                    m = (*where, rng(tiles))
                    mine[m] = mine[m] + bufs[phase][(2 + side, *inner, rng(tiles))]

                loop(phase, p, coord, fold)
                ship(p, phase, sign, sign, 0, 2)
        for p in range(3):
            dim = orders(p)[phase]
            if phase == 0:
                ready(p, 0)
            for side, sign in enumerate((1, -1)):
                landed(slot(phase, side, halves(p, sign)[1]), recv.at[base(p, phase, sign) + 1])
                landed(slot(phase, side, halves(p, sign)[0]), recv.at[base(p, phase, sign) + 2])
            lo, mid, hi = PARTS[p]

            def total(where, inner):
                m = (*where, rng((lo, hi)))
                f = jnp.float32
                value = mine[m].astype(f) + bufs[phase][(0, *inner, rng((lo, hi)))].astype(f) + bufs[phase][(1, *inner, rng((lo, hi)))].astype(f)
                if phase == 2:
                    out[rng((lo, hi))] = value
                else:
                    mine[m] = value.astype(jnp.bfloat16)

            loop(phase, p, coords[dim], total)
    for copy in sent:
        copy.wait_send()


def scatter(grads):
    bf = jnp.bfloat16
    return pl.pallas_call(
        scatter_kernel,
        out_shape=jax.ShapeDtypeStruct((TILES, 16, 128), jnp.float32),
        in_specs=[pl.BlockSpec(memory_space=pl.ANY)],
        out_specs=pl.BlockSpec(memory_space=pltpu.VMEM),
        scratch_shapes=[
            pltpu.VMEM((4, 4, 4, TILES, 16, 128), bf),
            pltpu.VMEM((4, 4, 4, TILES, 16, 128), bf),
            pltpu.VMEM((4, 4, 4, TILES, 16, 128), bf),
            pltpu.VMEM((4, 4, TILES, 16, 128), bf),
            pltpu.VMEM((4, TILES, 16, 128), bf),
            pltpu.SemaphoreType.DMA((54,)),
            pltpu.SemaphoreType.DMA((54,)),
            pltpu.SemaphoreType.DMA((12,)),
            pltpu.SemaphoreType.DMA((12,)),
            pltpu.SemaphoreType.DMA((12,)),
        ],
        compiler_params=pltpu.CompilerParams(collective_id=1, has_side_effects=True, vmem_limit_bytes=60 * 1024 * 1024),
    )(grads)


def pack(rows_48, rows_80, rows_15, gains, d, dtype):
    qkv = jnp.pad(rows_48, ((0, 0), (0, 64))).reshape(3, 16, 13, 128).transpose(0, 2, 1, 3).reshape(39, 16, 128)
    qkv = jnp.concatenate([qkv, gains[None]], axis=0)
    square = jnp.pad(rows_80, ((0, 0), (0, 64))).reshape(5, 16, 8, 128).transpose(0, 2, 1, 3).reshape(40, 16, 128)
    wide = jnp.pad(rows_15, ((0, 1), (0, 0))).reshape(16, 40, 128).transpose(1, 0, 2)
    return jnp.where(d < 20, qkv, jnp.where((d >= 32) & (d < 96), wide, square)).astype(dtype)


def to_block(shard, d):
    following = lax.ppermute(shard[:GAINS], "fsdp", [(i, (i + N - 1) % N) for i in range(N)])
    flat = lax.dynamic_slice(jnp.concatenate([shard, following]), (GAINS - 15 * d,), (BLOCK,))
    gains = jnp.pad(shard[:GAINS], (0, 128)).reshape(16, 128)
    return pack(flat.reshape(48, 1600), flat.reshape(80, D), flat.reshape(15, 2 * FF), gains, d, BF)


def from_block(tiles, d):
    qkv = tiles[:39].reshape(3, 13, 16, 128).transpose(0, 2, 1, 3).reshape(48, 1664)[:, :1600].reshape(-1)
    square = tiles.reshape(5, 8, 16, 128).transpose(0, 2, 1, 3).reshape(80, 1024)[:, :D].reshape(-1)
    wide = tiles.transpose(1, 0, 2)[:15].reshape(-1)
    flat = jnp.where(d < 20, qkv, jnp.where((d >= 32) & (d < 96), wide, square))
    before = lax.ppermute(flat[BLOCK - GAINS :], "fsdp", [(i, (i + 1) % N) for i in range(N)])
    before = jnp.where(d == 0, tiles[39].reshape(-1)[:GAINS], before)
    return lax.dynamic_slice(jnp.concatenate([before, flat]), (15 * d,), (BLOCK + 15,))


def tables(segment_ids):
    length = segment_ids.shape[0]
    places = jnp.arange(length, dtype=jnp.int32)
    batch = places // (length // MB)
    same = (segment_ids[:, None] == segment_ids[None, :]) & (batch[:, None] == batch[None, :])
    first_row = jnp.min(jnp.where(same, places[None, :], length), axis=1)
    position = (places - first_row).astype(F32)
    freq = jnp.exp(jnp.arange(HD // 2, dtype=F32) * (-2.0 * math.log(10000.0) / HD))
    angle = position[:, None] * freq[None, :]
    return jnp.cos(angle), jnp.sin(angle), same & (places[None, :] <= places[:, None])


def rotate(heads, cos_table, sin_table):
    a, b = heads[..., : HD // 2], heads[..., HD // 2 :]
    cos_part, sin_part = cos_table[:, None, :], sin_table[:, None, :]
    return jnp.concatenate([a * cos_part - b * sin_part, b * cos_part + a * sin_part], axis=-1)


def dot(a, b, ca=1, cb=0):
    return lax.dot_general(a, b, (((ca,), (cb,)), ((), ())), preferred_element_type=F32)


def compute(blocks, inputs, cotangent, segments, counts):
    rows = inputs.shape[0]
    blocks = blocks.reshape(N, 40, 16, 128)
    w_qkv = blocks[:20, :39].reshape(60, 13, 16, 128).transpose(0, 2, 1, 3).reshape(D, 1664)[:, :1600]
    w_out = blocks[20:32].reshape(60, 8, 16, 128).transpose(0, 2, 1, 3).reshape(D, 1024)[:, :D]
    w_in = blocks[32:96].transpose(0, 2, 1, 3).reshape(64, 16, 2 * FF)[:, :15].reshape(D, 2 * FF)
    w_down = blocks[96:].reshape(160, 8, 16, 128).transpose(0, 2, 1, 3).reshape(FF, 1024)[:, :D]
    gains = blocks[0, 39].reshape(-1).astype(F32)
    gain_attn, gain_mlp = gains[:D], gains[D : 2 * D]
    places = jnp.arange(rows, dtype=jnp.int32)
    live = (places % (rows // MB) < jnp.repeat(counts, rows // MB)).astype(F32)[:, None]
    cos_t, sin_t, allowed = tables(segments)
    x = inputs.astype(F32)
    inv1 = lax.rsqrt(jnp.mean(x * x, axis=-1, keepdims=True) + EPSILON)
    n1 = x * inv1
    normed = (n1 * gain_attn).astype(BF)
    qkv = dot(normed, w_qkv)
    q = rotate(qkv[:, : H * HD].reshape(rows, H, HD), cos_t, sin_t).astype(BF).reshape(rows, KV, 3, HD)
    k = rotate(qkv[:, H * HD : 20 * HD].reshape(rows, KV, HD), cos_t, sin_t).astype(BF)
    v = qkv[:, 20 * HD :].reshape(rows, KV, HD).astype(BF)
    s = jnp.einsum("qkgd,pkd->kgqp", q, k, preferred_element_type=F32) * 0.125
    s = jnp.where(allowed, s, -1e30)
    e = jnp.exp(s - jnp.max(s, axis=-1, keepdims=True))
    probs = e / jnp.sum(e, axis=-1, keepdims=True)
    probs_b = probs.astype(BF)
    mixed = jnp.einsum("kgqp,pkd->qkgd", probs_b, v, preferred_element_type=F32).reshape(rows, D).astype(BF)
    middle = x + dot(mixed, w_out)
    inv2 = lax.rsqrt(jnp.mean(middle * middle, axis=-1, keepdims=True) + EPSILON)
    n2 = middle * inv2
    normed2 = (n2 * gain_mlp).astype(BF)
    gate_up = dot(normed2, w_in)
    gate, up = gate_up[:, :FF], gate_up[:, FF:]
    sg = jax.nn.sigmoid(gate)
    hidden = (gate * sg * up).astype(BF)
    block_out = ((middle + dot(hidden, w_down)) * live).astype(BF)
    g_out = (cotangent.astype(F32) * live).astype(BF)
    g_hidden = dot(g_out, w_down, 1, 1)
    d_down = dot(hidden, g_out, 0, 0)
    g_gate = g_hidden * up * sg * (1.0 + gate * (1.0 - sg))
    g_up = g_hidden * gate * sg
    g_gu = jnp.concatenate([g_gate, g_up], axis=1).astype(BF)
    d_in = dot(normed2, g_gu, 0, 0)
    g_n2 = dot(g_gu, w_in, 1, 1)
    d_gain2 = jnp.sum(g_n2 * n2, axis=0)
    u = g_n2 * gain_mlp
    g_mid = g_out.astype(F32) + inv2 * (u - n2 * jnp.mean(u * n2, axis=-1, keepdims=True))
    g_mid_r = g_mid.astype(BF)
    d_out = dot(mixed, g_mid_r, 0, 0)
    g_mixed = dot(g_mid_r, w_out, 1, 1).astype(BF).reshape(rows, KV, 3, HD)
    g_v = jnp.einsum("kgqp,qkgd->pkd", probs_b, g_mixed, preferred_element_type=F32)
    g_p = jnp.einsum("qkgd,pkd->kgqp", g_mixed, v, preferred_element_type=F32)
    g_s = (probs * (g_p - jnp.sum(probs * g_p, axis=-1, keepdims=True))).astype(BF)
    g_q = jnp.einsum("kgqp,pkd->qkgd", g_s, k, preferred_element_type=F32) * 0.125
    g_k = jnp.einsum("kgqp,qkgd->pkd", g_s, q, preferred_element_type=F32) * 0.125
    g_q = rotate(g_q.reshape(rows, H, HD), cos_t, -sin_t)
    g_k = rotate(g_k, cos_t, -sin_t)
    g_qkv = jnp.concatenate([g.reshape(rows, -1) for g in (g_q, g_k, g_v)], axis=1).astype(BF)
    d_qkv = dot(normed, g_qkv, 0, 0)
    g_normed = dot(g_qkv, w_qkv, 1, 1)
    d_gain1 = jnp.sum(g_normed * n1, axis=0)
    u = g_normed * gain_attn
    g_in = (g_mid + inv1 * (u - n1 * jnp.mean(u * n1, axis=-1, keepdims=True))).astype(BF)
    d_gains = jnp.pad(jnp.concatenate([d_gain1, d_gain2]), (0, 128)).reshape(1, 1, 16, 128)
    d_gains = jnp.pad(d_gains, ((0, 19), (0, 0), (0, 0), (0, 0)))
    t_qkv = jnp.pad(d_qkv, ((0, 0), (0, 64))).reshape(60, 16, 13, 128).transpose(0, 2, 1, 3).reshape(20, 39, 16, 128)
    t_qkv = jnp.concatenate([t_qkv, d_gains], axis=1)
    t_out = jnp.pad(d_out, ((0, 0), (0, 64))).reshape(60, 16, 8, 128).transpose(0, 2, 1, 3).reshape(12, 40, 16, 128)
    t_in = jnp.pad(d_in.reshape(64, 15, 2 * FF), ((0, 0), (0, 1), (0, 0))).reshape(64, 16, 40, 128).transpose(0, 2, 1, 3)
    t_down = jnp.pad(d_down, ((0, 0), (0, 64))).reshape(160, 16, 8, 128).transpose(0, 2, 1, 3).reshape(32, 40, 16, 128)
    terms = jnp.concatenate([t_qkv, t_out, t_in, t_down], axis=0).astype(BF)
    return block_out, g_in, terms


def shards(inputs, cotangent, flat_weights, counts, segments):
    d = lax.axis_index("fsdp")
    blocks = gather(to_block(flat_weights, d))
    block_out, input_grad, terms = compute(blocks, inputs, cotangent, segments, counts)
    return block_out, input_grad, from_block(scatter(terms.reshape(4, 4, 4, 2, TILES, 16, 128)), d)


def solution(mesh):
    in_specs = (P("fsdp", None), P("fsdp", None), P("fsdp"), P("fsdp"), P("fsdp"))
    out_specs = (P("fsdp", None), P("fsdp", None), P("fsdp"))
    return jax.shard_map(shards, mesh=mesh, in_specs=in_specs, out_specs=out_specs, check_vma=False)
```

```python
import functools
import math

import jax
import jax.numpy as jnp
from jax import lax
from jax.experimental import pallas as pl
from jax.experimental.pallas import tpu as pltpu
from jax.sharding import PartitionSpec as P

D = 960
H = 15
KV = 5
HD = 64
FF = 2560
MB = 3
EPSILON = 1e-05
GAINS = 2 * D
BLOCK = 76800
N = 128
BF = jnp.bfloat16
F32 = jnp.float32

MESH = pl.DeviceIdType.MESH
TILES = 40
PARTS = ((0, 7, 14), (14, 20, 27), (27, 33, 40))


def place():
    me = lax.axis_index("fsdp")
    return [me // 32, (me // 8) % 4, (me // 2) % 4], me % 2


def device_at(coords, core):
    return (coords[0] * 32 + coords[1] * 8 + coords[2] * 2 + core,)


def moved(coords, dim, by):
    out = list(coords)
    out[dim] = (out[dim] + by + 4) % 4
    return out


def greet(coords, core):
    barrier = pltpu.get_barrier_semaphore()
    for dim in range(3):
        for by in (1, -1):
            pl.semaphore_signal(barrier, inc=1, device_id=device_at(moved(coords, dim, by), core), device_id_type=MESH)
    pl.semaphore_signal(barrier, inc=1, device_id=device_at(coords, 1 - core), device_id_type=MESH)
    pl.semaphore_wait(barrier, 7)


def gather_kernel(blk, out, send, recv, pair_send, pair_recv, own_sem):
    coords, core = place()
    greet(coords, core)
    sent = []

    def at(whole, fixed, tiles):
        index = [slice(None)] * 3
        for dim, value in fixed.items():
            index[dim] = value
        return whole.at[(*index, core, pl.ds(tiles[0], tiles[1] - tiles[0]))]

    def push(src, dst, device, ssem, rsem):
        copy = pltpu.make_async_remote_copy(src_ref=src, dst_ref=dst, send_sem=ssem, recv_sem=rsem, device_id=device, device_id_type=MESH)
        copy.start()
        sent.append(copy)

    def landed(dst, rsem):
        pltpu.make_async_copy(dst, dst, rsem).wait()

    own = {0: coords[0], 1: coords[1], 2: coords[2]}
    here = out.at[(*coords, core)]
    local = pltpu.make_async_copy(blk, here, own_sem)
    local.start()
    sibling = device_at(coords, 1 - core)
    push(blk, here, sibling, pair_send.at[36], pair_recv.at[36])

    def orders(p):
        return [(p + k) % 3 for k in range(3)]

    def halves(p, sign):
        lo, mid, hi = PARTS[p]
        first, second = (lo, mid), (mid, hi)
        return (first, second) if sign > 0 else (second, first)

    def fixed_at(p, phase, coord):
        fixed = {orders(p)[phase]: coord}
        for later in range(phase + 1, 3):
            fixed[orders(p)[later]] = coords[orders(p)[later]]
        return fixed

    def base(p, phase, sign):
        return ((p * 3 + phase) * 2 + (0 if sign > 0 else 1)) * 3

    def pair_base(p, phase):
        return (p * 3 + phase) * 4

    for phase in range(3):
        for half in range(2):
            for p in range(3):
                dim = orders(p)[phase]
                for sign in (1, -1):
                    tiles = halves(p, sign)[half]
                    ref = at(out, fixed_at(p, phase, coords[dim]), tiles)
                    src = blk.at[pl.ds(tiles[0], tiles[1] - tiles[0])] if phase == 0 else ref
                    k = base(p, phase, sign) + half
                    push(src, ref, device_at(moved(coords, dim, sign), core), send.at[k], recv.at[k])
        for p in range(3):
            dim = orders(p)[phase]
            for sign in (1, -1):
                tiles = halves(p, sign)[0]
                coord = moved(coords, dim, -sign)[dim]
                ref = at(out, fixed_at(p, phase, coord), tiles)
                k = base(p, phase, sign)
                landed(ref, recv.at[k])
                push(ref, ref, device_at(moved(coords, dim, sign), core), send.at[k + 2], recv.at[k + 2])
        for p in range(3):
            dim = orders(p)[phase]
            for n, sign in enumerate((1, -1)):
                tiles = halves(p, sign)[1]
                coord = moved(coords, dim, -sign)[dim]
                landed(at(out, fixed_at(p, phase, coord), tiles), recv.at[base(p, phase, sign) + 1])
                lo, mid, hi = PARTS[p]
                ref = at(out, fixed_at(p, phase, coord), (lo, hi))
                m = pair_base(p, phase) + n
                push(ref, ref, sibling, pair_send.at[m], pair_recv.at[m])
        for p in range(3):
            dim = orders(p)[phase]
            coord = moved(coords, dim, 2)[dim]
            for n, sign in enumerate((1, -1)):
                tiles = halves(p, sign)[0]
                ref = at(out, fixed_at(p, phase, coord), tiles)
                landed(ref, recv.at[base(p, phase, sign) + 2])
                m = pair_base(p, phase) + 2 + n
                push(ref, ref, sibling, pair_send.at[m], pair_recv.at[m])
        if phase == 0:
            local.wait()

    other = 1 - core

    def theirs(whole, fixed, tiles):
        index = [slice(None)] * 3
        for dim, value in fixed.items():
            index[dim] = value
        return whole.at[(*index, other, pl.ds(tiles[0], tiles[1] - tiles[0]))]

    landed(out.at[(*coords, other)], pair_recv.at[36])
    for phase in range(3):
        for p in range(3):
            dim = orders(p)[phase]
            lo, mid, hi = PARTS[p]
            for n, sign in enumerate((1, -1)):
                coord = moved(coords, dim, -sign)[dim]
                landed(theirs(out, fixed_at(p, phase, coord), (lo, hi)), pair_recv.at[pair_base(p, phase) + n])
            coord = moved(coords, dim, 2)[dim]
            for n, sign in enumerate((1, -1)):
                landed(theirs(out, fixed_at(p, phase, coord), halves(p, sign)[0]), pair_recv.at[pair_base(p, phase) + 2 + n])
    for copy in sent:
        copy.wait_send()


def gather(block):
    return pl.pallas_call(
        gather_kernel,
        out_shape=jax.ShapeDtypeStruct((4, 4, 4, 2, TILES, 16, 128), jnp.bfloat16),
        in_specs=[pl.BlockSpec(memory_space=pl.ANY)],
        out_specs=pl.BlockSpec(memory_space=pl.ANY),
        scratch_shapes=[
            pltpu.SemaphoreType.DMA((54,)),
            pltpu.SemaphoreType.DMA((54,)),
            pltpu.SemaphoreType.DMA((37,)),
            pltpu.SemaphoreType.DMA((37,)),
            pltpu.SemaphoreType.DMA,
        ],
        compiler_params=pltpu.CompilerParams(collective_id=0, has_side_effects=True),
    )(block)


def scatter_kernel(grads, out, mine, pair_buf, b1, b2, b3, send, recv, pair_send, pair_recv, own_sem):
    coords, core = place()
    greet(coords, core)
    other = 1 - core
    sibling = device_at(coords, other)
    bufs = (b1, b2, b3)
    sent = []

    def orders(p):
        return [(p + k) % 3 for k in range(3)]

    def index_of(fixed):
        index = [slice(None)] * 3
        for dim, value in fixed.items():
            index[dim] = value
        return tuple(index)

    def rng(tiles):
        return pl.ds(tiles[0], tiles[1] - tiles[0])

    def halves(p, sign):
        lo, mid, hi = PARTS[p]
        first, second = (lo, mid), (mid, hi)
        return (first, second) if sign > 0 else (second, first)

    def push(src, dst, device, ssem, rsem):
        copy = pltpu.make_async_remote_copy(src_ref=src, dst_ref=dst, send_sem=ssem, recv_sem=rsem, device_id=device, device_id_type=MESH)
        copy.start()
        sent.append(copy)

    def landed(dst, rsem):
        pltpu.make_async_copy(dst, dst, rsem).wait()

    order = (2, 1, -1, 0)
    local = {}
    for step in order:
        for p in range(3):
            dim = orders(p)[0]
            lo, mid, hi = PARTS[p]
            fixed = index_of({dim: moved(coords, dim, step)[dim]})
            k = p * 4 + step % 4
            push(grads.at[(*fixed, other, rng((lo, hi)))], pair_buf.at[(*fixed, rng((lo, hi)))], sibling, pair_send.at[k], pair_recv.at[k])
            copy = pltpu.make_async_copy(grads.at[(*fixed, core, rng((lo, hi)))], mine.at[(*fixed, rng((lo, hi)))], own_sem.at[k])
            copy.start()
            local[k] = copy

    def ready(p, step):
        dim = orders(p)[0]
        lo, mid, hi = PARTS[p]
        n = hi - lo
        coord = moved(coords, dim, step)[dim]
        fixed = index_of({dim: coord})
        k = p * 4 + step % 4
        local[k].wait()
        landed(pair_buf.at[(*fixed, rng((lo, hi)))], pair_recv.at[k])

        def body(t, _):
            index = [t // 4, t % 4]
            index.insert(dim, coord)
            where = (*index, rng((lo, hi)))
            mine[where] = mine[where] + pair_buf[where]
            return 0

        lax.fori_loop(0, 16, body, 0)

    def fixed_at(p, phase, coord):
        fixed = {}
        for earlier in range(phase):
            fixed[orders(p)[earlier]] = coords[orders(p)[earlier]]
        fixed[orders(p)[phase]] = coord
        return fixed

    def base(p, phase, sign):
        return ((p * 3 + phase) * 2 + (0 if sign > 0 else 1)) * 3

    def slot(phase, which, tiles):
        return bufs[phase].at[(which, *([slice(None)] * (2 - phase)), rng(tiles))]

    def ship(p, phase, sign, step, half, number):
        dim = orders(p)[phase]
        tiles = halves(p, sign)[half]
        fixed = index_of(fixed_at(p, phase, moved(coords, dim, step)[dim]))
        k = base(p, phase, sign) + number
        side = 0 if sign > 0 else 1
        which = 2 + side if number == 0 else side
        push(mine.at[(*fixed, rng(tiles))], slot(phase, which, tiles), device_at(moved(coords, dim, sign), core), send.at[k], recv.at[k])

    def loop(phase, p, coord, fn):
        dims = orders(p)
        if phase == 2:
            fn((*[coord if d == dims[2] else coords[d] for d in range(3)],), ())
            return
        free = [d for d in range(3) if d in dims[phase + 1:]]

        def body(t, _):
            inner = [t // 4, t % 4] if phase == 0 else [t]
            index = []
            for d in range(3):
                if d in free:
                    index.append(inner[free.index(d)])
                elif d == dims[phase]:
                    index.append(coord)
                else:
                    index.append(coords[d])
            fn(tuple(index), tuple(inner))
            return 0

        lax.fori_loop(0, 16 if phase == 0 else 4, body, 0)

    for phase in range(3):
        for p in range(3):
            if phase == 0:
                ready(p, 2)
            for sign in (1, -1):
                ship(p, phase, sign, 2, 0, 0)
        for p in range(3):
            for sign in (1, -1):
                if phase == 0:
                    ready(p, sign)
                ship(p, phase, sign, sign, 1, 1)
        for p in range(3):
            dim = orders(p)[phase]
            for side, sign in enumerate((1, -1)):
                tiles = halves(p, sign)[0]
                landed(slot(phase, 2 + side, tiles), recv.at[base(p, phase, sign)])
                coord = moved(coords, dim, sign)[dim]

                def fold(where, inner):
                    m = (*where, rng(tiles))
                    mine[m] = mine[m] + bufs[phase][(2 + side, *inner, rng(tiles))]

                loop(phase, p, coord, fold)
                ship(p, phase, sign, sign, 0, 2)
        for p in range(3):
            dim = orders(p)[phase]
            if phase == 0:
                ready(p, 0)
            for side, sign in enumerate((1, -1)):
                landed(slot(phase, side, halves(p, sign)[1]), recv.at[base(p, phase, sign) + 1])
                landed(slot(phase, side, halves(p, sign)[0]), recv.at[base(p, phase, sign) + 2])
            lo, mid, hi = PARTS[p]

            def total(where, inner):
                m = (*where, rng((lo, hi)))
                f = jnp.float32
                value = mine[m].astype(f) + bufs[phase][(0, *inner, rng((lo, hi)))].astype(f) + bufs[phase][(1, *inner, rng((lo, hi)))].astype(f)
                if phase == 2:
                    out[rng((lo, hi))] = value
                else:
                    mine[m] = value.astype(jnp.bfloat16)

            loop(phase, p, coords[dim], total)
    for copy in sent:
        copy.wait_send()


def scatter(grads):
    bf = jnp.bfloat16
    return pl.pallas_call(
        scatter_kernel,
        out_shape=jax.ShapeDtypeStruct((TILES, 16, 128), jnp.float32),
        in_specs=[pl.BlockSpec(memory_space=pl.ANY)],
        out_specs=pl.BlockSpec(memory_space=pltpu.VMEM),
        scratch_shapes=[
            pltpu.VMEM((4, 4, 4, TILES, 16, 128), bf),
            pltpu.VMEM((4, 4, 4, TILES, 16, 128), bf),
            pltpu.VMEM((4, 4, 4, TILES, 16, 128), bf),
            pltpu.VMEM((4, 4, TILES, 16, 128), bf),
            pltpu.VMEM((4, TILES, 16, 128), bf),
            pltpu.SemaphoreType.DMA((54,)),
            pltpu.SemaphoreType.DMA((54,)),
            pltpu.SemaphoreType.DMA((12,)),
            pltpu.SemaphoreType.DMA((12,)),
            pltpu.SemaphoreType.DMA((12,)),
        ],
        compiler_params=pltpu.CompilerParams(collective_id=1, has_side_effects=True, vmem_limit_bytes=60 * 1024 * 1024),
    )(grads)


def pack(rows_48, rows_80, rows_15, gains, d):
    qkv = jnp.pad(rows_48, ((0, 0), (0, 64))).reshape(3, 16, 13, 128).transpose(2, 0, 1, 3).reshape(39, 16, 128)
    qkv = jnp.concatenate([qkv, jnp.where(d == 0, gains, jnp.zeros_like(gains))[None]], axis=0)
    square = jnp.pad(rows_80, ((0, 0), (0, 64))).reshape(5, 16, 8, 128).transpose(2, 0, 1, 3).reshape(40, 16, 128)
    wide = jnp.pad(rows_15, ((0, 1), (0, 0))).reshape(16, 40, 128).transpose(1, 0, 2)
    return jnp.where(d < 20, qkv, jnp.where((d >= 32) & (d < 96), wide, square))


def to_block(shard, d):
    following = lax.ppermute(shard[:GAINS], "fsdp", [(i, (i + N - 1) % N) for i in range(N)])
    flat = lax.dynamic_slice(jnp.concatenate([shard, following]), (GAINS - 15 * d,), (BLOCK,))
    gains = jnp.pad(shard[:GAINS].reshape(2, D), ((0, 0), (0, 64))).reshape(16, 128)
    return pack(flat.reshape(48, 1600), flat.reshape(80, D), flat.reshape(15, 2 * FF), gains, d)


def from_block(tiles, d):
    qkv = tiles[:39].reshape(13, 3, 16, 128).transpose(1, 2, 0, 3).reshape(48, 1664)[:, :1600].reshape(-1)
    square = tiles.reshape(8, 5, 16, 128).transpose(1, 2, 0, 3).reshape(80, 1024)[:, :D].reshape(-1)
    wide = tiles.transpose(1, 0, 2)[:15].reshape(-1)
    flat = jnp.where(d < 20, qkv, jnp.where((d >= 32) & (d < 96), wide, square))
    before = lax.ppermute(flat[BLOCK - GAINS :], "fsdp", [(i, (i + 1) % N) for i in range(N)])
    before = jnp.where(d == 0, tiles[39].reshape(2, 1024)[:, :D].reshape(-1), before)
    return lax.dynamic_slice(jnp.concatenate([before, flat]), (15 * d,), (BLOCK + 15,))


ROWS = 240
MROWS = 80


def tables(segment_ids, counts):
    seg = segment_ids.reshape(MB, MROWS)
    places = jnp.arange(MROWS, dtype=jnp.int32)
    same = seg[:, :, None] == seg[:, None, :]
    first_row = jnp.min(jnp.where(same, places[None, None, :], MROWS), axis=2)
    position = (places[None, :] - first_row).astype(F32).reshape(ROWS)
    freq = jnp.exp(jnp.arange(HD // 2, dtype=F32) * (-2.0 * math.log(10000.0) / HD))
    angle = position[:, None] * freq[None, :]
    cos, sin = jnp.cos(angle), jnp.sin(angle)
    cos_t = jnp.concatenate([cos, cos, cos, cos], axis=1)
    sin_t = jnp.concatenate([-sin, sin, -sin, sin], axis=1)
    allowed = same & (places[None, None, :] <= places[None, :, None])
    bias = jnp.where(allowed, 0.0, -1e30).astype(F32).reshape(ROWS, MROWS)
    live = (places[None, :] < counts[:, None]).astype(F32).reshape(ROWS, 1)
    return cos_t, sin_t, bias, jnp.broadcast_to(live, (ROWS, 128))


def dot(a, b, ca=1, cb=0):
    return lax.dot_general(a, b, (((ca,), (cb,)), ((), ())), preferred_element_type=F32)


def mean_of(value):
    return jnp.sum(value, axis=-1, keepdims=True) * (1.0 / D)


def compute_kernel(
    blocks, x_ref, c_ref, cos_ref, sin_ref, bias_ref, live_ref,
    out_ref, gin_ref, terms,
    w, xs, go, nrm, qs, kk, vv, prob, mixed, mid, n2p, gate, up, hid, ggu, gq, gqb, spread, acc, in_sem, out_sem,
):
    spans = ((0, 20), (20, 32), (32, 96), (96, 128))

    def span(ref, i):
        return ref.at[pl.ds(spans[i][0], spans[i][1] - spans[i][0])]

    loads = [pltpu.make_async_copy(span(blocks, i), span(w, i), in_sem.at[i]) for i in range(4)]
    stores = [pltpu.make_async_copy(span(w, i), span(terms, i), out_sem.at[i]) for i in range(4)]
    for load in loads:
        load.start()

    def qkv_tiles(c):
        return w[0:20, 3 * c : 3 * c + 3].reshape(D, 128)

    def out_tiles(c):
        return w[20:32, 5 * c : 5 * c + 5].reshape(D, 128)

    def side(parts):
        return jnp.concatenate(parts, axis=1)

    def in_tiles(c):
        return side([w[32:96, 5 * c + i].reshape(1024, 128) for i in range(5)])

    def down_tiles(c):
        return side([w[pl.ds(96 + 8 * c, 8), 5 * i : 5 * i + 5].reshape(640, 128) for i in range(8)])

    lane = lax.broadcasted_iota(jnp.int32, (MROWS, 128), 1)
    half = (lane < 64, lane >= 64)
    lane_all = lax.broadcasted_iota(jnp.int32, (ROWS, 128), 1)
    low_all = lane_all < 64
    first_all = lane_all % 64 < 32

    def swap(v):
        return jnp.where(first_all, pltpu.roll(v, 96, 1), pltpu.roll(v, 32, 1))

    def both(v, h):
        other = pltpu.roll(v, 64, 1)
        return jnp.where(low_all, v, other) if h == 0 else jnp.where(low_all, other, v)

    r = lax.broadcasted_iota(jnp.int32, (1024, 1024), 0)
    c = lax.broadcasted_iota(jnp.int32, (1024, 1024), 1)
    spread[...] = jnp.where((r == (c // 16) * 15 + c % 16) & (c % 16 != 15), 1.0, 0.0).astype(BF)

    xs[:, 896:1024] = jnp.zeros((ROWS, 128), F32)
    xs[:, 0:D] = x_ref[...].astype(F32)
    go[:, 896:1024] = jnp.zeros((ROWS, 128), BF)
    live = live_ref[:, 0:1]
    go[:, 0:D] = (c_ref[...].astype(F32) * live).astype(BF)
    x = xs[...]
    inv1 = lax.rsqrt(mean_of(x * x) + EPSILON)
    loads[0].wait()
    gains = w[0, 39].astype(F32)
    gain1 = side([gains[i : i + 1] for i in range(8)])
    gain2 = side([gains[8 + i : 9 + i] for i in range(8)])
    nrm[...] = (x * inv1 * gain1).astype(BF)

    cos_t, sin_t = cos_ref[...], sin_ref[...]
    for c in range(0, 13, 2):
        group = [qkv_tiles(i) for i in range(c, min(c + 2, 13))]
        y2 = dot(nrm[:, 0:D], side(group))
        for i in range(len(group)):
            y = y2[:, 128 * i : 128 * i + 128]
            if c + i < 10:
                y = y * cos_t + swap(y) * sin_t
            if c + i < 8:
                qs[c + i] = y.astype(BF)
            for h in range(2):
                head = 2 * (c + i) + h
                if 15 <= head < 20:
                    kk[head - 15] = both(y, h).astype(BF)
                if 20 <= head < 25:
                    vv[head - 20] = both(y, h).astype(BF)

    mixed[:, 896:1024] = jnp.zeros((ROWS, 128), BF)
    zero_b = jnp.zeros((MROWS, 128), BF)

    def rows_of(m):
        return pl.ds(pl.multiple_of(m * MROWS, MROWS), MROWS)

    def chunk(head):
        return pl.ds(128 * (head // 2), 128)

    def attend(m, _):
        rows = rows_of(m)
        bias = bias_ref[rows, :]
        bias3 = jnp.concatenate([bias, bias, bias], axis=0)
        for g in range(KV):
            heads = [3 * g + i for i in range(3)]
            q = jnp.concatenate([jnp.where(half[h % 2], qs[h // 2, rows, :], zero_b) for h in heads], axis=0)
            s = dot(q, kk[g, rows, :], 1, 1) * 0.125 + bias3
            e = jnp.exp(s - jnp.max(s, axis=-1, keepdims=True))
            p = e / jnp.sum(e, axis=-1, keepdims=True)
            prob[m, g] = p
            o = dot(p.astype(BF), vv[g, rows, :]).astype(BF)
            for i, h in enumerate(heads):
                mixed[rows, chunk(h)] = jnp.where(half[h % 2], o[MROWS * i : MROWS * i + MROWS], mixed[rows, chunk(h)])
        return 0

    lax.fori_loop(0, MB, attend, 0)

    loads[1].wait()
    for c in range(0, 8, 2):
        cols = slice(128 * c, 128 * c + 256)
        mid[:, cols] = xs[:, cols] + dot(mixed[:, 0:D], side([out_tiles(c), out_tiles(c + 1)]))
    middle = mid[...]
    inv2 = lax.rsqrt(mean_of(middle * middle) + EPSILON)
    n2p[...] = dot((middle * inv2 * gain2).astype(BF), spread[...]).astype(BF)

    loads[2].wait()

    def expand(c, _):
        g = dot(n2p[...], in_tiles(c))
        u = dot(n2p[...], in_tiles(c + 4))
        gate[c] = g
        up[c] = u
        hid[c] = (g * jax.nn.sigmoid(g) * u).astype(BF)
        return 0

    lax.fori_loop(0, 4, expand, 0)
    loads[3].wait()
    acc[...] = mid[...]

    def reduce_(c, _):
        tiles = down_tiles(c)
        acc[...] += dot(hid[c], tiles)
        gh = dot(go[...], tiles, 1, 1)
        g, u = gate[c], up[c]
        sg = jax.nn.sigmoid(g)
        ggu[c] = (gh * u * sg * (1.0 + g * (1.0 - sg))).astype(BF)
        ggu[c + 4] = (gh * g * sg).astype(BF)
        term = dot(hid[c], go[...], 0, 0).astype(BF)
        for i in range(8):
            w[pl.ds(96 + 8 * c, 8), 5 * i : 5 * i + 5] = term[:, 128 * i : 128 * i + 128].reshape(8, 5, 16, 128)
        return 0

    lax.fori_loop(0, 4, reduce_, 0)
    stores[3].start()
    out_ref[...] = (acc[:, 0:D] * live).astype(BF)

    acc[...] = jnp.zeros((ROWS, 1024), F32)

    def back(c, _):
        gg = ggu[c]
        acc[...] += dot(gg, in_tiles(c), 1, 1)
        term = dot(n2p[...], gg, 0, 0).astype(BF)
        for i in range(5):
            w[32:96, 5 * c + i] = term[:, 128 * i : 128 * i + 128].reshape(64, 16, 128)
        return 0

    lax.fori_loop(0, 8, back, 0)
    stores[2].start()
    gn = acc[...]
    hi = gn.astype(BF)
    lo = (gn - hi.astype(F32)).astype(BF)
    gn = dot(hi, spread[...], 1, 1) + dot(lo, spread[...], 1, 1)
    n2 = mid[...] * inv2
    d_gain2 = jnp.sum(gn * n2, axis=0, keepdims=True)
    u = gn * gain2
    gm = go[...].astype(F32) + inv2 * (u - n2 * mean_of(u * n2))
    mid[...] = gm
    gmb = gm.astype(BF)
    gmix = jnp.zeros((ROWS, D), F32)
    for i in range(0, 8, 2):
        gmix = gmix + dot(gmb[:, 128 * i : 128 * i + 256], side([out_tiles(i), out_tiles(i + 1)]), 1, 1)
    term = dot(mixed[:, 0:D], gmb, 0, 0).astype(BF)
    for i in range(8):
        w[20:32, 5 * i : 5 * i + 5] = term[:, 128 * i : 128 * i + 128].reshape(12, 5, 16, 128)
    stores[1].start()
    mixed[:, 0:D] = gmix.astype(BF)
    gq[12] = jnp.zeros((ROWS, 128), F32)

    def attend_back(m, _):
        rows = rows_of(m)
        for g in range(KV):
            heads = [3 * g + i for i in range(3)]
            q = jnp.concatenate([jnp.where(half[h % 2], qs[h // 2, rows, :], zero_b) for h in heads], axis=0)
            gmx = jnp.concatenate([jnp.where(half[h % 2], mixed[rows, chunk(h)], zero_b) for h in heads], axis=0)
            p = prob[m, g]
            gv = dot(p.astype(BF), gmx, 0, 0)
            gp = dot(gmx, vv[g, rows, :], 1, 1)
            gs = (p * (gp - jnp.sum(p * gp, axis=-1, keepdims=True))).astype(BF)
            gqs = dot(gs, kk[g, rows, :]) * 0.125
            gk = dot(gs, q, 0, 0) * 0.125
            for i, h in enumerate(heads):
                gq[h // 2, rows, :] = jnp.where(half[h % 2], gqs[MROWS * i : MROWS * i + MROWS], gq[h // 2, rows, :])
            for head, value in ((15 + g, gk), (20 + g, gv)):
                value = value + pltpu.roll(value, 64, 1)
                gq[head // 2, rows, :] = jnp.where(half[head % 2], value, gq[head // 2, rows, :])
        return 0

    lax.fori_loop(0, MB, attend_back, 0)

    for c in range(13):
        y = gq[c]
        if c < 10:
            y = y * cos_t - swap(y) * sin_t
        gqb[c] = y.astype(BF)
    gn1 = jnp.zeros((ROWS, D), F32)
    for c in range(0, 13, 2):
        group = list(range(c, min(c + 2, 13)))
        gy = side([gqb[i] for i in group])
        gn1 = gn1 + dot(gy, side([qkv_tiles(i) for i in group]), 1, 1)
        term = dot(nrm[:, 0:D], gy, 0, 0).astype(BF)
        for n, i in enumerate(group):
            w[0:20, 3 * i : 3 * i + 3] = term[:, 128 * n : 128 * n + 128].reshape(20, 3, 16, 128)
    acc[:, 896:1024] = jnp.zeros((ROWS, 128), F32)
    acc[:, 0:D] = gn1
    gn1 = acc[...]
    n1 = xs[...] * inv1
    d_gain1 = jnp.sum(gn1 * n1, axis=0, keepdims=True)
    both_gains = jnp.concatenate([v[:, 128 * i : 128 * i + 128] for v in (d_gain1, d_gain2) for i in range(8)], axis=0)
    w[0, 39] = both_gains.astype(BF)
    stores[0].start()
    u = gn1 * gain1
    res = mid[...] + inv1 * (u - n1 * mean_of(u * n1))
    gin_ref[...] = res[:, 0:D].astype(BF)
    for store in stores:
        store.wait()


def compute(blocks, inputs, cotangent, segments, counts):
    vm = pl.BlockSpec(memory_space=pltpu.VMEM)
    hbm = pl.BlockSpec(memory_space=pl.ANY)
    return pl.pallas_call(
        compute_kernel,
        out_shape=(
            jax.ShapeDtypeStruct((ROWS, D), BF),
            jax.ShapeDtypeStruct((ROWS, D), BF),
            jax.ShapeDtypeStruct((N, 40, 16, 128), BF),
        ),
        in_specs=[hbm] + [vm] * 6,
        out_specs=(vm, vm, hbm),
        scratch_shapes=[
            pltpu.VMEM((N, 40, 16, 128), BF),
            pltpu.VMEM((ROWS, 1024), F32),
            pltpu.VMEM((ROWS, 1024), BF),
            pltpu.VMEM((ROWS, 1024), BF),
            pltpu.VMEM((8, ROWS, 128), BF),
            pltpu.VMEM((KV, ROWS, 128), BF),
            pltpu.VMEM((KV, ROWS, 128), BF),
            pltpu.VMEM((MB, KV, ROWS, MROWS), F32),
            pltpu.VMEM((ROWS, 1024), BF),
            pltpu.VMEM((ROWS, 1024), F32),
            pltpu.VMEM((ROWS, 1024), BF),
            pltpu.VMEM((4, ROWS, 640), F32),
            pltpu.VMEM((4, ROWS, 640), F32),
            pltpu.VMEM((4, ROWS, 640), BF),
            pltpu.VMEM((8, ROWS, 640), BF),
            pltpu.VMEM((13, ROWS, 128), F32),
            pltpu.VMEM((13, ROWS, 128), BF),
            pltpu.VMEM((1024, 1024), BF),
            pltpu.VMEM((ROWS, 1024), F32),
            pltpu.SemaphoreType.DMA((4,)),
            pltpu.SemaphoreType.DMA((4,)),
        ],
        compiler_params=pltpu.CompilerParams(vmem_limit_bytes=60 * 1024 * 1024),
    )(blocks.reshape(N, 40, 16, 128), inputs, cotangent, *tables(segments, counts))


def shards(inputs, cotangent, flat_weights, counts, segments):
    d = lax.axis_index("fsdp")
    blocks = gather(to_block(flat_weights, d))
    block_out, input_grad, terms = compute(blocks, inputs, cotangent, segments, counts)
    return block_out, input_grad, from_block(scatter(terms.reshape(4, 4, 4, 2, TILES, 16, 128)), d)


def solution(mesh):
    in_specs = (P("fsdp", None), P("fsdp", None), P("fsdp"), P("fsdp"), P("fsdp"))
    out_specs = (P("fsdp", None), P("fsdp", None), P("fsdp"))
    return jax.shard_map(shards, mesh=mesh, in_specs=in_specs, out_specs=out_specs, check_vma=False)
```

```python
import functools
import math

import jax
import jax.numpy as jnp
from jax import lax
from jax.experimental import pallas as pl
from jax.experimental.pallas import tpu as pltpu
from jax.sharding import PartitionSpec as P

D = 960
H = 15
KV = 5
HD = 64
FF = 2560
MB = 3
EPSILON = 1e-05
GAINS = 2 * D
BLOCK = 76800
N = 128
BF = jnp.bfloat16
F32 = jnp.float32
VMEM_BYTES = 63 * 1024 * 1024

MESH = pl.DeviceIdType.MESH
TILES = 40
PARTS = ((0, 7, 14), (14, 20, 27), (27, 33, 40))


def place():
    me = lax.axis_index("fsdp")
    return [me // 32, (me // 8) % 4, (me // 2) % 4], me % 2


def device_at(coords, core):
    return (coords[0] * 32 + coords[1] * 8 + coords[2] * 2 + core,)


def moved(coords, dim, by):
    out = list(coords)
    out[dim] = (out[dim] + by + 4) % 4
    return out


def greet(coords, core):
    barrier = pltpu.get_barrier_semaphore()
    for dim in range(3):
        for by in (1, -1, 2):
            pl.semaphore_signal(barrier, inc=1, device_id=device_at(moved(coords, dim, by), core), device_id_type=MESH)
    pl.semaphore_signal(barrier, inc=1, device_id=device_at(coords, 1 - core), device_id_type=MESH)
    pl.semaphore_wait(barrier, 10)


def gather_into(w, blk, coords, core, send, recv, pair_send, pair_recv, own_sem):
    sent, ids, pair_ids, swapped = [], {}, {}, []
    sibling = device_at(coords, 1 - core)

    def at(fixed, tiles, which):
        index = [slice(None)] * 3
        for dim, value in fixed.items():
            index[dim] = value
        return w.at[(*index, which, rng(tiles))]

    def push(src, dst, device, ssem, rsem):
        copy = pltpu.make_async_remote_copy(src_ref=src, dst_ref=dst, send_sem=ssem, recv_sem=rsem, device_id=device, device_id_type=MESH)
        copy.start()
        sent.append(copy)

    def forward(key, src, dst, dim, step):
        k = ids.setdefault(key, len(ids))
        push(src, dst, device_at(moved(coords, dim, step), core), send.at[k], recv.at[k])

    def arrived(key, ref):
        landed(ref, recv.at[ids[key]])

    def swap(fixed, tiles):
        k = len(swapped)
        push(at(fixed, tiles, core), at(fixed, tiles, core), sibling, pair_send.at[k], pair_recv.at[k])
        swapped.append((fixed, tiles, k))

    def half(p, sign, number):
        lo, mid, hi = PARTS[p]
        return ((lo, mid), (mid, hi))[(number == 1) ^ (sign < 0)]

    def whole(p):
        return (PARTS[p][0], PARTS[p][2])

    def near(dim, step):
        return moved(coords, dim, step)[dim]

    local = pltpu.make_async_copy(blk, w.at[(*coords, core)], own_sem)
    local.start()
    parts = range(3)
    dims = [[(p + k) % 3 for k in range(3)] for p in parts]
    for p in parts:
        a, b, c = dims[p]
        for step in (2, 1, -1):
            forward((p, 0, step), blk.at[rng(whole(p))], at({a: coords[a], b: coords[b], c: coords[c]}, whole(p), core), a, step)
    push(blk, w.at[(*coords, core)], sibling, pair_send.at[90], pair_recv.at[90])
    local.wait()

    def line(p, step):
        a, b, c = dims[p]
        return {b: near(b, step), c: coords[c]}

    def sheet(p, group, step):
        a, b, c = dims[p]
        return {b: near(b, group), c: near(c, step)}

    def send_line(p, number):
        for sign in (1, -1):
            ref = at(line(p, 0), half(p, sign, number), core)
            forward((p, 1, sign, number), ref, ref, dims[p][1], sign)

    def send_sheet(p, group, number):
        for sign in (1, -1):
            ref = at(sheet(p, group, 0), half(p, sign, number), core)
            forward((p, 2, group, sign, number), ref, ref, dims[p][2], sign)

    def relay_line(p):
        for sign in (1, -1):
            ref = at(line(p, -sign), half(p, sign, 0), core)
            arrived((p, 1, sign, 0), ref)
            forward((p, 1, sign, 2), ref, ref, dims[p][1], sign)

    def relay_sheet(p, group):
        for sign in (1, -1):
            ref = at(sheet(p, group, -sign), half(p, sign, 0), core)
            arrived((p, 2, group, sign, 0), ref)
            forward((p, 2, group, sign, 2), ref, ref, dims[p][2], sign)

    def rest_sheet(p, group):
        for sign in (1, -1):
            arrived((p, 2, group, sign, 1), at(sheet(p, group, -sign), half(p, sign, 1), core))
            swap(sheet(p, group, -sign), whole(p))

    def last_sheet(p, group):
        for sign in (1, -1):
            arrived((p, 2, group, sign, 2), at(sheet(p, group, 2), half(p, sign, 2), core))
        swap(sheet(p, group, 2), whole(p))

    for p in parts:
        a, b, c = dims[p]
        for step in (1, -1, 2):
            fixed = {a: near(a, -step), b: coords[b], c: coords[c]}
            arrived((p, 0, step), at(fixed, whole(p), core))
            swap(fixed, whole(p))
        for number in (0, 1):
            send_line(p, number)
    for p in parts:
        for number in (0, 1):
            send_sheet(p, 0, number)
    for p in parts:
        relay_line(p)
    for p in parts:
        for sign in (1, -1):
            arrived((p, 1, sign, 1), at(line(p, -sign), half(p, sign, 1), core))
        for sign in (1, -1):
            for number in (0, 1):
                send_sheet(p, -sign, number)
    for p in parts:
        relay_sheet(p, 0)
    for p in parts:
        for sign in (1, -1):
            arrived((p, 1, sign, 2), at(line(p, 2), half(p, sign, 2), core))
        for number in (0, 1):
            send_sheet(p, 2, number)
        for step in (1, -1, 2):
            swap(line(p, step), whole(p))
    for p in parts:
        rest_sheet(p, 0)
    for group in (-1, 1, 2):
        for p in parts:
            relay_sheet(p, group)
        for p in parts:
            rest_sheet(p, group)
    for group in (0, -1, 1, 2):
        for p in parts:
            last_sheet(p, group)
    landed(w.at[(*coords, 1 - core)], pair_recv.at[90])
    for fixed, tiles, k in swapped:
        landed(at(fixed, tiles, 1 - core), pair_recv.at[k])
    return sent


def pack(rows_48, rows_80, rows_15, gains, d):
    qkv = jnp.pad(rows_48, ((0, 0), (0, 64))).reshape(3, 16, 13, 128).transpose(2, 0, 1, 3).reshape(39, 16, 128)
    qkv = jnp.concatenate([qkv, jnp.where(d == 0, gains, jnp.zeros_like(gains))[None]], axis=0)
    square = jnp.pad(rows_80, ((0, 0), (0, 64))).reshape(5, 16, 8, 128).transpose(2, 0, 1, 3).reshape(40, 16, 128)
    wide = jnp.pad(rows_15, ((0, 1), (0, 0))).reshape(16, 40, 128).transpose(1, 0, 2)
    return jnp.where(d < 20, qkv, jnp.where((d >= 32) & (d < 96), wide, square))


def to_block(shard, d):
    following = lax.ppermute(shard[:GAINS], "fsdp", [(i, (i + N - 1) % N) for i in range(N)])
    flat = lax.dynamic_slice(jnp.concatenate([shard, following]), (GAINS - 15 * d,), (BLOCK,))
    gains = jnp.pad(shard[:GAINS].reshape(2, D), ((0, 0), (0, 64))).reshape(16, 128)
    return pack(flat.reshape(48, 1600), flat.reshape(80, D), flat.reshape(15, 2 * FF), gains, d)


def from_block(tiles, d):
    qkv = tiles[:39].reshape(13, 3, 16, 128).transpose(1, 2, 0, 3).reshape(48, 1664)[:, :1600].reshape(-1)
    square = tiles.reshape(8, 5, 16, 128).transpose(1, 2, 0, 3).reshape(80, 1024)[:, :D].reshape(-1)
    wide = tiles.transpose(1, 0, 2)[:15].reshape(-1)
    flat = jnp.where(d < 20, qkv, jnp.where((d >= 32) & (d < 96), wide, square))
    before = lax.ppermute(flat[BLOCK - GAINS :], "fsdp", [(i, (i + 1) % N) for i in range(N)])
    before = jnp.where(d == 0, tiles[39].reshape(2, 1024)[:, :D].reshape(-1), before)
    return lax.dynamic_slice(jnp.concatenate([before, flat]), (15 * d,), (BLOCK + 15,))


ROWS = 240
MROWS = 80


def tables(segment_ids, counts):
    seg = segment_ids.reshape(MB, MROWS)
    places = jnp.arange(MROWS, dtype=jnp.int32)
    same = seg[:, :, None] == seg[:, None, :]
    first_row = jnp.min(jnp.where(same, places[None, None, :], MROWS), axis=2)
    position = (places[None, :] - first_row).astype(F32).reshape(ROWS)
    freq = jnp.exp(jnp.arange(HD // 2, dtype=F32) * (-2.0 * math.log(10000.0) / HD))
    angle = position[:, None] * freq[None, :]
    cos, sin = jnp.cos(angle), jnp.sin(angle)
    cos_t = jnp.concatenate([cos, cos, cos, cos], axis=1)
    sin_t = jnp.concatenate([-sin, sin, -sin, sin], axis=1)
    allowed = same & (places[None, None, :] <= places[None, :, None])
    bias = jnp.where(allowed, 0.0, -1e30).astype(F32).reshape(ROWS, MROWS)
    live = (places[None, :] < counts[:, None]).astype(F32).reshape(ROWS, 1)
    return cos_t, sin_t, bias, jnp.broadcast_to(live, (ROWS, 128))


def dot(a, b, ca=1, cb=0):
    return lax.dot_general(a, b, (((ca,), (cb,)), ((), ())), preferred_element_type=F32)


def mean_of(value):
    return jnp.sum(value, axis=-1, keepdims=True) * (1.0 / D)


class Flow:
    def __init__(self, name, dims, tiles, bufs, first_plane):
        self.name, self.dims, self.tiles, self.bufs, self.first_plane = name, dims, tiles, bufs, first_plane

    def half(self, sign, which):
        lo, mid, hi = self.tiles
        pair = ((lo, mid), (mid, hi))
        return pair[which] if sign > 0 else pair[1 - which]


class Reduce:
    def __init__(self, w, pair_buf, bufs, red, coords, core, send, recv, pair_send, pair_recv):
        self.w, self.pair_buf, self.red = w, pair_buf, red
        self.coords, self.core = coords, core
        self.send, self.recv, self.pair_send, self.pair_recv = send, recv, pair_send, pair_recv
        self.sent, self.ids = [], {}
        b1, b2, b3, q1, q2, z2 = bufs
        self.P0 = Flow("P0", (0, 1, 2), (0, 5, 10), (b1, b2, b3), 0)
        self.P1 = Flow("P1", (1, 2, 0), (10, 17, 25), (b1, b2, None), 0)
        self.P2 = Flow("P2", (2, 1, 0), (25, 32, 40), (b1, b2, None), 0)
        self.Q1 = Flow("Q1", (1, 2, 0), (0, 10, 20), (q1, q2, None), 0)
        self.Q2 = Flow("Q2", (2, 1, 0), (20, 30, 40), (q1, q2, None), 0)
        self.Z1 = Flow("Z1", (1, 2, 0), (10, 25, 40), (None, None, b3), 0)
        self.Z2 = Flow("Z2", (1, 2, 0), (0, 5, 10), (None, None, z2), 0)

    def copy(self, src, dst, device, ssem, rsem):
        return pltpu.make_async_remote_copy(
            src_ref=src, dst_ref=dst, send_sem=ssem, recv_sem=rsem, device_id=device, device_id_type=MESH
        )

    def offer(self, z):
        one = self.copy(
            self.w.at[z, :, :, 1 - self.core], self.pair_buf.at[z % 3], device_at(self.coords, 1 - self.core),
            self.pair_send.at[z], self.pair_recv.at[z],
        )
        one.start()
        self.sent.append((None, one))

    def ready(self, z):
        slot = z % 3
        landed(self.pair_buf.at[slot], self.pair_recv.at[z])

        def body(t, _):
            at = (z, t // 4, t % 4, self.core)
            self.w[at] = self.w[at] + self.pair_buf[slot, t // 4, t % 4]
            return 0

        lax.fori_loop(0, 16, body, 0)

    def sem(self, flow, phase, planes, sign, number):
        return self.ids.setdefault((flow.name, phase, planes, sign, number), len(self.ids))

    def along(self, dim, step):
        return moved(self.coords, dim, step)[dim]

    def slot(self, flow, phase, planes, sign, number):
        which = 2 if number == 0 else (0 if sign > 0 else 1)
        inner = []
        for d in range(3):
            if d in flow.dims[phase + 1 :]:
                inner.append(pl.ds(planes[0], planes[1] - planes[0]) if d == 0 else slice(None))
        if flow.name in ("Q1", "Q2"):
            inner = inner[1:]
        tiles = flow.half(sign, 1 if number == 1 else 0)
        return flow.bufs[phase].at[(which, *inner, rng(tiles))]

    def ship(self, flow, phase, planes, sign, number):
        dim = flow.dims[phase]
        tiles = flow.half(sign, 1 if number == 1 else 0)
        fixed = []
        for d in range(3):
            if d in flow.dims[:phase]:
                fixed.append(self.coords[d])
            elif d == dim:
                fixed.append(self.along(d, 2 if number == 0 else sign))
            else:
                fixed.append(pl.ds(planes[0], planes[1] - planes[0]) if d == 0 else slice(None))
        slot = self.slot(flow, phase, planes, sign, number)
        if flow.name in ("Q1", "Q2"):
            fixed[0] = 0
        k = self.sem(flow, phase, planes, sign, number)
        return self.copy(
            self.w.at[(*fixed, self.core, rng(tiles))], slot,
            device_at(moved(self.coords, dim, sign), self.core), self.send.at[k], self.recv.at[k],
        )

    def go(self, flow, phase, planes, sign, number, guard=None):
        one = self.ship(flow, phase, planes, sign, number)
        if guard is None:
            one.start()
        else:
            pl.when(guard)(one.start)
        self.sent.append((guard, one))

    def loop(self, flow, phase, planes, coord, fn):
        dims = flow.dims
        free = [d for d in range(3) if d in dims[phase + 1 :]]
        sizes = [planes[1] - planes[0] if d == 0 else 4 for d in free]

        def body(t, _):
            inner = []
            if len(free) == 2:
                inner = [t // 4 + (planes[0] if free[0] == 0 else 0), t % 4]
            elif len(free) == 1:
                inner = [t + (planes[0] if free[0] == 0 else 0)]
            at = []
            for d in range(3):
                if d in free:
                    at.append(inner[free.index(d)])
                elif d == dims[phase]:
                    at.append(coord)
                else:
                    at.append(self.coords[d])
            if flow.name in ("Q1", "Q2"):
                at[0] = 0
                inner = inner[1:]
            fn((*at, self.core), tuple(inner))
            return 0

        count = math.prod(sizes)
        if count == 1:
            body(0, 0)
        else:
            lax.fori_loop(0, count, body, 0)

    def add_half(self, flow, phase, planes, sign):
        landed(self.slot(flow, phase, planes, sign, 0), self.recv.at[self.sem(flow, phase, planes, sign, 0)])
        tiles = rng(flow.half(sign, 0))
        buf = flow.bufs[phase]

        def fold(at, inner):
            self.w[(*at, tiles)] = self.w[(*at, tiles)] + buf[(2, *inner, tiles)]

        self.loop(flow, phase, planes, self.along(flow.dims[phase], sign), fold)

    def add_all(self, flow, phase, planes):
        for sign in (1, -1):
            for number in (1, 2):
                landed(self.slot(flow, phase, planes, sign, number), self.recv.at[self.sem(flow, phase, planes, sign, number)])
        tiles = rng((flow.tiles[0], flow.tiles[2]))
        buf = flow.bufs[phase]

        def total(at, inner):
            value = self.w[(*at, tiles)].astype(F32) + buf[(0, *inner, tiles)].astype(F32) + buf[(1, *inner, tiles)].astype(F32)
            if phase == 2:
                self.red[tiles] = value
            else:
                self.w[(*at, tiles)] = value.astype(BF)

        self.loop(flow, phase, planes, self.coords[flow.dims[phase]], total)

    def plane_in(self, planes, step):
        z = self.along(0, step)
        return (z >= planes[0]) & (z < planes[1])

    def first(self, planes):
        for z in range(*planes):
            self.ready(z)
        flows = (self.P1, self.P2) if planes[0] else (self.Q1, self.Q2)
        for number in (0, 1):
            for sign in (1, -1):
                for flow in flows:
                    self.go(flow, 0, planes, sign, number)
                if planes[0]:
                    one = self.ship(self.P0, 0, (0, 4), sign, number)
                    pl.when(self.plane_in(planes, 2 if number == 0 else sign))(one.start)

    def second(self, planes):
        for sign in (1, -1):
            if planes[0]:

                @pl.when(self.plane_in(planes, sign))
                def _():
                    self.add_half(self.P0, 0, (0, 4), sign)
                    self.ship(self.P0, 0, (0, 4), sign, 2).start()

            for flow in (self.P1, self.P2) if planes[0] else (self.Q1, self.Q2):
                self.add_half(flow, 0, planes, sign)
                self.go(flow, 0, planes, sign, 2)

    def start(self, flow, phase, planes, guards=None):
        for number in (0, 1):
            for sign in (1, -1):
                self.go(flow, phase, planes, sign, number, guards and guards(sign, number))

    def pass_on(self, flow, phase, planes, guards=None):
        for sign in (1, -1):
            guard = guards and guards(sign, 2)
            if guard is None:
                self.add_half(flow, phase, planes, sign)
            else:
                pl.when(guard)(functools.partial(self.add_half, flow, phase, planes, sign))
            self.go(flow, phase, planes, sign, 2, guard)

    def whole(self, flow):
        return rng((flow.tiles[0], flow.tiles[2]))

    def direct(self, flow, phase, planes, step):
        dim = flow.dims[phase]
        fixed, inner = [], []
        for d in range(3):
            if d in flow.dims[:phase]:
                fixed.append(self.coords[d])
            elif d == dim:
                fixed.append(self.along(d, step))
            else:
                span = pl.ds(planes[0], planes[1] - planes[0]) if d == 0 else slice(None)
                fixed.append(span)
                inner.append(span)
        if flow.name in ("Q1", "Q2"):
            fixed[0] = 0
            inner = inner[1:]
        k = self.sem(flow, phase, planes, step, 3)
        return self.copy(
            self.w.at[(*fixed, self.core, self.whole(flow))], flow.bufs[phase].at[(step % 4 - 1, *inner, self.whole(flow))],
            device_at(moved(self.coords, dim, step), self.core), self.send.at[k], self.recv.at[k],
        )

    def start_direct(self, flow, phase, planes, guards=None):
        for step in (2, 1, -1):
            guard = guards and guards(step)
            one = self.direct(flow, phase, planes, step)
            if guard is None:
                one.start()
            else:
                pl.when(guard)(one.start)
            self.sent.append((guard, one))

    def add_direct(self, flow, phase, planes):
        for step in (1, -1, 2):
            self.direct(flow, phase, planes, step).wait_recv()
        tiles = self.whole(flow)
        buf = flow.bufs[phase]

        def total(at, inner):
            value = self.w[(*at, tiles)].astype(F32)
            for slot in range(3):
                value = value + buf[(slot, *inner, tiles)].astype(F32)
            if phase == 2:
                self.red[tiles] = value
            else:
                self.w[(*at, tiles)] = value.astype(BF)

        self.loop(flow, phase, planes, self.coords[flow.dims[phase]], total)

    def finish(self):
        late, early, every = (0, 1), (1, 4), (0, 4)
        z = self.coords[0]
        upper = lambda sign, number=0: z != 0
        to_zero = lambda step: self.along(0, step) == 0
        for number in (0, 1, 2):
            for sign in (1, -1):
                guard = self.plane_in((1, 4), 2 if number == 0 else sign)
                self.sent.append((guard, self.ship(self.P0, 0, every, sign, number)))
        for flow in (self.P1, self.P2):
            for planes in ((3, 4), (1, 3)):
                self.add_all(flow, 0, planes)
            self.start(flow, 1, early)
        self.second(late)
        pl.when(z != 0)(lambda: self.add_all(self.P0, 0, every))
        self.start(self.P0, 1, every, upper)
        for flow in (self.P1, self.P2):
            self.pass_on(flow, 1, early)
        for flow in (self.Q1, self.Q2):
            self.add_all(flow, 0, late)
            self.start_direct(flow, 1, late)
        self.pass_on(self.P0, 1, every, upper)
        for flow in (self.P1, self.P2):
            self.add_all(flow, 1, early)
        for flow in (self.Q1, self.Q2):
            self.add_direct(flow, 1, late)
        self.start_direct(self.Z1, 2, every)
        self.start_direct(self.Z2, 2, every, to_zero)
        pl.when(z != 0)(lambda: self.add_all(self.P0, 1, every))
        self.start_direct(self.P0, 2, every, upper)
        self.add_direct(self.Z1, 2, every)
        pl.when(z != 0)(lambda: self.add_direct(self.P0, 2, every))
        pl.when(z == 0)(lambda: self.add_direct(self.Z2, 2, every))
        for guard, one in self.sent:
            if guard is None:
                one.wait_send()
            else:
                pl.when(guard)(one.wait_send)


def rng(tiles):
    return pl.ds(tiles[0], tiles[1] - tiles[0])


def landed(dst, rsem):
    pltpu.make_async_copy(dst, dst, rsem).wait()


def layer_kernel(
    blk, x_ref, c_ref, cos_ref, sin_ref, bias_ref, live_ref,
    out_ref, gin_ref, red_ref,
    w, pair_buf, b1, b2, b3, q1, q2, z2, xs, go, nrm, qs, kk, vv, prob, mixed, mid, n2p, gate, up, hid, ggu, gq, gqb, spread, acc,
    send, recv, pair_send, pair_recv, own_sem, rs_send, rs_recv, rp_send, rp_recv,
):
    coords, core = place()
    greet(coords, core)
    sent = gather_into(w, blk, coords, core, send, recv, pair_send, pair_recv, own_sem)
    rs = Reduce(w, pair_buf, (b1, b2, b3, q1, q2, z2), red_ref, coords, core, rs_send, rs_recv, rp_send, rp_recv)

    def join(parts):
        return jnp.concatenate(parts, axis=0)

    def qkv_tiles(c):
        t = slice(3 * c, 3 * c + 3)
        return join([w[0, 0:2, :, :, t].reshape(768, 128), w[0, 2, 0:2, :, t].reshape(192, 128)])

    def put_qkv(c, v):
        t = slice(3 * c, 3 * c + 3)
        w[0, 0:2, :, :, t] = v[:768].reshape(2, 4, 2, 3, 16, 128)
        w[0, 2, 0:2, :, t] = v[768:].reshape(2, 2, 3, 16, 128)

    def out_tiles(c):
        t = slice(5 * c, 5 * c + 5)
        return join([w[0, 2, 2:4, :, t].reshape(320, 128), w[0, 3, :, :, t].reshape(640, 128)])

    def put_out(c, v):
        t = slice(5 * c, 5 * c + 5)
        w[0, 2, 2:4, :, t] = v[:320].reshape(2, 2, 5, 16, 128)
        w[0, 3, :, :, t] = v[320:].reshape(4, 2, 5, 16, 128)

    def in_tiles(c):
        return side([w[1:3, :, :, :, 5 * c + i].reshape(1024, 128) for i in range(5)])

    def down_tiles(c):
        return side([w[3, c, :, :, 5 * i : 5 * i + 5].reshape(640, 128) for i in range(8)])

    def side(parts):
        return jnp.concatenate(parts, axis=1)

    lane = lax.broadcasted_iota(jnp.int32, (MROWS, 128), 1)
    half = (lane < 64, lane >= 64)
    lane_all = lax.broadcasted_iota(jnp.int32, (ROWS, 128), 1)
    low_all = lane_all < 64
    first_all = lane_all % 64 < 32

    def swap(v):
        return jnp.where(first_all, pltpu.roll(v, 96, 1), pltpu.roll(v, 32, 1))

    def both(v, h):
        other = pltpu.roll(v, 64, 1)
        return jnp.where(low_all, v, other) if h == 0 else jnp.where(low_all, other, v)

    for k in range(8):
        r = lax.broadcasted_iota(jnp.int32, (256, 128), 0) + 128 * (k - 1)
        c = lax.broadcasted_iota(jnp.int32, (256, 128), 1) + 128 * k
        spread[k] = jnp.where((r == (c // 16) * 15 + c % 16) & (c % 16 != 15), 1.0, 0.0).astype(BF)

    xs[:, 896:1024] = jnp.zeros((ROWS, 128), BF)
    xs[:, 0:D] = x_ref[...]
    go[:, 896:1024] = jnp.zeros((ROWS, 128), BF)
    live = live_ref[:, 0:1]
    go[:, 0:D] = (c_ref[...].astype(F32) * live).astype(BF)
    x = xs[...].astype(F32)
    inv1 = lax.rsqrt(mean_of(x * x) + EPSILON)
    gains = w[0, 0, 0, 0, 39].astype(F32)
    gain1 = side([gains[i : i + 1] for i in range(8)])
    gain2 = side([gains[8 + i : 9 + i] for i in range(8)])
    nrm[...] = (x * inv1 * gain1).astype(BF)

    cos_t, sin_t = cos_ref[...], sin_ref[...]
    for c in range(0, 13, 2):
        group = [qkv_tiles(i) for i in range(c, min(c + 2, 13))]
        y2 = dot(nrm[:, 0:D], side(group))
        for i in range(len(group)):
            y = y2[:, 128 * i : 128 * i + 128]
            if c + i < 10:
                y = y * cos_t + swap(y) * sin_t
            if c + i < 8:
                qs[c + i] = y.astype(BF)
            for h in range(2):
                head = 2 * (c + i) + h
                if 15 <= head < 20:
                    kk[head - 15] = both(y, h).astype(BF)
                if 20 <= head < 25:
                    vv[head - 20] = both(y, h).astype(BF)

    mixed[:, 896:1024] = jnp.zeros((ROWS, 128), BF)
    zero_b = jnp.zeros((MROWS, 128), BF)

    def rows_of(m):
        return pl.ds(pl.multiple_of(m * MROWS, MROWS), MROWS)

    def chunk(head):
        return pl.ds(128 * (head // 2), 128)

    def attend(m, _):
        rows = rows_of(m)
        bias = bias_ref[rows, :]
        bias3 = jnp.concatenate([bias, bias, bias], axis=0)
        for g in range(KV):
            heads = [3 * g + i for i in range(3)]
            q = jnp.concatenate([jnp.where(half[h % 2], qs[h // 2, rows, :], zero_b) for h in heads], axis=0)
            s = dot(q, kk[g, rows, :], 1, 1) * 0.125 + bias3
            e = jnp.exp(s - jnp.max(s, axis=-1, keepdims=True))
            p = e / jnp.sum(e, axis=-1, keepdims=True)
            prob[m, g] = p
            o = dot(p.astype(BF), vv[g, rows, :]).astype(BF)
            for i, h in enumerate(heads):
                mixed[rows, chunk(h)] = jnp.where(half[h % 2], o[MROWS * i : MROWS * i + MROWS], mixed[rows, chunk(h)])
        return 0

    lax.fori_loop(0, MB, attend, 0)

    for c in range(0, 8, 2):
        cols = slice(128 * c, 128 * c + 256)
        mid[:, cols] = xs[:, cols].astype(F32) + dot(mixed[:, 0:D], side([out_tiles(c), out_tiles(c + 1)]))
    middle = mid[...]
    inv2 = lax.rsqrt(mean_of(middle * middle) + EPSILON)
    n2b = (middle * inv2 * gain2).astype(BF)
    n2p[:, 0:128] = dot(n2b[:, 0:128], spread[0, 128:256]).astype(BF)
    for k in range(1, 8):
        n2p[:, 128 * k : 128 * k + 128] = dot(n2b[:, 128 * k - 128 : 128 * k + 128], spread[k]).astype(BF)


    def expand(c, _):
        g = dot(n2p[...], in_tiles(c))
        u = dot(n2p[...], in_tiles(c + 4))
        gate[c] = g.astype(BF)
        up[c] = u.astype(BF)
        hid[c] = (g * jax.nn.sigmoid(g) * u).astype(BF)
        return 0

    lax.fori_loop(0, 4, expand, 0)
    for copy in sent:
        copy.wait_send()
    acc[...] = mid[...]

    def reduce_(c, _):
        tiles = down_tiles(c)
        acc[...] += dot(hid[c], tiles)
        gh = dot(go[...], tiles, 1, 1)
        g, u = gate[c].astype(F32), up[c].astype(F32)
        sg = jax.nn.sigmoid(g)
        ggu[c] = (gh * u * sg * (1.0 + g * (1.0 - sg))).astype(BF)
        ggu[c + 4] = (gh * g * sg).astype(BF)
        for i in range(0, 8, 2):
            term = dot(hid[c], go[:, 128 * i : 128 * i + 256], 0, 0).astype(BF)
            for n in range(2):
                w[3, c, :, :, 5 * (i + n) : 5 * (i + n) + 5] = term[:, 128 * n : 128 * n + 128].reshape(4, 2, 5, 16, 128)
        return 0

    lax.fori_loop(0, 4, reduce_, 0)
    rs.offer(3)
    out_ref[...] = (acc[:, 0:D] * live).astype(BF)

    acc[...] = jnp.zeros((ROWS, 1024), F32)

    def back(c, _):
        gg = ggu[c]
        acc[...] += dot(gg, in_tiles(c), 1, 1)
        for i in range(0, 5, 2):
            term = dot(n2p[...], gg[:, 128 * i : min(128 * i + 256, 640)], 0, 0).astype(BF)
            for n in range(min(2, 5 - i)):
                w[1:3, :, :, :, 5 * c + i + n] = term[:, 128 * n : 128 * n + 128].reshape(2, 4, 4, 2, 16, 128)
        return 0

    lax.fori_loop(0, 4, back, 0)
    rs.first((3, 4))
    lax.fori_loop(4, 8, back, 0)
    rs.offer(1)
    rs.offer(2)
    rs.second((3, 4))
    gn = acc[...]
    hi = gn.astype(BF)
    lo = (gn - hi.astype(F32)).astype(BF)

    def close(k, part):
        cols = slice(128 * k, 128 * k + 128)
        return dot(hi[:, cols], spread[k, part], 1, 1) + dot(lo[:, cols], spread[k, part], 1, 1)

    before, same = slice(0, 128), slice(128, 256)
    gn = side([close(k, same) + close(k + 1, before) if k < 7 else close(k, same) for k in range(8)])
    n2 = mid[...] * inv2
    d_gain2 = jnp.sum(gn * n2, axis=0, keepdims=True)
    u = gn * gain2
    gm = go[...].astype(F32) + inv2 * (u - n2 * mean_of(u * n2))
    mid[...] = gm
    gmb = gm.astype(BF)
    gmix = jnp.zeros((ROWS, D), F32)
    for i in range(0, 8, 2):
        gmix = gmix + dot(gmb[:, 128 * i : 128 * i + 256], side([out_tiles(i), out_tiles(i + 1)]), 1, 1)
    term = dot(mixed[:, 0:D], gmb, 0, 0).astype(BF)
    for i in range(8):
        put_out(i, term[:, 128 * i : 128 * i + 128])
    rs.first((1, 3))
    mixed[:, 0:D] = gmix.astype(BF)
    gq[12] = jnp.zeros((ROWS, 128), F32)

    def attend_back(m, _):
        rows = rows_of(m)
        for g in range(KV):
            heads = [3 * g + i for i in range(3)]
            q = jnp.concatenate([jnp.where(half[h % 2], qs[h // 2, rows, :], zero_b) for h in heads], axis=0)
            gmx = jnp.concatenate([jnp.where(half[h % 2], mixed[rows, chunk(h)], zero_b) for h in heads], axis=0)
            p = prob[m, g]
            gv = dot(p.astype(BF), gmx, 0, 0)
            gp = dot(gmx, vv[g, rows, :], 1, 1)
            gs = (p * (gp - jnp.sum(p * gp, axis=-1, keepdims=True))).astype(BF)
            gqs = dot(gs, kk[g, rows, :]) * 0.125
            gk = dot(gs, q, 0, 0) * 0.125
            for i, h in enumerate(heads):
                gq[h // 2, rows, :] = jnp.where(half[h % 2], gqs[MROWS * i : MROWS * i + MROWS], gq[h // 2, rows, :])
            for head, value in ((15 + g, gk), (20 + g, gv)):
                value = value + pltpu.roll(value, 64, 1)
                gq[head // 2, rows, :] = jnp.where(half[head % 2], value, gq[head // 2, rows, :])
        return 0

    lax.fori_loop(0, 2, attend_back, 0)
    rs.second((1, 3))
    lax.fori_loop(2, MB, attend_back, 0)

    for c in range(13):
        y = gq[c]
        if c < 10:
            y = y * cos_t - swap(y) * sin_t
        gqb[c] = y.astype(BF)
    gn1 = jnp.zeros((ROWS, D), F32)
    for c in range(0, 13, 2):
        group = list(range(c, min(c + 2, 13)))
        gy = side([gqb[i] for i in group])
        gn1 = gn1 + dot(gy, side([qkv_tiles(i) for i in group]), 1, 1)
        term = dot(nrm[:, 0:D], gy, 0, 0).astype(BF)
        for n, i in enumerate(group):
            put_qkv(i, term[:, 128 * n : 128 * n + 128])
    acc[:, 896:1024] = jnp.zeros((ROWS, 128), F32)
    acc[:, 0:D] = gn1
    gn1 = acc[...]
    n1 = xs[...].astype(F32) * inv1
    d_gain1 = jnp.sum(gn1 * n1, axis=0, keepdims=True)
    both_gains = jnp.concatenate([v[:, 128 * i : 128 * i + 128] for v in (d_gain1, d_gain2) for i in range(8)], axis=0)
    w[0, 0, 0, 0, 39] = both_gains.astype(BF)
    rs.offer(0)
    u = gn1 * gain1
    res = mid[...] + inv1 * (u - n1 * mean_of(u * n1))
    gin_ref[...] = res[:, 0:D].astype(BF)
    rs.first((0, 1))
    rs.finish()


def layer(block, inputs, cotangent, segments, counts):
    vm = pl.BlockSpec(memory_space=pltpu.VMEM)
    dma = pltpu.SemaphoreType.DMA
    return pl.pallas_call(
        layer_kernel,
        out_shape=(
            jax.ShapeDtypeStruct((ROWS, D), BF),
            jax.ShapeDtypeStruct((ROWS, D), BF),
            jax.ShapeDtypeStruct((TILES, 16, 128), F32),
        ),
        in_specs=[vm] * 7,
        out_specs=(vm, vm, vm),
        scratch_shapes=[
            pltpu.VMEM((4, 4, 4, 2, TILES, 16, 128), BF),
            pltpu.VMEM((3, 4, 4, TILES, 16, 128), BF),
            pltpu.VMEM((3, 4, 4, TILES, 16, 128), BF),
            pltpu.VMEM((3, 4, TILES, 16, 128), BF),
            pltpu.VMEM((3, TILES, 16, 128), BF),
            pltpu.VMEM((3, 4, TILES, 16, 128), BF),
            pltpu.VMEM((3, TILES, 16, 128), BF),
            pltpu.VMEM((3, 14, 16, 128), BF),
            pltpu.VMEM((ROWS, 1024), BF),
            pltpu.VMEM((ROWS, 1024), BF),
            pltpu.VMEM((ROWS, 1024), BF),
            pltpu.VMEM((8, ROWS, 128), BF),
            pltpu.VMEM((KV, ROWS, 128), BF),
            pltpu.VMEM((KV, ROWS, 128), BF),
            pltpu.VMEM((MB, KV, ROWS, MROWS), F32),
            pltpu.VMEM((ROWS, 1024), BF),
            pltpu.VMEM((ROWS, 1024), F32),
            pltpu.VMEM((ROWS, 1024), BF),
            pltpu.VMEM((4, ROWS, 640), BF),
            pltpu.VMEM((4, ROWS, 640), BF),
            pltpu.VMEM((4, ROWS, 640), BF),
            pltpu.VMEM((8, ROWS, 640), BF),
            pltpu.VMEM((13, ROWS, 128), F32),
            pltpu.VMEM((13, ROWS, 128), BF),
            pltpu.VMEM((8, 256, 128), BF),
            pltpu.VMEM((ROWS, 1024), F32),
            dma((99,)), dma((99,)), dma((91,)), dma((91,)), dma,
            dma((120,)), dma((120,)), dma((4,)), dma((4,)),
        ],
        compiler_params=pltpu.CompilerParams(collective_id=0, has_side_effects=True, vmem_limit_bytes=VMEM_BYTES),
    )(block, inputs, cotangent, *tables(segments, counts))


def shards(inputs, cotangent, flat_weights, counts, segments):
    d = lax.axis_index("fsdp")
    block_out, input_grad, block_grad = layer(to_block(flat_weights, d), inputs, cotangent, segments, counts)
    return block_out, input_grad, from_block(block_grad, d)


def solution(mesh):
    in_specs = (P("fsdp", None), P("fsdp", None), P("fsdp"), P("fsdp"), P("fsdp"))
    out_specs = (P("fsdp", None), P("fsdp", None), P("fsdp"))
    return jax.shard_map(shards, mesh=mesh, in_specs=in_specs, out_specs=out_specs, check_vma=False)
```

```python
import functools
import math

import jax
import jax.numpy as jnp
from jax import lax
from jax.experimental import pallas as pl
from jax.experimental.pallas import tpu as pltpu
from jax.sharding import PartitionSpec as P

D = 960
H = 15
KV = 5
HD = 64
FF = 2560
MB = 3
EPSILON = 1e-05
GAINS = 2 * D
BLOCK = 76800
N = 128
BF = jnp.bfloat16
F32 = jnp.float32
VMEM_BYTES = 63 * 1024 * 1024

MESH = pl.DeviceIdType.MESH
TILES = 40
PARTS = ((0, 7, 14), (14, 20, 27), (27, 33, 40))


def place():
    me = lax.axis_index("fsdp")
    return [me // 32, (me // 8) % 4, (me // 2) % 4], me % 2


def device_at(coords, core):
    return (coords[0] * 32 + coords[1] * 8 + coords[2] * 2 + core,)


def moved(coords, dim, by):
    out = list(coords)
    out[dim] = (out[dim] + by + 4) % 4
    return out


def beside(by):
    return (lax.axis_index("fsdp") + by) % N


def greet(coords, core):
    barrier = pltpu.get_barrier_semaphore()
    for dim in range(3):
        for by in (1, -1, 2):
            pl.semaphore_signal(barrier, inc=1, device_id=device_at(moved(coords, dim, by), core), device_id_type=MESH)
    pl.semaphore_signal(barrier, inc=1, device_id=device_at(coords, 1 - core), device_id_type=MESH)
    for by in (1, N - 1):
        pl.semaphore_signal(barrier, inc=1, device_id=(beside(by),), device_id_type=MESH)
    pl.semaphore_wait(barrier, 12)


def gather_into(w, blk, coords, core, send, recv, pair_send, pair_recv, own_sem):
    sent, ids, pair_ids, swapped = [], {}, {}, []
    sibling = device_at(coords, 1 - core)

    def at(fixed, tiles, which):
        index = [slice(None)] * 3
        for dim, value in fixed.items():
            index[dim] = value
        return w.at[(*index, which, rng(tiles))]

    def push(src, dst, device, ssem, rsem):
        copy = pltpu.make_async_remote_copy(src_ref=src, dst_ref=dst, send_sem=ssem, recv_sem=rsem, device_id=device, device_id_type=MESH)
        copy.start()
        sent.append(copy)

    def forward(key, src, dst, dim, step):
        k = ids.setdefault(key, len(ids))
        push(src, dst, device_at(moved(coords, dim, step), core), send.at[k], recv.at[k])

    def arrived(key, ref):
        landed(ref, recv.at[ids[key]])

    def swap(fixed, tiles):
        k = len(swapped)
        push(at(fixed, tiles, core), at(fixed, tiles, core), sibling, pair_send.at[k], pair_recv.at[k])
        swapped.append((fixed, tiles, k))

    def half(p, sign, number):
        lo, mid, hi = PARTS[p]
        return ((lo, mid), (mid, hi))[(number == 1) ^ (sign < 0)]

    def whole(p):
        return (PARTS[p][0], PARTS[p][2])

    def near(dim, step):
        return moved(coords, dim, step)[dim]

    local = pltpu.make_async_copy(blk, w.at[(*coords, core)], own_sem)
    local.start()
    parts = range(3)
    dims = [[(p + k) % 3 for k in range(3)] for p in parts]
    for p in parts:
        a, b, c = dims[p]
        for step in (2, 1, -1):
            forward((p, 0, step), blk.at[rng(whole(p))], at({a: coords[a], b: coords[b], c: coords[c]}, whole(p), core), a, step)
    push(blk, w.at[(*coords, core)], sibling, pair_send.at[90], pair_recv.at[90])
    local.wait()

    def line(p, step):
        a, b, c = dims[p]
        return {b: near(b, step), c: coords[c]}

    def sheet(p, group, step):
        a, b, c = dims[p]
        return {b: near(b, group), c: near(c, step)}

    def send_line(p, number):
        for sign in (1, -1):
            ref = at(line(p, 0), half(p, sign, number), core)
            forward((p, 1, sign, number), ref, ref, dims[p][1], sign)

    def send_sheet(p, group, number):
        for sign in (1, -1):
            ref = at(sheet(p, group, 0), half(p, sign, number), core)
            forward((p, 2, group, sign, number), ref, ref, dims[p][2], sign)

    def relay_line(p):
        for sign in (1, -1):
            ref = at(line(p, -sign), half(p, sign, 0), core)
            arrived((p, 1, sign, 0), ref)
            forward((p, 1, sign, 2), ref, ref, dims[p][1], sign)

    def relay_sheet(p, group):
        for sign in (1, -1):
            ref = at(sheet(p, group, -sign), half(p, sign, 0), core)
            arrived((p, 2, group, sign, 0), ref)
            forward((p, 2, group, sign, 2), ref, ref, dims[p][2], sign)

    def rest_sheet(p, group):
        for sign in (1, -1):
            arrived((p, 2, group, sign, 1), at(sheet(p, group, -sign), half(p, sign, 1), core))
            swap(sheet(p, group, -sign), whole(p))

    def last_sheet(p, group):
        for sign in (1, -1):
            arrived((p, 2, group, sign, 2), at(sheet(p, group, 2), half(p, sign, 2), core))
        swap(sheet(p, group, 2), whole(p))

    for p in parts:
        a, b, c = dims[p]
        for step in (1, -1, 2):
            fixed = {a: near(a, -step), b: coords[b], c: coords[c]}
            arrived((p, 0, step), at(fixed, whole(p), core))
            swap(fixed, whole(p))
        for number in (0, 1):
            send_line(p, number)
    for p in parts:
        for number in (0, 1):
            send_sheet(p, 0, number)
    for p in parts:
        relay_line(p)
    for p in parts:
        for sign in (1, -1):
            arrived((p, 1, sign, 1), at(line(p, -sign), half(p, sign, 1), core))
        for sign in (1, -1):
            for number in (0, 1):
                send_sheet(p, -sign, number)
    for p in parts:
        relay_sheet(p, 0)
    for p in parts:
        for sign in (1, -1):
            arrived((p, 1, sign, 2), at(line(p, 2), half(p, sign, 2), core))
        for number in (0, 1):
            send_sheet(p, 2, number)
        for step in (1, -1, 2):
            swap(line(p, step), whole(p))
    for p in parts:
        rest_sheet(p, 0)
    for group in (-1, 1, 2):
        for p in parts:
            relay_sheet(p, group)
        for p in parts:
            rest_sheet(p, group)
    for group in (0, -1, 1, 2):
        for p in parts:
            last_sheet(p, group)
    landed(w.at[(*coords, 1 - core)], pair_recv.at[90])
    for fixed, tiles, k in swapped:
        landed(at(fixed, tiles, 1 - core), pair_recv.at[k])
    return sent


def pack(rows_48, rows_80, rows_15, gains, d):
    qkv = jnp.pad(rows_48, ((0, 0), (0, 64))).reshape(3, 16, 13, 128).transpose(2, 0, 1, 3).reshape(39, 16, 128)
    qkv = jnp.concatenate([qkv, jnp.where(d == 0, gains, jnp.zeros_like(gains))[None]], axis=0)
    square = jnp.pad(rows_80, ((0, 0), (0, 64))).reshape(5, 16, 8, 128).transpose(2, 0, 1, 3).reshape(40, 16, 128)
    wide = jnp.pad(rows_15, ((0, 1), (0, 0))).reshape(16, 40, 128).transpose(1, 0, 2)
    return kind(d, qkv, square, wide)


def kind(d, qkv, square, wide):
    return jnp.where(d < 20, qkv, jnp.where((d >= 32) & (d < 96), wide, square))


def to_block(shard, d):
    none = jnp.zeros((GAINS,), BF)
    flat = lax.dynamic_slice(jnp.concatenate([shard, none]), (GAINS - 15 * d,), (BLOCK,))
    gains = jnp.pad(shard[:GAINS].reshape(2, D), ((0, 0), (0, 64))).reshape(16, 128)
    block = pack(flat.reshape(48, 1600), flat.reshape(80, D), flat.reshape(15, 2 * FF), gains, d)
    e = (d + N - 1) % N
    last = lax.dynamic_slice(jnp.concatenate([none, shard[:GAINS]]), (GAINS - 15 - 15 * e,), (GAINS,))
    qkv = jnp.stack([jnp.pad(last[:320], (1280, 64)).reshape(13, 128), jnp.pad(last[320:], (0, 64)).reshape(13, 128)], axis=1)
    qkv = jnp.pad(jnp.pad(qkv[:, None], ((0, 0), (2, 0), (0, 0), (0, 0))).reshape(39, 2, 128), ((0, 1), (0, 0), (0, 0)))
    square = jnp.pad(last.reshape(2, D), ((0, 0), (0, 64))).reshape(2, 8, 128).transpose(1, 0, 2)
    square = jnp.pad(square[:, None], ((0, 0), (4, 0), (0, 0), (0, 0))).reshape(40, 2, 128)
    wide = jnp.pad(last.reshape(15, 1, 128), ((25, 0), (0, 1), (0, 0)))
    return block, kind(e, qkv, square, wide).reshape(5, 16, 128)


def from_block(rows, prev, d):
    tiles = rows.reshape(40, 16, 128)
    qkv = tiles[:39].reshape(13, 3, 16, 128).transpose(1, 2, 0, 3).reshape(48, 1664)[:, :1600].reshape(-1)
    square = tiles.reshape(8, 5, 16, 128).transpose(1, 2, 0, 3).reshape(80, 1024)[:, :D].reshape(-1)
    wide = tiles.transpose(1, 0, 2)[:15].reshape(-1)
    flat = kind(d, qkv, square, wide)
    two = prev[:, 2:39:3].reshape(2, 1664)
    before = kind(
        d - 1,
        jnp.concatenate([two[0, 1280:1600], two[1, :1600]]),
        prev[:, 4::5].reshape(2, 1024)[:, :D].reshape(-1),
        prev[0, 25:].reshape(-1),
    )
    before = jnp.where(d == 0, tiles[39].reshape(2, 1024)[:, :D].reshape(-1), before)
    return lax.dynamic_slice(jnp.concatenate([before, flat]), (15 * d,), (BLOCK + 15,))


ROWS = 240
MROWS = 80


def tables(segment_ids, counts):
    seg = segment_ids.reshape(MB, MROWS)
    places = jnp.arange(MROWS, dtype=jnp.int32)
    same = seg[:, :, None] == seg[:, None, :]
    first_row = jnp.min(jnp.where(same, places[None, None, :], MROWS), axis=2)
    position = (places[None, :] - first_row).astype(F32).reshape(ROWS)
    freq = jnp.exp(jnp.arange(HD // 2, dtype=F32) * (-2.0 * math.log(10000.0) / HD))
    angle = position[:, None] * freq[None, :]
    cos, sin = jnp.cos(angle), jnp.sin(angle)
    cos_t = jnp.concatenate([cos, cos, cos, cos], axis=1)
    sin_t = jnp.concatenate([-sin, sin, -sin, sin], axis=1)
    allowed = same & (places[None, None, :] <= places[None, :, None])
    bias = jnp.where(allowed, 0.0, -1e30).astype(F32).reshape(ROWS, MROWS)
    live = (places[None, :] < counts[:, None]).astype(F32).reshape(ROWS, 1)
    return cos_t, sin_t, bias, jnp.broadcast_to(live, (ROWS, 128))


def dot(a, b, ca=1, cb=0):
    return lax.dot_general(a, b, (((ca,), (cb,)), ((), ())), preferred_element_type=F32)


def mean_of(value):
    return jnp.sum(value, axis=-1, keepdims=True) * (1.0 / D)


class Flow:
    def __init__(self, name, dims, tiles, bufs, first_plane):
        self.name, self.dims, self.tiles, self.bufs, self.first_plane = name, dims, tiles, bufs, first_plane

    def half(self, sign, which):
        lo, mid, hi = self.tiles
        pair = ((lo, mid), (mid, hi))
        return pair[which] if sign > 0 else pair[1 - which]


class Reduce:
    def __init__(self, w, pair_buf, bufs, red, coords, core, send, recv, pair_send, pair_recv):
        self.w, self.pair_buf, self.red = w, pair_buf, red
        self.coords, self.core = coords, core
        self.send, self.recv, self.pair_send, self.pair_recv = send, recv, pair_send, pair_recv
        self.sent, self.ids = [], {}
        b1, b2, b3, q1, q2, z2 = bufs
        self.P0 = Flow("P0", (0, 1, 2), (0, 4, 8), (b1, b2, b3), 0)
        self.P1 = Flow("P1", (1, 2, 0), (8, 16, 24), (b1, b2, None), 0)
        self.P2 = Flow("P2", (2, 1, 0), (24, 32, 40), (b1, b2, None), 0)
        self.Q1 = Flow("Q1", (1, 2, 0), (0, 10, 20), (q1, q2, None), 0)
        self.Q2 = Flow("Q2", (2, 1, 0), (20, 30, 40), (q1, q2, None), 0)
        self.Z1 = Flow("Z1", (1, 2, 0), (8, 24, 40), (None, None, b3), 0)
        self.Z2 = Flow("Z2", (1, 2, 0), (0, 4, 8), (None, None, z2), 0)

    def copy(self, src, dst, device, ssem, rsem):
        return pltpu.make_async_remote_copy(
            src_ref=src, dst_ref=dst, send_sem=ssem, recv_sem=rsem, device_id=device, device_id_type=MESH
        )

    def offer(self, k, z, tiles=(0, TILES), xs=(0, 4)):
        x, t = rng(xs), rng(tiles)
        one = self.copy(
            self.w.at[z, x, :, 1 - self.core, t], self.pair_buf.at[z % 3, x, :, t],
            device_at(self.coords, 1 - self.core), self.pair_send.at[k], self.pair_recv.at[k],
        )
        one.start()
        self.sent.append((None, one))

    def ready(self, k, z, tiles=(0, TILES), xs=(0, 4)):
        slot, span = z % 3, rng(tiles)
        landed(self.pair_buf.at[slot, rng(xs), :, span], self.pair_recv.at[k])

        def body(t, _):
            at = (z, xs[0] + t // 4, t % 4, self.core, span)
            self.w[at] = self.w[at] + self.pair_buf[slot, xs[0] + t // 4, t % 4, span]
            return 0

        lax.fori_loop(0, 4 * (xs[1] - xs[0]), body, 0)

    def sem(self, flow, phase, planes, sign, number):
        return self.ids.setdefault((flow.name, phase, planes, sign, number), len(self.ids))

    def along(self, dim, step):
        return moved(self.coords, dim, step)[dim]

    def slot(self, flow, phase, planes, sign, number):
        which = 2 if number == 0 else (0 if sign > 0 else 1)
        inner = []
        for d in range(3):
            if d in flow.dims[phase + 1 :]:
                inner.append(pl.ds(planes[0], planes[1] - planes[0]) if d == 0 else slice(None))
        if flow.name in ("Q1", "Q2"):
            inner = inner[1:]
        tiles = flow.half(sign, 1 if number == 1 else 0)
        return flow.bufs[phase].at[(which, *inner, rng(tiles))]

    def ship(self, flow, phase, planes, sign, number):
        dim = flow.dims[phase]
        tiles = flow.half(sign, 1 if number == 1 else 0)
        fixed = []
        for d in range(3):
            if d in flow.dims[:phase]:
                fixed.append(self.coords[d])
            elif d == dim:
                fixed.append(self.along(d, 2 if number == 0 else sign))
            else:
                fixed.append(pl.ds(planes[0], planes[1] - planes[0]) if d == 0 else slice(None))
        slot = self.slot(flow, phase, planes, sign, number)
        if flow.name in ("Q1", "Q2"):
            fixed[0] = 0
        k = self.sem(flow, phase, planes, sign, number)
        return self.copy(
            self.w.at[(*fixed, self.core, rng(tiles))], slot,
            device_at(moved(self.coords, dim, sign), self.core), self.send.at[k], self.recv.at[k],
        )

    def go(self, flow, phase, planes, sign, number, guard=None):
        one = self.ship(flow, phase, planes, sign, number)
        if guard is None:
            one.start()
        else:
            pl.when(guard)(one.start)
        self.sent.append((guard, one))

    def loop(self, flow, phase, planes, coord, fn):
        dims = flow.dims
        free = [d for d in range(3) if d in dims[phase + 1 :]]
        sizes = [planes[1] - planes[0] if d == 0 else 4 for d in free]

        def body(t, _):
            inner = []
            if len(free) == 2:
                inner = [t // 4 + (planes[0] if free[0] == 0 else 0), t % 4]
            elif len(free) == 1:
                inner = [t + (planes[0] if free[0] == 0 else 0)]
            at = []
            for d in range(3):
                if d in free:
                    at.append(inner[free.index(d)])
                elif d == dims[phase]:
                    at.append(coord)
                else:
                    at.append(self.coords[d])
            if flow.name in ("Q1", "Q2"):
                at[0] = 0
                inner = inner[1:]
            fn((*at, self.core), tuple(inner))
            return 0

        count = math.prod(sizes)
        if count == 1:
            body(0, 0)
        else:
            lax.fori_loop(0, count, body, 0)

    def add_half(self, flow, phase, planes, sign):
        landed(self.slot(flow, phase, planes, sign, 0), self.recv.at[self.sem(flow, phase, planes, sign, 0)])
        tiles = rng(flow.half(sign, 0))
        buf = flow.bufs[phase]

        def fold(at, inner):
            self.w[(*at, tiles)] = self.w[(*at, tiles)] + buf[(2, *inner, tiles)]

        self.loop(flow, phase, planes, self.along(flow.dims[phase], sign), fold)

    def add_all(self, flow, phase, planes):
        for sign in (1, -1):
            for number in (1, 2):
                landed(self.slot(flow, phase, planes, sign, number), self.recv.at[self.sem(flow, phase, planes, sign, number)])
        tiles = rng((flow.tiles[0], flow.tiles[2]))
        buf = flow.bufs[phase]

        def total(at, inner):
            value = self.w[(*at, tiles)].astype(F32) + buf[(0, *inner, tiles)].astype(F32) + buf[(1, *inner, tiles)].astype(F32)
            if phase == 2:
                self.red[pl.ds(16 * flow.tiles[0], 16 * (flow.tiles[2] - flow.tiles[0])), :] = value.reshape(-1, 128)
            else:
                self.w[(*at, tiles)] = value.astype(BF)

        self.loop(flow, phase, planes, self.coords[flow.dims[phase]], total)

    def plane_in(self, planes, step):
        z = self.along(0, step)
        return (z >= planes[0]) & (z < planes[1])

    def open(self, planes, flows, along_z=False):
        for number in (0, 1):
            for sign in (1, -1):
                for flow in flows:
                    self.go(flow, 0, planes, sign, number)
                if along_z:
                    one = self.ship(self.P0, 0, (0, 4), sign, number)
                    pl.when(self.plane_in(planes, 2 if number == 0 else sign))(one.start)

    def relay(self, planes, flows, along_z=False):
        for sign in (1, -1):
            if along_z:

                @pl.when(self.plane_in(planes, sign))
                def _():
                    self.add_half(self.P0, 0, (0, 4), sign)
                    self.ship(self.P0, 0, (0, 4), sign, 2).start()

            for flow in flows:
                self.add_half(flow, 0, planes, sign)
                self.go(flow, 0, planes, sign, 2)

    def start(self, flow, phase, planes, guards=None):
        for number in (0, 1):
            for sign in (1, -1):
                self.go(flow, phase, planes, sign, number, guards and guards(sign, number))

    def pass_on(self, flow, phase, planes, guards=None):
        for sign in (1, -1):
            guard = guards and guards(sign, 2)
            if guard is None:
                self.add_half(flow, phase, planes, sign)
            else:
                pl.when(guard)(functools.partial(self.add_half, flow, phase, planes, sign))
            self.go(flow, phase, planes, sign, 2, guard)

    def whole(self, flow):
        return rng((flow.tiles[0], flow.tiles[2]))

    def direct(self, flow, phase, planes, step):
        dim = flow.dims[phase]
        fixed, inner = [], []
        for d in range(3):
            if d in flow.dims[:phase]:
                fixed.append(self.coords[d])
            elif d == dim:
                fixed.append(self.along(d, step))
            else:
                span = pl.ds(planes[0], planes[1] - planes[0]) if d == 0 else slice(None)
                fixed.append(span)
                inner.append(span)
        if flow.name in ("Q1", "Q2"):
            fixed[0] = 0
            inner = inner[1:]
        k = self.sem(flow, phase, planes, step, 3)
        return self.copy(
            self.w.at[(*fixed, self.core, self.whole(flow))], flow.bufs[phase].at[(step % 4 - 1, *inner, self.whole(flow))],
            device_at(moved(self.coords, dim, step), self.core), self.send.at[k], self.recv.at[k],
        )

    def start_direct(self, flow, phase, planes, guards=None):
        for step in (2, 1, -1):
            guard = guards and guards(step)
            one = self.direct(flow, phase, planes, step)
            if guard is None:
                one.start()
            else:
                pl.when(guard)(one.start)
            self.sent.append((guard, one))

    def add_direct(self, flow, phase, planes):
        for step in (1, -1, 2):
            self.direct(flow, phase, planes, step).wait_recv()
        tiles = self.whole(flow)
        buf = flow.bufs[phase]

        def total(at, inner):
            value = self.w[(*at, tiles)].astype(F32)
            for slot in range(3):
                value = value + buf[(slot, *inner, tiles)].astype(F32)
            if phase == 2:
                self.red[pl.ds(16 * flow.tiles[0], 16 * (flow.tiles[2] - flow.tiles[0])), :] = value.reshape(-1, 128)
            else:
                self.w[(*at, tiles)] = value.astype(BF)

        self.loop(flow, phase, planes, self.coords[flow.dims[phase]], total)

    def finish(self):
        late, early, every = (0, 1), (1, 4), (0, 4)
        z = self.coords[0]
        upper = lambda sign, number=0: z != 0
        to_zero = lambda step: self.along(0, step) == 0
        for number in (0, 1, 2):
            for sign in (1, -1):
                guard = self.plane_in((1, 4), 2 if number == 0 else sign)
                self.sent.append((guard, self.ship(self.P0, 0, every, sign, number)))
        for flow in (self.P1, self.P2):
            for planes in ((3, 4), (1, 3)):
                self.add_all(flow, 0, planes)
            self.start(flow, 1, early)
        self.relay(late, (self.Q1, self.Q2))
        pl.when(z != 0)(lambda: self.add_all(self.P0, 0, every))
        self.start(self.P0, 1, every, upper)
        for flow in (self.P1, self.P2):
            self.pass_on(flow, 1, early)
        for flow in (self.Q1, self.Q2):
            self.add_all(flow, 0, late)
            self.start_direct(flow, 1, late)
        self.pass_on(self.P0, 1, every, upper)
        for flow in (self.P1, self.P2):
            self.add_all(flow, 1, early)
        for flow in (self.Q1, self.Q2):
            self.add_direct(flow, 1, late)
        self.start_direct(self.Z1, 2, every)
        self.start_direct(self.Z2, 2, every, to_zero)
        pl.when(z != 0)(lambda: self.add_all(self.P0, 1, every))
        self.start_direct(self.P0, 2, every, upper)
        self.add_direct(self.Z1, 2, every)
        pl.when(z != 0)(lambda: self.add_direct(self.P0, 2, every))
        pl.when(z == 0)(lambda: self.add_direct(self.Z2, 2, every))

    def drain(self):
        for guard, one in self.sent:
            if guard is None:
                one.wait_send()
            else:
                pl.when(guard)(one.wait_send)


def rng(tiles):
    return pl.ds(tiles[0], tiles[1] - tiles[0])


def landed(dst, rsem):
    pltpu.make_async_copy(dst, dst, rsem).wait()


def layer_kernel(
    own_ref, tail_ref, x_ref, c_ref, cos_ref, sin_ref, bias_ref, live_ref,
    out_ref, gin_ref, red_ref, prev_ref,
    blk, tail_in, tail_out, tail_back, tail_sem, w, pair_buf, b1, b2, b3, q1, q2, z2, xs, go, nrm, qs, kk, vv, prob, mixed, mid, n2p, gate, up, hid, ggu, gq, gqb, spread, acc,
    send, recv, pair_send, pair_recv, own_sem, rs_send, rs_recv, rp_send, rp_recv,
):
    coords, core = place()
    greet(coords, core)
    handed = pltpu.make_async_remote_copy(
        src_ref=tail_ref, dst_ref=tail_in, send_sem=tail_sem.at[0], recv_sem=tail_sem.at[1],
        device_id=(beside(N - 1),), device_id_type=MESH,
    )
    handed.start()
    r = lax.broadcasted_iota(jnp.int32, (640, 80), 0)
    c = lax.broadcasted_iota(jnp.int32, (640, 80), 1)
    last_rows = jnp.where((r // 16 == c // 2) & (r % 16 == 14 + c % 2), 1.0, 0.0).astype(BF)
    handed.wait()
    blk[...] = own_ref[...] + dot(last_rows, tail_in[...].reshape(80, 128)).astype(BF).reshape(TILES, 16, 128)
    sent = gather_into(w, blk, coords, core, send, recv, pair_send, pair_recv, own_sem)
    rs = Reduce(w, pair_buf, (b1, b2, b3, q1, q2, z2), red_ref, coords, core, rs_send, rs_recv, rp_send, rp_recv)

    def join(parts):
        return jnp.concatenate(parts, axis=0)

    def qkv_tiles(c):
        t = slice(3 * c, 3 * c + 3)
        return join([w[0, 0:2, :, :, t].reshape(768, 128), w[0, 2, 0:2, :, t].reshape(192, 128)])

    def put_qkv(c, v):
        t = slice(3 * c, 3 * c + 3)
        w[0, 0:2, :, :, t] = v[:768].reshape(2, 4, 2, 3, 16, 128)
        w[0, 2, 0:2, :, t] = v[768:].reshape(2, 2, 3, 16, 128)

    def out_tiles(c):
        t = slice(5 * c, 5 * c + 5)
        return join([w[0, 2, 2:4, :, t].reshape(320, 128), w[0, 3, :, :, t].reshape(640, 128)])

    def put_out(c, v):
        t = slice(5 * c, 5 * c + 5)
        w[0, 2, 2:4, :, t] = v[:320].reshape(2, 2, 5, 16, 128)
        w[0, 3, :, :, t] = v[320:].reshape(4, 2, 5, 16, 128)

    def in_tiles(c):
        return side([w[1:3, :, :, :, 5 * c + i].reshape(1024, 128) for i in range(5)])

    def down_tiles(c):
        return side([w[3, c, :, :, 5 * i : 5 * i + 5].reshape(640, 128) for i in range(8)])

    def side(parts):
        return jnp.concatenate(parts, axis=1)

    lane = lax.broadcasted_iota(jnp.int32, (MROWS, 128), 1)
    half = (lane < 64, lane >= 64)
    lane_all = lax.broadcasted_iota(jnp.int32, (ROWS, 128), 1)
    low_all = lane_all < 64
    first_all = lane_all % 64 < 32

    def swap(v):
        return jnp.where(first_all, pltpu.roll(v, 96, 1), pltpu.roll(v, 32, 1))

    def both(v, h):
        other = pltpu.roll(v, 64, 1)
        return jnp.where(low_all, v, other) if h == 0 else jnp.where(low_all, other, v)

    for k in range(8):
        r = lax.broadcasted_iota(jnp.int32, (256, 128), 0) + 128 * (k - 1)
        c = lax.broadcasted_iota(jnp.int32, (256, 128), 1) + 128 * k
        spread[k] = jnp.where((r == (c // 16) * 15 + c % 16) & (c % 16 != 15), 1.0, 0.0).astype(BF)

    xs[:, 896:1024] = jnp.zeros((ROWS, 128), BF)
    xs[:, 0:D] = x_ref[...]
    go[:, 896:1024] = jnp.zeros((ROWS, 128), BF)
    live = live_ref[:, 0:1]
    go[:, 0:D] = (c_ref[...].astype(F32) * live).astype(BF)
    x = xs[...].astype(F32)
    inv1 = lax.rsqrt(mean_of(x * x) + EPSILON)
    gains = w[0, 0, 0, 0, 39].astype(F32)
    gain1 = side([gains[i : i + 1] for i in range(8)])
    gain2 = side([gains[8 + i : 9 + i] for i in range(8)])
    nrm[...] = (x * inv1 * gain1).astype(BF)

    cos_t, sin_t = cos_ref[...], sin_ref[...]
    for c in range(0, 13, 2):
        group = [qkv_tiles(i) for i in range(c, min(c + 2, 13))]
        y2 = dot(nrm[:, 0:D], side(group))
        for i in range(len(group)):
            y = y2[:, 128 * i : 128 * i + 128]
            if c + i < 10:
                y = y * cos_t + swap(y) * sin_t
            if c + i < 8:
                qs[c + i] = y.astype(BF)
            for h in range(2):
                head = 2 * (c + i) + h
                if 15 <= head < 20:
                    kk[head - 15] = both(y, h).astype(BF)
                if 20 <= head < 25:
                    vv[head - 20] = both(y, h).astype(BF)

    mixed[:, 896:1024] = jnp.zeros((ROWS, 128), BF)
    zero_b = jnp.zeros((MROWS, 128), BF)

    def rows_of(m):
        return pl.ds(pl.multiple_of(m * MROWS, MROWS), MROWS)

    def chunk(head):
        return pl.ds(128 * (head // 2), 128)

    def attend(m, _):
        rows = rows_of(m)
        bias = bias_ref[rows, :]
        bias3 = jnp.concatenate([bias, bias, bias], axis=0)
        for g in range(KV):
            heads = [3 * g + i for i in range(3)]
            q = jnp.concatenate([jnp.where(half[h % 2], qs[h // 2, rows, :], zero_b) for h in heads], axis=0)
            s = dot(q, kk[g, rows, :], 1, 1) * 0.125 + bias3
            e = jnp.exp(s - jnp.max(s, axis=-1, keepdims=True))
            p = e / jnp.sum(e, axis=-1, keepdims=True)
            prob[m, g] = p.astype(BF)
            o = dot(p.astype(BF), vv[g, rows, :]).astype(BF)
            for i, h in enumerate(heads):
                mixed[rows, chunk(h)] = jnp.where(half[h % 2], o[MROWS * i : MROWS * i + MROWS], mixed[rows, chunk(h)])
        return 0

    lax.fori_loop(0, MB, attend, 0)

    for c in range(0, 8, 2):
        cols = slice(128 * c, 128 * c + 256)
        mid[:, cols] = xs[:, cols].astype(F32) + dot(mixed[:, 0:D], side([out_tiles(c), out_tiles(c + 1)]))
    middle = mid[...]
    inv2 = lax.rsqrt(mean_of(middle * middle) + EPSILON)
    n2b = (middle * inv2 * gain2).astype(BF)
    n2p[:, 0:128] = dot(n2b[:, 0:128], spread[0, 128:256]).astype(BF)
    for k in range(1, 8):
        n2p[:, 128 * k : 128 * k + 128] = dot(n2b[:, 128 * k - 128 : 128 * k + 128], spread[k]).astype(BF)


    def expand(c, _):
        g = dot(n2p[...], in_tiles(c))
        u = dot(n2p[...], in_tiles(c + 4))
        gate[c] = g.astype(BF)
        up[c] = u.astype(BF)
        hid[c] = (g * jax.nn.sigmoid(g) * u).astype(BF)
        return 0

    lax.fori_loop(0, 4, expand, 0)
    for copy in sent:
        copy.wait_send()
    acc[...] = mid[...]

    def reduce_(c, _):
        tiles = down_tiles(c)
        acc[...] += dot(hid[c], tiles)
        gh = dot(go[...], tiles, 1, 1)
        g, u = gate[c].astype(F32), up[c].astype(F32)
        sg = jax.nn.sigmoid(g)
        ggu[c] = (gh * u * sg * (1.0 + g * (1.0 - sg))).astype(BF)
        ggu[c + 4] = (gh * g * sg).astype(BF)
        for i in range(0, 8, 2):
            term = dot(hid[c], go[:, 128 * i : 128 * i + 256], 0, 0).astype(BF)
            for n in range(2):
                w[3, c, :, :, 5 * (i + n) : 5 * (i + n) + 5] = term[:, 128 * n : 128 * n + 128].reshape(4, 2, 5, 16, 128)
        return 0

    lax.fori_loop(0, 2, reduce_, 0)
    rs.offer(0, 3, xs=(0, 2))
    lax.fori_loop(2, 4, reduce_, 0)
    rs.offer(1, 3, xs=(2, 4))
    out_ref[...] = (acc[:, 0:D] * live).astype(BF)

    acc[...] = jnp.zeros((ROWS, 1024), F32)

    def back(c, _):
        gg = ggu[c]
        acc[...] += dot(gg, in_tiles(c), 1, 1)
        for i in range(0, 5, 2):
            term = dot(n2p[...], gg[:, 128 * i : min(128 * i + 256, 640)], 0, 0).astype(BF)
            for n in range(min(2, 5 - i)):
                w[1:3, :, :, :, 5 * c + i + n] = term[:, 128 * n : 128 * n + 128].reshape(2, 4, 4, 2, 16, 128)
        return 0

    lax.fori_loop(0, 2, back, 0)
    rs.ready(0, 3, xs=(0, 2))
    rs.ready(1, 3, xs=(2, 4))
    rs.open((3, 4), (rs.P1, rs.P2), True)
    lax.fori_loop(2, 5, back, 0)
    rs.offer(2, 1, (0, 25))
    rs.offer(3, 2, (0, 25))
    lax.fori_loop(5, 8, back, 0)
    rs.offer(4, 1, (25, 40))
    rs.offer(5, 2, (25, 40))
    rs.relay((3, 4), (rs.P1, rs.P2), True)
    rs.ready(2, 1, (0, 25))
    rs.ready(3, 2, (0, 25))
    rs.open((1, 3), (rs.P1,), True)
    gn = acc[...]
    hi = gn.astype(BF)
    lo = (gn - hi.astype(F32)).astype(BF)

    def close(k, part):
        cols = slice(128 * k, 128 * k + 128)
        return dot(hi[:, cols], spread[k, part], 1, 1) + dot(lo[:, cols], spread[k, part], 1, 1)

    before, same = slice(0, 128), slice(128, 256)
    gn = side([close(k, same) + close(k + 1, before) if k < 7 else close(k, same) for k in range(8)])
    n2 = mid[...] * inv2
    d_gain2 = jnp.sum(gn * n2, axis=0, keepdims=True)
    u = gn * gain2
    gm = go[...].astype(F32) + inv2 * (u - n2 * mean_of(u * n2))
    mid[...] = gm
    gmb = gm.astype(BF)
    gmix = jnp.zeros((ROWS, D), F32)
    for i in range(0, 8, 2):
        gmix = gmix + dot(gmb[:, 128 * i : 128 * i + 256], side([out_tiles(i), out_tiles(i + 1)]), 1, 1)
    term = dot(mixed[:, 0:D], gmb, 0, 0).astype(BF)
    for i in range(8):
        put_out(i, term[:, 128 * i : 128 * i + 128])
    rs.ready(4, 1, (25, 40))
    rs.ready(5, 2, (25, 40))
    rs.open((1, 3), (rs.P2,))
    mixed[:, 0:D] = gmix.astype(BF)
    gq[12] = jnp.zeros((ROWS, 128), F32)

    def attend_back(m, _):
        rows = rows_of(m)
        for g in range(KV):
            heads = [3 * g + i for i in range(3)]
            q = jnp.concatenate([jnp.where(half[h % 2], qs[h // 2, rows, :], zero_b) for h in heads], axis=0)
            gmx = jnp.concatenate([jnp.where(half[h % 2], mixed[rows, chunk(h)], zero_b) for h in heads], axis=0)
            gv = dot(prob[m, g], gmx, 0, 0)
            p = prob[m, g].astype(F32)
            gp = dot(gmx, vv[g, rows, :], 1, 1)
            gs = (p * (gp - jnp.sum(p * gp, axis=-1, keepdims=True))).astype(BF)
            gqs = dot(gs, kk[g, rows, :]) * 0.125
            gk = dot(gs, q, 0, 0) * 0.125
            for i, h in enumerate(heads):
                gq[h // 2, rows, :] = jnp.where(half[h % 2], gqs[MROWS * i : MROWS * i + MROWS], gq[h // 2, rows, :])
            for head, value in ((15 + g, gk), (20 + g, gv)):
                value = value + pltpu.roll(value, 64, 1)
                gq[head // 2, rows, :] = jnp.where(half[head % 2], value, gq[head // 2, rows, :])
        return 0

    lax.fori_loop(0, 1, attend_back, 0)
    rs.relay((1, 3), (rs.P1,), True)
    lax.fori_loop(1, 2, attend_back, 0)
    rs.relay((1, 3), (rs.P2,))
    lax.fori_loop(2, MB, attend_back, 0)

    for c in range(13):
        y = gq[c]
        if c < 10:
            y = y * cos_t - swap(y) * sin_t
        gqb[c] = y.astype(BF)
    gn1 = jnp.zeros((ROWS, D), F32)
    for c in range(0, 13, 2):
        group = list(range(c, min(c + 2, 13)))
        gy = side([gqb[i] for i in group])
        gn1 = gn1 + dot(gy, side([qkv_tiles(i) for i in group]), 1, 1)
        term = dot(nrm[:, 0:D], gy, 0, 0).astype(BF)
        for n, i in enumerate(group):
            put_qkv(i, term[:, 128 * n : 128 * n + 128])
    acc[:, 896:1024] = jnp.zeros((ROWS, 128), F32)
    acc[:, 0:D] = gn1
    gn1 = acc[...]
    n1 = xs[...].astype(F32) * inv1
    d_gain1 = jnp.sum(gn1 * n1, axis=0, keepdims=True)
    both_gains = jnp.concatenate([v[:, 128 * i : 128 * i + 128] for v in (d_gain1, d_gain2) for i in range(8)], axis=0)
    w[0, 0, 0, 0, 39] = both_gains.astype(BF)
    rs.offer(6, 0, (0, 20))
    rs.offer(7, 0, (20, 40))
    u = gn1 * gain1
    res = mid[...] + inv1 * (u - n1 * mean_of(u * n1))
    gin_ref[...] = res[:, 0:D].astype(BF)
    rs.ready(6, 0, (0, 20))
    rs.open((0, 1), (rs.Q1,))
    rs.ready(7, 0, (20, 40))
    rs.open((0, 1), (rs.Q2,))
    rs.finish()
    for n in range(2):
        tail_out[n] = red_ref[pl.ds(14 + n, TILES, stride=16), :]
    handed = pltpu.make_async_remote_copy(
        src_ref=tail_out, dst_ref=tail_back, send_sem=tail_sem.at[2], recv_sem=tail_sem.at[3],
        device_id=(beside(1),), device_id_type=MESH,
    )
    handed.start()
    rs.drain()
    handed.wait()
    prev_ref[...] = tail_back[...]


def layer(block, tail, inputs, cotangent, segments, counts):
    vm = pl.BlockSpec(memory_space=pltpu.VMEM)
    dma = pltpu.SemaphoreType.DMA
    return pl.pallas_call(
        layer_kernel,
        out_shape=(
            jax.ShapeDtypeStruct((ROWS, D), BF),
            jax.ShapeDtypeStruct((ROWS, D), BF),
            jax.ShapeDtypeStruct((TILES * 16, 128), F32),
            jax.ShapeDtypeStruct((2, TILES, 128), F32),
        ),
        in_specs=[vm] * 8,
        out_specs=(vm, vm, vm, vm),
        scratch_shapes=[
            pltpu.VMEM((TILES, 16, 128), BF),
            pltpu.VMEM((5, 16, 128), BF),
            pltpu.VMEM((2, TILES, 128), F32),
            pltpu.VMEM((2, TILES, 128), F32),
            dma((4,)),
            pltpu.VMEM((4, 4, 4, 2, TILES, 16, 128), BF),
            pltpu.VMEM((3, 4, 4, TILES, 16, 128), BF),
            pltpu.VMEM((3, 4, 4, TILES, 16, 128), BF),
            pltpu.VMEM((3, 4, TILES, 16, 128), BF),
            pltpu.VMEM((3, TILES, 16, 128), BF),
            pltpu.VMEM((3, 4, TILES, 16, 128), BF),
            pltpu.VMEM((3, TILES, 16, 128), BF),
            pltpu.VMEM((3, 14, 16, 128), BF),
            pltpu.VMEM((ROWS, 1024), BF),
            pltpu.VMEM((ROWS, 1024), BF),
            pltpu.VMEM((ROWS, 1024), BF),
            pltpu.VMEM((8, ROWS, 128), BF),
            pltpu.VMEM((KV, ROWS, 128), BF),
            pltpu.VMEM((KV, ROWS, 128), BF),
            pltpu.VMEM((MB, KV, ROWS, MROWS), BF),
            pltpu.VMEM((ROWS, 1024), BF),
            pltpu.VMEM((ROWS, 1024), F32),
            pltpu.VMEM((ROWS, 1024), BF),
            pltpu.VMEM((4, ROWS, 640), BF),
            pltpu.VMEM((4, ROWS, 640), BF),
            pltpu.VMEM((4, ROWS, 640), BF),
            pltpu.VMEM((8, ROWS, 640), BF),
            pltpu.VMEM((13, ROWS, 128), F32),
            pltpu.VMEM((13, ROWS, 128), BF),
            pltpu.VMEM((8, 256, 128), BF),
            pltpu.VMEM((ROWS, 1024), F32),
            dma((99,)), dma((99,)), dma((91,)), dma((91,)), dma,
            dma((120,)), dma((120,)), dma((8,)), dma((8,)),
        ],
        compiler_params=pltpu.CompilerParams(collective_id=0, has_side_effects=True, vmem_limit_bytes=VMEM_BYTES),
    )(block, tail, inputs, cotangent, *tables(segments, counts))


def shards(inputs, cotangent, flat_weights, counts, segments):
    d = lax.axis_index("fsdp")
    block, tail = to_block(flat_weights, d)
    block_out, input_grad, rows, prev = layer(block, tail, inputs, cotangent, segments, counts)
    return block_out, input_grad, from_block(rows, prev, d)


def solution(mesh):
    in_specs = (P("fsdp", None), P("fsdp", None), P("fsdp"), P("fsdp"), P("fsdp"))
    out_specs = (P("fsdp", None), P("fsdp", None), P("fsdp"))
    return jax.shard_map(shards, mesh=mesh, in_specs=in_specs, out_specs=out_specs, check_vma=False)
```

```python
import functools
import math

import jax
import jax.numpy as jnp
from jax import lax
from jax.experimental import pallas as pl
from jax.experimental.pallas import tpu as pltpu
from jax.sharding import PartitionSpec as P

D = 960
H = 15
KV = 5
HD = 64
FF = 2560
MB = 3
EPSILON = 1e-05
GAINS = 2 * D
BLOCK = 76800
N = 128
BF = jnp.bfloat16
F32 = jnp.float32
VMEM_BYTES = 63 * 1024 * 1024

MESH = pl.DeviceIdType.MESH
TILES = 40
PARTS = ((0, 7, 14), (14, 20, 27), (27, 33, 40))


def place():
    me = lax.axis_index("fsdp")
    return [me // 32, (me // 8) % 4, (me // 2) % 4], me % 2


def device_at(coords, core):
    return (coords[0] * 32 + coords[1] * 8 + coords[2] * 2 + core,)


def moved(coords, dim, by):
    out = list(coords)
    out[dim] = (out[dim] + by + 4) % 4
    return out


def beside(by):
    return (lax.axis_index("fsdp") + by) % N


def greet(coords, core):
    barrier = pltpu.get_barrier_semaphore()
    for dim in range(3):
        for by in (1, -1, 2):
            pl.semaphore_signal(barrier, inc=1, device_id=device_at(moved(coords, dim, by), core), device_id_type=MESH)
    pl.semaphore_signal(barrier, inc=1, device_id=device_at(coords, 1 - core), device_id_type=MESH)
    for by in (1, N - 1):
        pl.semaphore_signal(barrier, inc=1, device_id=(beside(by),), device_id_type=MESH)
    pl.semaphore_wait(barrier, 12)


def gather_into(w, blk, coords, core, send, recv, pair_send, pair_recv, own_sem):
    sent, ids, pair_ids, swapped = [], {}, {}, []
    sibling = device_at(coords, 1 - core)

    def at(fixed, tiles, which):
        index = [slice(None)] * 3
        for dim, value in fixed.items():
            index[dim] = value
        return w.at[(*index, which, rng(tiles))]

    def push(src, dst, device, ssem, rsem):
        copy = pltpu.make_async_remote_copy(src_ref=src, dst_ref=dst, send_sem=ssem, recv_sem=rsem, device_id=device, device_id_type=MESH)
        copy.start()
        sent.append(copy)

    def forward(key, src, dst, dim, step):
        k = ids.setdefault(key, len(ids))
        push(src, dst, device_at(moved(coords, dim, step), core), send.at[k], recv.at[k])

    def arrived(key, ref):
        landed(ref, recv.at[ids[key]])

    def swap(fixed, tiles):
        k = len(swapped)
        push(at(fixed, tiles, core), at(fixed, tiles, core), sibling, pair_send.at[k], pair_recv.at[k])
        swapped.append((fixed, tiles, k))

    def half(p, sign, number):
        lo, mid, hi = PARTS[p]
        return ((lo, mid), (mid, hi))[(number == 1) ^ (sign < 0)]

    def whole(p):
        return (PARTS[p][0], PARTS[p][2])

    def near(dim, step):
        return moved(coords, dim, step)[dim]

    local = pltpu.make_async_copy(blk, w.at[(*coords, core)], own_sem)
    local.start()
    parts = range(3)
    dims = [[(p + k) % 3 for k in range(3)] for p in parts]
    for p in parts:
        a, b, c = dims[p]
        for step in (2, 1, -1):
            forward((p, 0, step), blk.at[rng(whole(p))], at({a: coords[a], b: coords[b], c: coords[c]}, whole(p), core), a, step)
    push(blk, w.at[(*coords, core)], sibling, pair_send.at[90], pair_recv.at[90])
    local.wait()

    def line(p, step):
        a, b, c = dims[p]
        return {b: near(b, step), c: coords[c]}

    def sheet(p, group, step):
        a, b, c = dims[p]
        return {b: near(b, group), c: near(c, step)}

    def send_line(p, number):
        for sign in (1, -1):
            ref = at(line(p, 0), half(p, sign, number), core)
            forward((p, 1, sign, number), ref, ref, dims[p][1], sign)

    def send_sheet(p, group, number):
        for sign in (1, -1):
            ref = at(sheet(p, group, 0), half(p, sign, number), core)
            forward((p, 2, group, sign, number), ref, ref, dims[p][2], sign)

    def relay_line(p):
        for sign in (1, -1):
            ref = at(line(p, -sign), half(p, sign, 0), core)
            arrived((p, 1, sign, 0), ref)
            forward((p, 1, sign, 2), ref, ref, dims[p][1], sign)

    def relay_sheet(p, group):
        for sign in (1, -1):
            ref = at(sheet(p, group, -sign), half(p, sign, 0), core)
            arrived((p, 2, group, sign, 0), ref)
            forward((p, 2, group, sign, 2), ref, ref, dims[p][2], sign)

    def rest_sheet(p, group):
        for sign in (1, -1):
            arrived((p, 2, group, sign, 1), at(sheet(p, group, -sign), half(p, sign, 1), core))
            swap(sheet(p, group, -sign), whole(p))

    def last_sheet(p, group):
        for sign in (1, -1):
            arrived((p, 2, group, sign, 2), at(sheet(p, group, 2), half(p, sign, 2), core))
        swap(sheet(p, group, 2), whole(p))

    for p in parts:
        a, b, c = dims[p]
        for step in (1, -1, 2):
            fixed = {a: near(a, -step), b: coords[b], c: coords[c]}
            arrived((p, 0, step), at(fixed, whole(p), core))
            swap(fixed, whole(p))
        for number in (0, 1):
            send_line(p, number)
    for p in parts:
        for number in (0, 1):
            send_sheet(p, 0, number)
    for p in parts:
        relay_line(p)
    for p in parts:
        for sign in (1, -1):
            arrived((p, 1, sign, 1), at(line(p, -sign), half(p, sign, 1), core))
        for sign in (1, -1):
            for number in (0, 1):
                send_sheet(p, -sign, number)
    for p in parts:
        relay_sheet(p, 0)
    for p in parts:
        for sign in (1, -1):
            arrived((p, 1, sign, 2), at(line(p, 2), half(p, sign, 2), core))
        for number in (0, 1):
            send_sheet(p, 2, number)
        for step in (1, -1, 2):
            swap(line(p, step), whole(p))
    for p in parts:
        rest_sheet(p, 0)
    for group in (-1, 1, 2):
        for p in parts:
            relay_sheet(p, group)
        for p in parts:
            rest_sheet(p, group)
    for group in (0, -1, 1, 2):
        for p in parts:
            last_sheet(p, group)
    landed(w.at[(*coords, 1 - core)], pair_recv.at[90])
    for fixed, tiles, k in swapped:
        landed(at(fixed, tiles, 1 - core), pair_recv.at[k])
    return sent


def pack(rows_48, rows_80, rows_15, gains, d):
    qkv = jnp.pad(rows_48, ((0, 0), (0, 64))).reshape(3, 16, 13, 128).transpose(2, 0, 1, 3).reshape(39, 16, 128)
    qkv = jnp.concatenate([qkv, jnp.where(d == 0, gains, jnp.zeros_like(gains))[None]], axis=0)
    square = jnp.pad(rows_80, ((0, 0), (0, 64))).reshape(5, 16, 8, 128).transpose(2, 0, 1, 3).reshape(40, 16, 128)
    wide = jnp.pad(rows_15, ((0, 1), (0, 0))).reshape(16, 40, 128).transpose(1, 0, 2)
    return kind(d, qkv, square, wide)


def kind(d, qkv, square, wide):
    return jnp.where(d < 20, qkv, jnp.where((d >= 32) & (d < 96), wide, square))


def to_block(shard, d):
    none = jnp.zeros((GAINS,), BF)
    flat = lax.dynamic_slice(jnp.concatenate([shard, none]), (GAINS - 15 * d,), (BLOCK,))
    gains = jnp.pad(shard[:GAINS].reshape(2, D), ((0, 0), (0, 64))).reshape(16, 128)
    block = pack(flat.reshape(48, 1600), flat.reshape(80, D), flat.reshape(15, 2 * FF), gains, d)
    e = (d + N - 1) % N
    last = lax.dynamic_slice(jnp.concatenate([none, shard[:GAINS]]), (GAINS - 15 - 15 * e,), (GAINS,))
    qkv = jnp.stack([jnp.pad(last[:320], (1280, 64)).reshape(13, 128), jnp.pad(last[320:], (0, 64)).reshape(13, 128)], axis=1)
    qkv = jnp.pad(jnp.pad(qkv[:, None], ((0, 0), (2, 0), (0, 0), (0, 0))).reshape(39, 2, 128), ((0, 1), (0, 0), (0, 0)))
    square = jnp.pad(last.reshape(2, D), ((0, 0), (0, 64))).reshape(2, 8, 128).transpose(1, 0, 2)
    square = jnp.pad(square[:, None], ((0, 0), (4, 0), (0, 0), (0, 0))).reshape(40, 2, 128)
    wide = jnp.pad(last.reshape(15, 1, 128), ((25, 0), (0, 1), (0, 0)))
    return block, kind(e, qkv, square, wide).reshape(5, 16, 128)


def from_block(rows, prev, d):
    tiles = rows.reshape(40, 16, 128)
    qkv = tiles[:39].reshape(13, 3, 16, 128).transpose(1, 2, 0, 3).reshape(48, 1664)[:, :1600].reshape(-1)
    square = tiles.reshape(8, 5, 16, 128).transpose(1, 2, 0, 3).reshape(80, 1024)[:, :D].reshape(-1)
    wide = tiles.transpose(1, 0, 2)[:15].reshape(-1)
    flat = kind(d, qkv, square, wide)
    two = prev[:, 2:39:3].reshape(2, 1664)
    before = kind(
        d - 1,
        jnp.concatenate([two[0, 1280:1600], two[1, :1600]]),
        prev[:, 4::5].reshape(2, 1024)[:, :D].reshape(-1),
        prev[0, 25:].reshape(-1),
    )
    before = jnp.where(d == 0, tiles[39].reshape(2, 1024)[:, :D].reshape(-1), before)
    return lax.dynamic_slice(jnp.concatenate([before, flat]), (15 * d,), (BLOCK + 15,))


ROWS = 240
MROWS = 80


def tables(segment_ids, counts):
    seg = segment_ids.reshape(MB, MROWS)
    places = jnp.arange(MROWS, dtype=jnp.int32)
    same = seg[:, :, None] == seg[:, None, :]
    first_row = jnp.min(jnp.where(same, places[None, None, :], MROWS), axis=2)
    position = (places[None, :] - first_row).astype(F32).reshape(ROWS)
    freq = jnp.exp(jnp.arange(HD // 2, dtype=F32) * (-2.0 * math.log(10000.0) / HD))
    angle = position[:, None] * freq[None, :]
    cos, sin = jnp.cos(angle), jnp.sin(angle)
    cos_t = jnp.concatenate([cos, cos, cos, cos], axis=1)
    sin_t = jnp.concatenate([-sin, sin, -sin, sin], axis=1)
    allowed = same & (places[None, None, :] <= places[None, :, None])
    bias = jnp.where(allowed, 0.0, -1e30).astype(F32).reshape(ROWS, MROWS)
    live = (places[None, :] < counts[:, None]).astype(F32).reshape(ROWS, 1)
    return cos_t, sin_t, jnp.concatenate([bias, jnp.broadcast_to(live, (ROWS, 48))], axis=1)


def dot(a, b, ca=1, cb=0):
    return lax.dot_general(a, b, (((ca,), (cb,)), ((), ())), preferred_element_type=F32)


def mean_of(value):
    return jnp.sum(value, axis=-1, keepdims=True) * (1.0 / D)


class Flow:
    def __init__(self, name, dims, tiles, bufs, first_plane):
        self.name, self.dims, self.tiles, self.bufs, self.first_plane = name, dims, tiles, bufs, first_plane

    def half(self, sign, which):
        lo, mid, hi = self.tiles
        pair = ((lo, mid), (mid, hi))
        return pair[which] if sign > 0 else pair[1 - which]


class Reduce:
    def __init__(self, w, pair_buf, bufs, red, coords, core, send, recv, pair_send, pair_recv):
        self.w, self.pair_buf, self.red = w, pair_buf, red
        self.coords, self.core = coords, core
        self.send, self.recv, self.pair_send, self.pair_recv = send, recv, pair_send, pair_recv
        self.sent, self.ids = [], {}
        b1, b2, b3, q1, q2, z2 = bufs
        self.P0 = Flow("P0", (0, 1, 2), (0, 4, 8), (b1, b2, b3), 0)
        self.P1 = Flow("P1", (1, 2, 0), (8, 16, 24), (b1, b2, None), 0)
        self.P2 = Flow("P2", (2, 1, 0), (24, 32, 40), (b1, b2, None), 0)
        self.Q1 = Flow("Q1", (1, 2, 0), (0, 10, 20), (q1, q2, None), 0)
        self.Q2 = Flow("Q2", (2, 1, 0), (20, 30, 40), (q1, q2, None), 0)
        self.Z1 = Flow("Z1", (1, 2, 0), (8, 24, 40), (None, None, b3), 0)
        self.Z2 = Flow("Z2", (1, 2, 0), (0, 4, 8), (None, None, z2), 0)

    def copy(self, src, dst, device, ssem, rsem):
        return pltpu.make_async_remote_copy(
            src_ref=src, dst_ref=dst, send_sem=ssem, recv_sem=rsem, device_id=device, device_id_type=MESH
        )

    def offer(self, k, z, tiles=(0, TILES), xs=(0, 4)):
        x, t = rng(xs), rng(tiles)
        one = self.copy(
            self.w.at[z, x, :, 1 - self.core, t], self.pair_buf.at[z % 3, x, :, t],
            device_at(self.coords, 1 - self.core), self.pair_send.at[k], self.pair_recv.at[k],
        )
        one.start()
        self.sent.append((None, one))

    def ready(self, k, z, tiles=(0, TILES), xs=(0, 4)):
        slot, span = z % 3, rng(tiles)
        landed(self.pair_buf.at[slot, rng(xs), :, span], self.pair_recv.at[k])

        def body(t, _):
            at = (z, xs[0] + t // 4, t % 4, self.core, span)
            self.w[at] = self.w[at] + self.pair_buf[slot, xs[0] + t // 4, t % 4, span]
            return 0

        lax.fori_loop(0, 4 * (xs[1] - xs[0]), body, 0)

    def sem(self, flow, phase, planes, sign, number):
        return self.ids.setdefault((flow.name, phase, planes, sign, number), len(self.ids))

    def along(self, dim, step):
        return moved(self.coords, dim, step)[dim]

    def slot(self, flow, phase, planes, sign, number):
        which = 2 if number == 0 else (0 if sign > 0 else 1)
        inner = []
        for d in range(3):
            if d in flow.dims[phase + 1 :]:
                inner.append(pl.ds(planes[0], planes[1] - planes[0]) if d == 0 else slice(None))
        if flow.name in ("Q1", "Q2"):
            inner = inner[1:]
        tiles = flow.half(sign, 1 if number == 1 else 0)
        return flow.bufs[phase].at[(which, *inner, rng(tiles))]

    def ship(self, flow, phase, planes, sign, number):
        dim = flow.dims[phase]
        tiles = flow.half(sign, 1 if number == 1 else 0)
        fixed = []
        for d in range(3):
            if d in flow.dims[:phase]:
                fixed.append(self.coords[d])
            elif d == dim:
                fixed.append(self.along(d, 2 if number == 0 else sign))
            else:
                fixed.append(pl.ds(planes[0], planes[1] - planes[0]) if d == 0 else slice(None))
        slot = self.slot(flow, phase, planes, sign, number)
        if flow.name in ("Q1", "Q2"):
            fixed[0] = 0
        k = self.sem(flow, phase, planes, sign, number)
        return self.copy(
            self.w.at[(*fixed, self.core, rng(tiles))], slot,
            device_at(moved(self.coords, dim, sign), self.core), self.send.at[k], self.recv.at[k],
        )

    def go(self, flow, phase, planes, sign, number, guard=None):
        one = self.ship(flow, phase, planes, sign, number)
        if guard is None:
            one.start()
        else:
            pl.when(guard)(one.start)
        self.sent.append((guard, one))

    def loop(self, flow, phase, planes, coord, fn):
        dims = flow.dims
        free = [d for d in range(3) if d in dims[phase + 1 :]]
        sizes = [planes[1] - planes[0] if d == 0 else 4 for d in free]

        def body(t, _):
            inner = []
            if len(free) == 2:
                inner = [t // 4 + (planes[0] if free[0] == 0 else 0), t % 4]
            elif len(free) == 1:
                inner = [t + (planes[0] if free[0] == 0 else 0)]
            at = []
            for d in range(3):
                if d in free:
                    at.append(inner[free.index(d)])
                elif d == dims[phase]:
                    at.append(coord)
                else:
                    at.append(self.coords[d])
            if flow.name in ("Q1", "Q2"):
                at[0] = 0
                inner = inner[1:]
            fn((*at, self.core), tuple(inner))
            return 0

        count = math.prod(sizes)
        if count == 1:
            body(0, 0)
        else:
            lax.fori_loop(0, count, body, 0)

    def add_half(self, flow, phase, planes, sign):
        landed(self.slot(flow, phase, planes, sign, 0), self.recv.at[self.sem(flow, phase, planes, sign, 0)])
        tiles = rng(flow.half(sign, 0))
        buf = flow.bufs[phase]

        def fold(at, inner):
            self.w[(*at, tiles)] = self.w[(*at, tiles)] + buf[(2, *inner, tiles)]

        self.loop(flow, phase, planes, self.along(flow.dims[phase], sign), fold)

    def add_all(self, flow, phase, planes):
        for sign in (1, -1):
            for number in (1, 2):
                landed(self.slot(flow, phase, planes, sign, number), self.recv.at[self.sem(flow, phase, planes, sign, number)])
        tiles = rng((flow.tiles[0], flow.tiles[2]))
        buf = flow.bufs[phase]

        def total(at, inner):
            value = self.w[(*at, tiles)].astype(F32) + buf[(0, *inner, tiles)].astype(F32) + buf[(1, *inner, tiles)].astype(F32)
            if phase == 2:
                self.red[pl.ds(16 * flow.tiles[0], 16 * (flow.tiles[2] - flow.tiles[0])), :] = value.reshape(-1, 128)
            else:
                self.w[(*at, tiles)] = value.astype(BF)

        self.loop(flow, phase, planes, self.coords[flow.dims[phase]], total)

    def plane_in(self, planes, step):
        z = self.along(0, step)
        return (z >= planes[0]) & (z < planes[1])

    def open(self, planes, flows, along_z=False):
        for number in (0, 1):
            for sign in (1, -1):
                for flow in flows:
                    self.go(flow, 0, planes, sign, number)
                if along_z:
                    one = self.ship(self.P0, 0, (0, 4), sign, number)
                    pl.when(self.plane_in(planes, 2 if number == 0 else sign))(one.start)

    def relay(self, planes, flows, along_z=False):
        for sign in (1, -1):
            if along_z:

                @pl.when(self.plane_in(planes, sign))
                def _():
                    self.add_half(self.P0, 0, (0, 4), sign)
                    self.ship(self.P0, 0, (0, 4), sign, 2).start()

            for flow in flows:
                self.add_half(flow, 0, planes, sign)
                self.go(flow, 0, planes, sign, 2)

    def start(self, flow, phase, planes, guards=None):
        for number in (0, 1):
            for sign in (1, -1):
                self.go(flow, phase, planes, sign, number, guards and guards(sign, number))

    def pass_on(self, flow, phase, planes, guards=None):
        for sign in (1, -1):
            guard = guards and guards(sign, 2)
            if guard is None:
                self.add_half(flow, phase, planes, sign)
            else:
                pl.when(guard)(functools.partial(self.add_half, flow, phase, planes, sign))
            self.go(flow, phase, planes, sign, 2, guard)

    def whole(self, flow):
        return rng((flow.tiles[0], flow.tiles[2]))

    def direct(self, flow, phase, planes, step):
        dim = flow.dims[phase]
        fixed, inner = [], []
        for d in range(3):
            if d in flow.dims[:phase]:
                fixed.append(self.coords[d])
            elif d == dim:
                fixed.append(self.along(d, step))
            else:
                span = pl.ds(planes[0], planes[1] - planes[0]) if d == 0 else slice(None)
                fixed.append(span)
                inner.append(span)
        if flow.name in ("Q1", "Q2"):
            fixed[0] = 0
            inner = inner[1:]
        k = self.sem(flow, phase, planes, step, 3)
        return self.copy(
            self.w.at[(*fixed, self.core, self.whole(flow))], flow.bufs[phase].at[(step % 4 - 1, *inner, self.whole(flow))],
            device_at(moved(self.coords, dim, step), self.core), self.send.at[k], self.recv.at[k],
        )

    def start_direct(self, flow, phase, planes, guards=None):
        for step in (2, 1, -1):
            guard = guards and guards(step)
            one = self.direct(flow, phase, planes, step)
            if guard is None:
                one.start()
            else:
                pl.when(guard)(one.start)
            self.sent.append((guard, one))

    def add_direct(self, flow, phase, planes):
        for step in (1, -1, 2):
            self.direct(flow, phase, planes, step).wait_recv()
        tiles = self.whole(flow)
        buf = flow.bufs[phase]

        def total(at, inner):
            value = self.w[(*at, tiles)].astype(F32)
            for slot in range(3):
                value = value + buf[(slot, *inner, tiles)].astype(F32)
            if phase == 2:
                self.red[pl.ds(16 * flow.tiles[0], 16 * (flow.tiles[2] - flow.tiles[0])), :] = value.reshape(-1, 128)
            else:
                self.w[(*at, tiles)] = value.astype(BF)

        self.loop(flow, phase, planes, self.coords[flow.dims[phase]], total)

    def finish(self):
        late, early, every = (0, 1), (1, 4), (0, 4)
        z = self.coords[0]
        upper = lambda sign, number=0: z != 0
        to_zero = lambda step: self.along(0, step) == 0
        for number in (0, 1, 2):
            for sign in (1, -1):
                guard = self.plane_in((1, 4), 2 if number == 0 else sign)
                self.sent.append((guard, self.ship(self.P0, 0, every, sign, number)))
        for flow in (self.P1, self.P2):
            for planes in ((3, 4), (1, 3)):
                self.add_all(flow, 0, planes)
            self.start(flow, 1, early)
        self.relay(late, (self.Q1, self.Q2))
        pl.when(z != 0)(lambda: self.add_all(self.P0, 0, every))
        self.start(self.P0, 1, every, upper)
        for flow in (self.P1, self.P2):
            self.pass_on(flow, 1, early)
        for flow in (self.Q1, self.Q2):
            self.add_all(flow, 0, late)
            self.start_direct(flow, 1, late)
        self.pass_on(self.P0, 1, every, upper)
        for flow in (self.P1, self.P2):
            self.add_all(flow, 1, early)
        for flow in (self.Q1, self.Q2):
            self.add_direct(flow, 1, late)
        self.start_direct(self.Z1, 2, every)
        self.start_direct(self.Z2, 2, every, to_zero)
        pl.when(z != 0)(lambda: self.add_all(self.P0, 1, every))
        self.start_direct(self.P0, 2, every, upper)
        self.add_direct(self.Z1, 2, every)
        pl.when(z != 0)(lambda: self.add_direct(self.P0, 2, every))
        pl.when(z == 0)(lambda: self.add_direct(self.Z2, 2, every))

    def drain(self):
        for guard, one in self.sent:
            if guard is None:
                one.wait_send()
            else:
                pl.when(guard)(one.wait_send)


def rng(tiles):
    return pl.ds(tiles[0], tiles[1] - tiles[0])


def landed(dst, rsem):
    pltpu.make_async_copy(dst, dst, rsem).wait()


def layer_kernel(
    own_ref, tail_ref, x_ref, c_ref, cos_ref, sin_ref, bias_ref,
    out_ref, gin_ref, red_ref, prev_ref,
    blk, tail_in, tail_out, tail_back, tail_sem, w, pair_buf, b1, b2, b3, q1, q2, z2, xs, go, nrm, qs, kk, vv, prob, mixed, mid, n2p, gate, up, hid, ggu, gq, gqb, spread, acc,
    send, recv, pair_send, pair_recv, own_sem, rs_send, rs_recv, rp_send, rp_recv,
):
    coords, core = place()
    greet(coords, core)
    handed = pltpu.make_async_remote_copy(
        src_ref=tail_ref, dst_ref=tail_in, send_sem=tail_sem.at[0], recv_sem=tail_sem.at[1],
        device_id=(beside(N - 1),), device_id_type=MESH,
    )
    handed.start()
    r = lax.broadcasted_iota(jnp.int32, (640, 80), 0)
    c = lax.broadcasted_iota(jnp.int32, (640, 80), 1)
    last_rows = jnp.where((r // 16 == c // 2) & (r % 16 == 14 + c % 2), 1.0, 0.0).astype(BF)
    for k in range(8):
        r = lax.broadcasted_iota(jnp.int32, (256, 128), 0) + 128 * (k - 1)
        c = lax.broadcasted_iota(jnp.int32, (256, 128), 1) + 128 * k
        spread[k] = jnp.where((r == (c // 16) * 15 + c % 16) & (c % 16 != 15), 1.0, 0.0).astype(BF)

    xs[:, 896:1024] = jnp.zeros((ROWS, 128), BF)
    xs[:, 0:D] = x_ref[...]
    go[:, 896:1024] = jnp.zeros((ROWS, 128), BF)
    live = bias_ref[:, MROWS : MROWS + 1]
    go[:, 0:D] = (c_ref[...].astype(F32) * live).astype(BF)
    x = xs[...].astype(F32)
    inv1 = lax.rsqrt(mean_of(x * x) + EPSILON)
    mixed[:, 896:1024] = jnp.zeros((ROWS, 128), BF)
    gq[12] = jnp.zeros((ROWS, 128), F32)
    handed.wait()
    blk[...] = own_ref[...] + dot(last_rows, tail_in[...].reshape(80, 128)).astype(BF).reshape(TILES, 16, 128)
    sent = gather_into(w, blk, coords, core, send, recv, pair_send, pair_recv, own_sem)
    rs = Reduce(w, pair_buf, (b1, b2, b3, q1, q2, z2), red_ref, coords, core, rs_send, rs_recv, rp_send, rp_recv)

    def join(parts):
        return jnp.concatenate(parts, axis=0)

    def qkv_tiles(c):
        t = slice(3 * c, 3 * c + 3)
        return join([w[0, 0:2, :, :, t].reshape(768, 128), w[0, 2, 0:2, :, t].reshape(192, 128)])

    def put_qkv(c, v):
        t = slice(3 * c, 3 * c + 3)
        w[0, 0:2, :, :, t] = v[:768].reshape(2, 4, 2, 3, 16, 128)
        w[0, 2, 0:2, :, t] = v[768:].reshape(2, 2, 3, 16, 128)

    def out_tiles(c):
        t = slice(5 * c, 5 * c + 5)
        return join([w[0, 2, 2:4, :, t].reshape(320, 128), w[0, 3, :, :, t].reshape(640, 128)])

    def put_out(c, v):
        t = slice(5 * c, 5 * c + 5)
        w[0, 2, 2:4, :, t] = v[:320].reshape(2, 2, 5, 16, 128)
        w[0, 3, :, :, t] = v[320:].reshape(4, 2, 5, 16, 128)

    def in_tiles(c):
        return side([w[1:3, :, :, :, 5 * c + i].reshape(1024, 128) for i in range(5)])

    def down_tiles(c):
        return side([w[3, c, :, :, 5 * i : 5 * i + 5].reshape(640, 128) for i in range(8)])

    def side(parts):
        return jnp.concatenate(parts, axis=1)

    lane = lax.broadcasted_iota(jnp.int32, (MROWS, 128), 1)
    half = (lane < 64, lane >= 64)
    lane_all = lax.broadcasted_iota(jnp.int32, (ROWS, 128), 1)
    low_all = lane_all < 64
    first_all = lane_all % 64 < 32

    def swap(v):
        return jnp.where(first_all, pltpu.roll(v, 96, 1), pltpu.roll(v, 32, 1))

    def both(v, h):
        other = pltpu.roll(v, 64, 1)
        return jnp.where(low_all, v, other) if h == 0 else jnp.where(low_all, other, v)

    gains = w[0, 0, 0, 0, 39].astype(F32)
    gain1 = side([gains[i : i + 1] for i in range(8)])
    gain2 = side([gains[8 + i : 9 + i] for i in range(8)])
    nrm[...] = (xs[...].astype(F32) * inv1 * gain1).astype(BF)

    cos_t, sin_t = cos_ref[...], sin_ref[...]
    for c in range(0, 13, 2):
        group = [qkv_tiles(i) for i in range(c, min(c + 2, 13))]
        y2 = dot(nrm[:, 0:D], side(group))
        for i in range(len(group)):
            y = y2[:, 128 * i : 128 * i + 128]
            if c + i < 10:
                y = y * cos_t + swap(y) * sin_t
            if c + i < 8:
                qs[c + i] = y.astype(BF)
            for h in range(2):
                head = 2 * (c + i) + h
                if 15 <= head < 20:
                    kk[head - 15] = both(y, h).astype(BF)
                if 20 <= head < 25:
                    vv[head - 20] = both(y, h).astype(BF)

    zero_b = jnp.zeros((MROWS, 128), BF)

    def rows_of(m):
        return pl.ds(pl.multiple_of(m * MROWS, MROWS), MROWS)

    def chunk(head):
        return pl.ds(128 * (head // 2), 128)

    def attend(m, _):
        rows = rows_of(m)
        bias = bias_ref[rows, 0:MROWS]
        bias3 = jnp.concatenate([bias, bias, bias], axis=0)
        for g in range(KV):
            heads = [3 * g + i for i in range(3)]
            q = jnp.concatenate([jnp.where(half[h % 2], qs[h // 2, rows, :], zero_b) for h in heads], axis=0)
            s = dot(q, kk[g, rows, :], 1, 1) * 0.125 + bias3
            e = jnp.exp(s - jnp.max(s, axis=-1, keepdims=True))
            p = e / jnp.sum(e, axis=-1, keepdims=True)
            prob[m, g] = p.astype(BF)
            o = dot(p.astype(BF), vv[g, rows, :]).astype(BF)
            for i, h in enumerate(heads):
                mixed[rows, chunk(h)] = jnp.where(half[h % 2], o[MROWS * i : MROWS * i + MROWS], mixed[rows, chunk(h)])
        return 0

    lax.fori_loop(0, MB, attend, 0)

    for c in range(0, 8, 2):
        cols = slice(128 * c, 128 * c + 256)
        mid[:, cols] = xs[:, cols].astype(F32) + dot(mixed[:, 0:D], side([out_tiles(c), out_tiles(c + 1)]))
    middle = mid[...]
    inv2 = lax.rsqrt(mean_of(middle * middle) + EPSILON)
    n2b = (middle * inv2 * gain2).astype(BF)
    n2p[:, 0:128] = dot(n2b[:, 0:128], spread[0, 128:256]).astype(BF)
    for k in range(1, 8):
        n2p[:, 128 * k : 128 * k + 128] = dot(n2b[:, 128 * k - 128 : 128 * k + 128], spread[k]).astype(BF)


    def expand(c, _):
        g = dot(n2p[...], in_tiles(c))
        u = dot(n2p[...], in_tiles(c + 4))
        gate[c] = g.astype(BF)
        up[c] = u.astype(BF)
        hid[c] = (g * jax.nn.sigmoid(g) * u).astype(BF)
        return 0

    lax.fori_loop(0, 4, expand, 0)
    for copy in sent:
        copy.wait_send()
    acc[...] = mid[...]

    def reduce_(c, _):
        tiles = down_tiles(c)
        acc[...] += dot(hid[c], tiles)
        gh = dot(go[...], tiles, 1, 1)
        g, u = gate[c].astype(F32), up[c].astype(F32)
        sg = jax.nn.sigmoid(g)
        ggu[c] = (gh * u * sg * (1.0 + g * (1.0 - sg))).astype(BF)
        ggu[c + 4] = (gh * g * sg).astype(BF)
        for i in range(0, 8, 2):
            term = dot(hid[c], go[:, 128 * i : 128 * i + 256], 0, 0).astype(BF)
            for n in range(2):
                w[3, c, :, :, 5 * (i + n) : 5 * (i + n) + 5] = term[:, 128 * n : 128 * n + 128].reshape(4, 2, 5, 16, 128)
        return 0

    lax.fori_loop(0, 2, reduce_, 0)
    rs.offer(0, 3, xs=(0, 2))
    lax.fori_loop(2, 4, reduce_, 0)
    rs.offer(1, 3, xs=(2, 4))
    out_ref[...] = (acc[:, 0:D] * live).astype(BF)

    acc[...] = jnp.zeros((ROWS, 1024), F32)

    def back(c, _):
        gg = ggu[c]
        acc[...] += dot(gg, in_tiles(c), 1, 1)
        for i in range(0, 5, 2):
            term = dot(n2p[...], gg[:, 128 * i : min(128 * i + 256, 640)], 0, 0).astype(BF)
            for n in range(min(2, 5 - i)):
                w[1:3, :, :, :, 5 * c + i + n] = term[:, 128 * n : 128 * n + 128].reshape(2, 4, 4, 2, 16, 128)
        return 0

    lax.fori_loop(0, 2, back, 0)
    rs.ready(0, 3, xs=(0, 2))
    rs.ready(1, 3, xs=(2, 4))
    rs.open((3, 4), (rs.P1, rs.P2), True)
    lax.fori_loop(2, 5, back, 0)
    rs.offer(2, 1, (0, 25))
    rs.offer(3, 2, (0, 25))
    lax.fori_loop(5, 8, back, 0)
    rs.offer(4, 1, (25, 40))
    rs.offer(5, 2, (25, 40))
    rs.relay((3, 4), (rs.P1, rs.P2), True)
    rs.ready(2, 1, (0, 25))
    rs.ready(3, 2, (0, 25))
    rs.open((1, 3), (rs.P1,), True)
    gn = acc[...]
    hi = gn.astype(BF)
    lo = (gn - hi.astype(F32)).astype(BF)

    def close(k, part):
        cols = slice(128 * k, 128 * k + 128)
        return dot(hi[:, cols], spread[k, part], 1, 1) + dot(lo[:, cols], spread[k, part], 1, 1)

    before, same = slice(0, 128), slice(128, 256)
    gn = side([close(k, same) + close(k + 1, before) if k < 7 else close(k, same) for k in range(8)])
    n2 = mid[...] * inv2
    d_gain2 = jnp.sum(gn * n2, axis=0, keepdims=True)
    u = gn * gain2
    gm = go[...].astype(F32) + inv2 * (u - n2 * mean_of(u * n2))
    mid[...] = gm
    gmb = gm.astype(BF)
    gmix = jnp.zeros((ROWS, D), F32)
    for i in range(0, 8, 2):
        gmix = gmix + dot(gmb[:, 128 * i : 128 * i + 256], side([out_tiles(i), out_tiles(i + 1)]), 1, 1)
    term = dot(mixed[:, 0:D], gmb, 0, 0).astype(BF)
    for i in range(8):
        put_out(i, term[:, 128 * i : 128 * i + 128])
    rs.ready(4, 1, (25, 40))
    rs.ready(5, 2, (25, 40))
    rs.open((1, 3), (rs.P2,))
    mixed[:, 0:D] = gmix.astype(BF)

    def attend_back(m, _):
        rows = rows_of(m)
        for g in range(KV):
            heads = [3 * g + i for i in range(3)]
            q = jnp.concatenate([jnp.where(half[h % 2], qs[h // 2, rows, :], zero_b) for h in heads], axis=0)
            gmx = jnp.concatenate([jnp.where(half[h % 2], mixed[rows, chunk(h)], zero_b) for h in heads], axis=0)
            gv = dot(prob[m, g], gmx, 0, 0)
            p = prob[m, g].astype(F32)
            gp = dot(gmx, vv[g, rows, :], 1, 1)
            gs = (p * (gp - jnp.sum(p * gp, axis=-1, keepdims=True))).astype(BF)
            gqs = dot(gs, kk[g, rows, :]) * 0.125
            gk = dot(gs, q, 0, 0) * 0.125
            for i, h in enumerate(heads):
                gq[h // 2, rows, :] = jnp.where(half[h % 2], gqs[MROWS * i : MROWS * i + MROWS], gq[h // 2, rows, :])
            for head, value in ((15 + g, gk), (20 + g, gv)):
                value = value + pltpu.roll(value, 64, 1)
                gq[head // 2, rows, :] = jnp.where(half[head % 2], value, gq[head // 2, rows, :])
        return 0

    lax.fori_loop(0, 1, attend_back, 0)
    rs.relay((1, 3), (rs.P1,), True)
    lax.fori_loop(1, 2, attend_back, 0)
    rs.relay((1, 3), (rs.P2,))
    lax.fori_loop(2, MB, attend_back, 0)

    for c in range(13):
        y = gq[c]
        if c < 10:
            y = y * cos_t - swap(y) * sin_t
        gqb[c] = y.astype(BF)
    gn1 = jnp.zeros((ROWS, D), F32)
    for c in range(0, 13, 2):
        group = list(range(c, min(c + 2, 13)))
        gy = side([gqb[i] for i in group])
        gn1 = gn1 + dot(gy, side([qkv_tiles(i) for i in group]), 1, 1)
        term = dot(nrm[:, 0:D], gy, 0, 0).astype(BF)
        for n, i in enumerate(group):
            put_qkv(i, term[:, 128 * n : 128 * n + 128])
    acc[:, 896:1024] = jnp.zeros((ROWS, 128), F32)
    acc[:, 0:D] = gn1
    gn1 = acc[...]
    n1 = xs[...].astype(F32) * inv1
    d_gain1 = jnp.sum(gn1 * n1, axis=0, keepdims=True)
    both_gains = jnp.concatenate([v[:, 128 * i : 128 * i + 128] for v in (d_gain1, d_gain2) for i in range(8)], axis=0)
    w[0, 0, 0, 0, 39] = both_gains.astype(BF)
    rs.offer(6, 0, (0, 20))
    rs.offer(7, 0, (20, 40))
    u = gn1 * gain1
    res = mid[...] + inv1 * (u - n1 * mean_of(u * n1))
    gin_ref[...] = res[:, 0:D].astype(BF)
    rs.ready(6, 0, (0, 20))
    rs.open((0, 1), (rs.Q1,))
    rs.ready(7, 0, (20, 40))
    rs.open((0, 1), (rs.Q2,))
    rs.finish()
    for n in range(2):
        tail_out[n] = red_ref[pl.ds(14 + n, TILES, stride=16), :]
    handed = pltpu.make_async_remote_copy(
        src_ref=tail_out, dst_ref=tail_back, send_sem=tail_sem.at[2], recv_sem=tail_sem.at[3],
        device_id=(beside(1),), device_id_type=MESH,
    )
    handed.start()
    rs.drain()
    handed.wait()
    prev_ref[...] = tail_back[...]


def layer(block, tail, inputs, cotangent, segments, counts):
    vm = pl.BlockSpec(memory_space=pltpu.VMEM)
    dma = pltpu.SemaphoreType.DMA
    return pl.pallas_call(
        layer_kernel,
        out_shape=(
            jax.ShapeDtypeStruct((ROWS, D), BF),
            jax.ShapeDtypeStruct((ROWS, D), BF),
            jax.ShapeDtypeStruct((TILES * 16, 128), F32),
            jax.ShapeDtypeStruct((2, TILES, 128), F32),
        ),
        in_specs=[vm] * 7,
        out_specs=(vm, vm, vm, vm),
        scratch_shapes=[
            pltpu.VMEM((TILES, 16, 128), BF),
            pltpu.VMEM((5, 16, 128), BF),
            pltpu.VMEM((2, TILES, 128), F32),
            pltpu.VMEM((2, TILES, 128), F32),
            dma((4,)),
            pltpu.VMEM((4, 4, 4, 2, TILES, 16, 128), BF),
            pltpu.VMEM((3, 4, 4, TILES, 16, 128), BF),
            pltpu.VMEM((3, 4, 4, TILES, 16, 128), BF),
            pltpu.VMEM((3, 4, TILES, 16, 128), BF),
            pltpu.VMEM((3, TILES, 16, 128), BF),
            pltpu.VMEM((3, 4, TILES, 16, 128), BF),
            pltpu.VMEM((3, TILES, 16, 128), BF),
            pltpu.VMEM((3, 14, 16, 128), BF),
            pltpu.VMEM((ROWS, 1024), BF),
            pltpu.VMEM((ROWS, 1024), BF),
            pltpu.VMEM((ROWS, 1024), BF),
            pltpu.VMEM((8, ROWS, 128), BF),
            pltpu.VMEM((KV, ROWS, 128), BF),
            pltpu.VMEM((KV, ROWS, 128), BF),
            pltpu.VMEM((MB, KV, ROWS, MROWS), BF),
            pltpu.VMEM((ROWS, 1024), BF),
            pltpu.VMEM((ROWS, 1024), F32),
            pltpu.VMEM((ROWS, 1024), BF),
            pltpu.VMEM((4, ROWS, 640), BF),
            pltpu.VMEM((4, ROWS, 640), BF),
            pltpu.VMEM((4, ROWS, 640), BF),
            pltpu.VMEM((8, ROWS, 640), BF),
            pltpu.VMEM((13, ROWS, 128), F32),
            pltpu.VMEM((13, ROWS, 128), BF),
            pltpu.VMEM((8, 256, 128), BF),
            pltpu.VMEM((ROWS, 1024), F32),
            dma((99,)), dma((99,)), dma((91,)), dma((91,)), dma,
            dma((120,)), dma((120,)), dma((8,)), dma((8,)),
        ],
        compiler_params=pltpu.CompilerParams(collective_id=0, has_side_effects=True, vmem_limit_bytes=VMEM_BYTES),
    )(block, tail, inputs, cotangent, *tables(segments, counts))


def shards(inputs, cotangent, flat_weights, counts, segments):
    d = lax.axis_index("fsdp")
    block, tail = to_block(flat_weights, d)
    block_out, input_grad, rows, prev = layer(block, tail, inputs, cotangent, segments, counts)
    return block_out, input_grad, from_block(rows, prev, d)


def solution(mesh):
    in_specs = (P("fsdp", None), P("fsdp", None), P("fsdp"), P("fsdp"), P("fsdp"))
    out_specs = (P("fsdp", None), P("fsdp", None), P("fsdp"))
    return jax.shard_map(shards, mesh=mesh, in_specs=in_specs, out_specs=out_specs, check_vma=False)
```

```python
import functools
import math

import jax
import jax.numpy as jnp
from jax import lax
from jax.experimental import pallas as pl
from jax.experimental.pallas import tpu as pltpu
from jax.sharding import PartitionSpec as P

D = 960
H = 15
KV = 5
HD = 64
FF = 2560
MB = 3
EPSILON = 1e-05
GAINS = 2 * D
BLOCK = 76800
N = 128
BF = jnp.bfloat16
F32 = jnp.float32
VMEM_BYTES = 63 * 1024 * 1024

MESH = pl.DeviceIdType.MESH
TILES = 40
PARTS = ((0, 7, 14), (14, 20, 27), (27, 33, 40))


def place():
    me = lax.axis_index("fsdp")
    return [me // 32, (me // 8) % 4, (me // 2) % 4], me % 2


def device_at(coords, core):
    return (coords[0] * 32 + coords[1] * 8 + coords[2] * 2 + core,)


def moved(coords, dim, by):
    out = list(coords)
    out[dim] = (out[dim] + by + 4) % 4
    return out


def beside(by):
    return (lax.axis_index("fsdp") + by) % N


def greet(coords, core):
    barrier = pltpu.get_barrier_semaphore()
    for dim in range(3):
        for by in (1, -1, 2):
            pl.semaphore_signal(barrier, inc=1, device_id=device_at(moved(coords, dim, by), core), device_id_type=MESH)
    pl.semaphore_signal(barrier, inc=1, device_id=device_at(coords, 1 - core), device_id_type=MESH)
    for by in (1, N - 1):
        pl.semaphore_signal(barrier, inc=1, device_id=(beside(by),), device_id_type=MESH)
    pl.semaphore_wait(barrier, 12)


def gather_into(w, blk, coords, core, send, recv, pair_send, pair_recv, own_sem):
    sent, ids, pair_ids, swapped = [], {}, {}, []
    sibling = device_at(coords, 1 - core)

    def at(fixed, tiles, which):
        index = [slice(None)] * 3
        for dim, value in fixed.items():
            index[dim] = value
        return w.at[(*index, which, rng(tiles))]

    def push(src, dst, device, ssem, rsem):
        copy = pltpu.make_async_remote_copy(src_ref=src, dst_ref=dst, send_sem=ssem, recv_sem=rsem, device_id=device, device_id_type=MESH)
        copy.start()
        sent.append(copy)

    def forward(key, src, dst, dim, step):
        k = ids.setdefault(key, len(ids))
        push(src, dst, device_at(moved(coords, dim, step), core), send.at[k], recv.at[k])

    def arrived(key, ref):
        landed(ref, recv.at[ids[key]])

    def swap(fixed, tiles):
        k = len(swapped)
        push(at(fixed, tiles, core), at(fixed, tiles, core), sibling, pair_send.at[k], pair_recv.at[k])
        swapped.append((fixed, tiles, k))

    def half(p, sign, number):
        lo, mid, hi = PARTS[p]
        return ((lo, mid), (mid, hi))[(number == 1) ^ (sign < 0)]

    def whole(p):
        return (PARTS[p][0], PARTS[p][2])

    def near(dim, step):
        return moved(coords, dim, step)[dim]

    local = pltpu.make_async_copy(blk, w.at[(*coords, core)], own_sem)
    local.start()
    parts = range(3)
    dims = [[(p + k) % 3 for k in range(3)] for p in parts]
    for p in parts:
        a, b, c = dims[p]
        for step in (2, 1, -1):
            forward((p, 0, step), blk.at[rng(whole(p))], at({a: coords[a], b: coords[b], c: coords[c]}, whole(p), core), a, step)
    push(blk, w.at[(*coords, core)], sibling, pair_send.at[90], pair_recv.at[90])
    local.wait()

    def line(p, step):
        a, b, c = dims[p]
        return {b: near(b, step), c: coords[c]}

    def sheet(p, group, step):
        a, b, c = dims[p]
        return {b: near(b, group), c: near(c, step)}

    def send_line(p, number):
        for sign in (1, -1):
            ref = at(line(p, 0), half(p, sign, number), core)
            forward((p, 1, sign, number), ref, ref, dims[p][1], sign)

    def send_sheet(p, group, number):
        for sign in (1, -1):
            ref = at(sheet(p, group, 0), half(p, sign, number), core)
            forward((p, 2, group, sign, number), ref, ref, dims[p][2], sign)

    def relay_line(p):
        for sign in (1, -1):
            ref = at(line(p, -sign), half(p, sign, 0), core)
            arrived((p, 1, sign, 0), ref)
            forward((p, 1, sign, 2), ref, ref, dims[p][1], sign)

    def relay_sheet(p, group):
        for sign in (1, -1):
            ref = at(sheet(p, group, -sign), half(p, sign, 0), core)
            arrived((p, 2, group, sign, 0), ref)
            forward((p, 2, group, sign, 2), ref, ref, dims[p][2], sign)

    def rest_sheet(p, group):
        for sign in (1, -1):
            arrived((p, 2, group, sign, 1), at(sheet(p, group, -sign), half(p, sign, 1), core))
            swap(sheet(p, group, -sign), whole(p))

    def last_sheet(p, group):
        for sign in (1, -1):
            arrived((p, 2, group, sign, 2), at(sheet(p, group, 2), half(p, sign, 2), core))
        swap(sheet(p, group, 2), whole(p))

    for p in parts:
        a, b, c = dims[p]
        for step in (1, -1, 2):
            fixed = {a: near(a, -step), b: coords[b], c: coords[c]}
            arrived((p, 0, step), at(fixed, whole(p), core))
            swap(fixed, whole(p))
        for number in (0, 1):
            send_line(p, number)
    for p in parts:
        for number in (0, 1):
            send_sheet(p, 0, number)
    for p in parts:
        relay_line(p)
    for p in parts:
        for sign in (1, -1):
            arrived((p, 1, sign, 1), at(line(p, -sign), half(p, sign, 1), core))
        for sign in (1, -1):
            for number in (0, 1):
                send_sheet(p, -sign, number)
    for p in parts:
        relay_sheet(p, 0)
    for p in parts:
        for sign in (1, -1):
            arrived((p, 1, sign, 2), at(line(p, 2), half(p, sign, 2), core))
        for number in (0, 1):
            send_sheet(p, 2, number)
        for step in (1, -1, 2):
            swap(line(p, step), whole(p))
    for p in parts:
        rest_sheet(p, 0)
    for group in (-1, 1, 2):
        for p in parts:
            relay_sheet(p, group)
        for p in parts:
            rest_sheet(p, group)
    for group in (0, -1, 1, 2):
        for p in parts:
            last_sheet(p, group)
    landed(w.at[(*coords, 1 - core)], pair_recv.at[90])
    for fixed, tiles, k in swapped:
        landed(at(fixed, tiles, 1 - core), pair_recv.at[k])
    return sent


def pack(rows_48, rows_80, rows_15, gains, d):
    qkv = jnp.pad(rows_48, ((0, 0), (0, 64))).reshape(3, 16, 13, 128).transpose(2, 0, 1, 3).reshape(39, 16, 128)
    qkv = jnp.concatenate([qkv, jnp.where(d == 0, gains, jnp.zeros_like(gains))[None]], axis=0)
    square = jnp.pad(rows_80, ((0, 0), (0, 64))).reshape(5, 16, 8, 128).transpose(2, 0, 1, 3).reshape(40, 16, 128)
    wide = jnp.pad(rows_15, ((0, 1), (0, 0))).reshape(16, 40, 128).transpose(1, 0, 2)
    return kind(d, qkv, square, wide)


def kind(d, qkv, square, wide):
    return jnp.where(d < 20, qkv, jnp.where((d >= 32) & (d < 96), wide, square))


def to_block(shard, d):
    none = jnp.zeros((GAINS,), BF)
    flat = lax.dynamic_slice(jnp.concatenate([shard, none]), (GAINS - 15 * d,), (BLOCK,))
    gains = jnp.pad(shard[:GAINS].reshape(2, D), ((0, 0), (0, 64))).reshape(16, 128)
    block = pack(flat.reshape(48, 1600), flat.reshape(80, D), flat.reshape(15, 2 * FF), gains, d)
    e = (d + N - 1) % N
    last = lax.dynamic_slice(jnp.concatenate([none, shard[:GAINS]]), (GAINS - 15 - 15 * e,), (GAINS,))
    qkv = jnp.stack([jnp.pad(last[:320], (1280, 64)).reshape(13, 128), jnp.pad(last[320:], (0, 64)).reshape(13, 128)], axis=1)
    qkv = jnp.pad(jnp.pad(qkv[:, None], ((0, 0), (2, 0), (0, 0), (0, 0))).reshape(39, 2, 128), ((0, 1), (0, 0), (0, 0)))
    square = jnp.pad(last.reshape(2, D), ((0, 0), (0, 64))).reshape(2, 8, 128).transpose(1, 0, 2)
    square = jnp.pad(square[:, None], ((0, 0), (4, 0), (0, 0), (0, 0))).reshape(40, 2, 128)
    wide = jnp.pad(last.reshape(15, 1, 128), ((25, 0), (0, 1), (0, 0)))
    return block, kind(e, qkv, square, wide).reshape(5, 16, 128)


def from_block(rows, prev, d):
    tiles = rows.reshape(40, 16, 128)
    qkv = tiles[:39].reshape(13, 3, 16, 128).transpose(1, 2, 0, 3).reshape(48, 1664)[:, :1600].reshape(-1)
    square = tiles.reshape(8, 5, 16, 128).transpose(1, 2, 0, 3).reshape(80, 1024)[:, :D].reshape(-1)
    wide = tiles.transpose(1, 0, 2)[:15].reshape(-1)
    flat = kind(d, qkv, square, wide)
    two = prev[:, 2:39:3].reshape(2, 1664)
    before = kind(
        d - 1,
        jnp.concatenate([two[0, 1280:1600], two[1, :1600]]),
        prev[:, 4::5].reshape(2, 1024)[:, :D].reshape(-1),
        prev[0, 25:].reshape(-1),
    )
    before = jnp.where(d == 0, tiles[39].reshape(2, 1024)[:, :D].reshape(-1), before)
    return lax.dynamic_slice(jnp.concatenate([before, flat]), (15 * d,), (BLOCK + 15,))


ROWS = 240
MROWS = 80


def tables(segment_ids, counts):
    seg = segment_ids.reshape(MB, MROWS)
    places = jnp.arange(MROWS, dtype=jnp.int32)
    same = seg[:, :, None] == seg[:, None, :]
    first_row = jnp.min(jnp.where(same, places[None, None, :], MROWS), axis=2)
    position = (places[None, :] - first_row).astype(F32).reshape(ROWS)
    freq = jnp.exp(jnp.arange(HD // 2, dtype=F32) * (-2.0 * math.log(10000.0) / HD))
    angle = position[:, None] * freq[None, :]
    cos, sin = jnp.cos(angle), jnp.sin(angle)
    cos_t = jnp.concatenate([cos, cos, cos, cos], axis=1)
    sin_t = jnp.concatenate([-sin, sin, -sin, sin], axis=1)
    allowed = same & (places[None, None, :] <= places[None, :, None])
    bias = jnp.where(allowed, 0.0, -1e30).astype(F32).reshape(ROWS, MROWS)
    live = (places[None, :] < counts[:, None]).astype(F32).reshape(ROWS, 1)
    return cos_t, sin_t, jnp.concatenate([bias, jnp.broadcast_to(live, (ROWS, 48))], axis=1)


def dot(a, b, ca=1, cb=0):
    return lax.dot_general(a, b, (((ca,), (cb,)), ((), ())), preferred_element_type=F32)


def mean_of(value):
    return jnp.sum(value, axis=-1, keepdims=True) * (1.0 / D)


class Flow:
    def __init__(self, name, dims, tiles, bufs, first_plane):
        self.name, self.dims, self.tiles, self.bufs, self.first_plane = name, dims, tiles, bufs, first_plane

    def half(self, sign, which):
        lo, mid, hi = self.tiles
        pair = ((lo, mid), (mid, hi))
        return pair[which] if sign > 0 else pair[1 - which]


class Reduce:
    def __init__(self, w, pair_buf, bufs, red, coords, core, send, recv, pair_send, pair_recv):
        self.w, self.pair_buf, self.red = w, pair_buf, red
        self.coords, self.core = coords, core
        self.send, self.recv, self.pair_send, self.pair_recv = send, recv, pair_send, pair_recv
        self.sent, self.ids = [], {}
        b1, b2, b3, q1, q2, z2 = bufs
        self.P0 = Flow("P0", (0, 1, 2), (0, 4, 8), (b1, b2, b3), 0)
        self.P1 = Flow("P1", (1, 2, 0), (8, 16, 24), (b1, b2, None), 0)
        self.P2 = Flow("P2", (2, 1, 0), (24, 32, 40), (b1, b2, None), 0)
        self.Q1 = Flow("Q1", (1, 2, 0), (0, 10, 20), (q1, q2, None), 0)
        self.Q2 = Flow("Q2", (2, 1, 0), (20, 30, 40), (q1, q2, None), 0)
        self.Z1 = Flow("Z1", (1, 2, 0), (8, 24, 40), (None, None, b3), 0)
        self.Z2 = Flow("Z2", (1, 2, 0), (0, 4, 8), (None, None, z2), 0)

    def copy(self, src, dst, device, ssem, rsem):
        return pltpu.make_async_remote_copy(
            src_ref=src, dst_ref=dst, send_sem=ssem, recv_sem=rsem, device_id=device, device_id_type=MESH
        )

    def offer(self, k, z, tiles=(0, TILES), xs=(0, 4)):
        x, t = rng(xs), rng(tiles)
        one = self.copy(
            self.w.at[z, x, :, 1 - self.core, t], self.pair_buf.at[z % 3, x, :, t],
            device_at(self.coords, 1 - self.core), self.pair_send.at[k], self.pair_recv.at[k],
        )
        one.start()
        self.sent.append((None, one))

    def ready(self, k, z, tiles=(0, TILES), xs=(0, 4)):
        slot, span = z % 3, rng(tiles)
        landed(self.pair_buf.at[slot, rng(xs), :, span], self.pair_recv.at[k])

        def body(t, _):
            at = (z, xs[0] + t // 4, t % 4, self.core, span)
            self.w[at] = self.w[at] + self.pair_buf[slot, xs[0] + t // 4, t % 4, span]
            return 0

        lax.fori_loop(0, 4 * (xs[1] - xs[0]), body, 0)

    def sem(self, flow, phase, planes, sign, number):
        return self.ids.setdefault((flow.name, phase, planes, sign, number), len(self.ids))

    def along(self, dim, step):
        return moved(self.coords, dim, step)[dim]

    def slot(self, flow, phase, planes, sign, number):
        which = 2 if number == 0 else (0 if sign > 0 else 1)
        inner = []
        for d in range(3):
            if d in flow.dims[phase + 1 :]:
                inner.append(pl.ds(planes[0], planes[1] - planes[0]) if d == 0 else slice(None))
        if flow.name in ("Q1", "Q2"):
            inner = inner[1:]
        tiles = flow.half(sign, 1 if number == 1 else 0)
        return flow.bufs[phase].at[(which, *inner, rng(tiles))]

    def ship(self, flow, phase, planes, sign, number):
        dim = flow.dims[phase]
        tiles = flow.half(sign, 1 if number == 1 else 0)
        fixed = []
        for d in range(3):
            if d in flow.dims[:phase]:
                fixed.append(self.coords[d])
            elif d == dim:
                fixed.append(self.along(d, 2 if number == 0 else sign))
            else:
                fixed.append(pl.ds(planes[0], planes[1] - planes[0]) if d == 0 else slice(None))
        slot = self.slot(flow, phase, planes, sign, number)
        if flow.name in ("Q1", "Q2"):
            fixed[0] = 0
        k = self.sem(flow, phase, planes, sign, number)
        return self.copy(
            self.w.at[(*fixed, self.core, rng(tiles))], slot,
            device_at(moved(self.coords, dim, sign), self.core), self.send.at[k], self.recv.at[k],
        )

    def go(self, flow, phase, planes, sign, number, guard=None):
        one = self.ship(flow, phase, planes, sign, number)
        if guard is None:
            one.start()
        else:
            pl.when(guard)(one.start)
        self.sent.append((guard, one))

    def loop(self, flow, phase, planes, coord, fn):
        dims = flow.dims
        free = [d for d in range(3) if d in dims[phase + 1 :]]
        sizes = [planes[1] - planes[0] if d == 0 else 4 for d in free]

        def body(t, _):
            inner = []
            if len(free) == 2:
                inner = [t // 4 + (planes[0] if free[0] == 0 else 0), t % 4]
            elif len(free) == 1:
                inner = [t + (planes[0] if free[0] == 0 else 0)]
            at = []
            for d in range(3):
                if d in free:
                    at.append(inner[free.index(d)])
                elif d == dims[phase]:
                    at.append(coord)
                else:
                    at.append(self.coords[d])
            if flow.name in ("Q1", "Q2"):
                at[0] = 0
                inner = inner[1:]
            fn((*at, self.core), tuple(inner))
            return 0

        count = math.prod(sizes)
        if count == 1:
            body(0, 0)
        else:
            lax.fori_loop(0, count, body, 0)

    def add_half(self, flow, phase, planes, sign):
        landed(self.slot(flow, phase, planes, sign, 0), self.recv.at[self.sem(flow, phase, planes, sign, 0)])
        tiles = rng(flow.half(sign, 0))
        buf = flow.bufs[phase]

        def fold(at, inner):
            self.w[(*at, tiles)] = self.w[(*at, tiles)] + buf[(2, *inner, tiles)]

        self.loop(flow, phase, planes, self.along(flow.dims[phase], sign), fold)

    def add_all(self, flow, phase, planes):
        for sign in (1, -1):
            for number in (1, 2):
                landed(self.slot(flow, phase, planes, sign, number), self.recv.at[self.sem(flow, phase, planes, sign, number)])
        tiles = rng((flow.tiles[0], flow.tiles[2]))
        buf = flow.bufs[phase]

        def total(at, inner):
            value = self.w[(*at, tiles)].astype(F32) + buf[(0, *inner, tiles)].astype(F32) + buf[(1, *inner, tiles)].astype(F32)
            if phase == 2:
                self.red[pl.ds(16 * flow.tiles[0], 16 * (flow.tiles[2] - flow.tiles[0])), :] = value.reshape(-1, 128)
            else:
                self.w[(*at, tiles)] = value.astype(BF)

        self.loop(flow, phase, planes, self.coords[flow.dims[phase]], total)

    def plane_in(self, planes, step):
        z = self.along(0, step)
        return (z >= planes[0]) & (z < planes[1])

    def open(self, planes, flows, along_z=False):
        for number in (0, 1):
            for sign in (1, -1):
                for flow in flows:
                    self.go(flow, 0, planes, sign, number)
                if along_z:
                    one = self.ship(self.P0, 0, (0, 4), sign, number)
                    pl.when(self.plane_in(planes, 2 if number == 0 else sign))(one.start)

    def relay(self, planes, flows, along_z=False):
        for sign in (1, -1):
            if along_z:

                @pl.when(self.plane_in(planes, sign))
                def _():
                    self.add_half(self.P0, 0, (0, 4), sign)
                    self.ship(self.P0, 0, (0, 4), sign, 2).start()

            for flow in flows:
                self.add_half(flow, 0, planes, sign)
                self.go(flow, 0, planes, sign, 2)

    def start(self, flow, phase, planes, guards=None):
        for number in (0, 1):
            for sign in (1, -1):
                self.go(flow, phase, planes, sign, number, guards and guards(sign, number))

    def pass_on(self, flow, phase, planes, guards=None):
        for sign in (1, -1):
            guard = guards and guards(sign, 2)
            if guard is None:
                self.add_half(flow, phase, planes, sign)
            else:
                pl.when(guard)(functools.partial(self.add_half, flow, phase, planes, sign))
            self.go(flow, phase, planes, sign, 2, guard)

    def whole(self, flow):
        return rng((flow.tiles[0], flow.tiles[2]))

    def direct(self, flow, phase, planes, step):
        dim = flow.dims[phase]
        fixed, inner = [], []
        for d in range(3):
            if d in flow.dims[:phase]:
                fixed.append(self.coords[d])
            elif d == dim:
                fixed.append(self.along(d, step))
            else:
                span = pl.ds(planes[0], planes[1] - planes[0]) if d == 0 else slice(None)
                fixed.append(span)
                inner.append(span)
        if flow.name in ("Q1", "Q2"):
            fixed[0] = 0
            inner = inner[1:]
        k = self.sem(flow, phase, planes, step, 3)
        return self.copy(
            self.w.at[(*fixed, self.core, self.whole(flow))], flow.bufs[phase].at[(step % 4 - 1, *inner, self.whole(flow))],
            device_at(moved(self.coords, dim, step), self.core), self.send.at[k], self.recv.at[k],
        )

    def start_direct(self, flow, phase, planes, guards=None):
        for step in (2, 1, -1):
            guard = guards and guards(step)
            one = self.direct(flow, phase, planes, step)
            if guard is None:
                one.start()
            else:
                pl.when(guard)(one.start)
            self.sent.append((guard, one))

    def add_direct(self, flow, phase, planes):
        for step in (1, -1, 2):
            self.direct(flow, phase, planes, step).wait_recv()
        tiles = self.whole(flow)
        buf = flow.bufs[phase]

        def total(at, inner):
            value = self.w[(*at, tiles)].astype(F32)
            for slot in range(3):
                value = value + buf[(slot, *inner, tiles)].astype(F32)
            if phase == 2:
                self.red[pl.ds(16 * flow.tiles[0], 16 * (flow.tiles[2] - flow.tiles[0])), :] = value.reshape(-1, 128)
            else:
                self.w[(*at, tiles)] = value.astype(BF)

        self.loop(flow, phase, planes, self.coords[flow.dims[phase]], total)

    def finish(self):
        late, early, every = (0, 1), (1, 4), (0, 4)
        z = self.coords[0]
        upper = lambda sign, number=0: z != 0
        to_zero = lambda step: self.along(0, step) == 0
        for number in (0, 1, 2):
            for sign in (1, -1):
                guard = self.plane_in((1, 4), 2 if number == 0 else sign)
                self.sent.append((guard, self.ship(self.P0, 0, every, sign, number)))
        for flow in (self.P1, self.P2):
            for planes in ((3, 4), (1, 3)):
                self.add_all(flow, 0, planes)
            self.start(flow, 1, early)
        self.relay(late, (self.Q1, self.Q2))
        pl.when(z != 0)(lambda: self.add_all(self.P0, 0, every))
        self.start(self.P0, 1, every, upper)
        for flow in (self.P1, self.P2):
            self.pass_on(flow, 1, early)
        for flow in (self.Q1, self.Q2):
            self.add_all(flow, 0, late)
            self.start_direct(flow, 1, late)
        self.pass_on(self.P0, 1, every, upper)
        for flow in (self.P1, self.P2):
            self.add_all(flow, 1, early)
        for flow in (self.Q1, self.Q2):
            self.add_direct(flow, 1, late)
        self.start_direct(self.Z1, 2, every)
        self.start_direct(self.Z2, 2, every, to_zero)
        pl.when(z != 0)(lambda: self.add_all(self.P0, 1, every))
        self.start_direct(self.P0, 2, every, upper)
        self.add_direct(self.Z1, 2, every)
        pl.when(z != 0)(lambda: self.add_direct(self.P0, 2, every))
        pl.when(z == 0)(lambda: self.add_direct(self.Z2, 2, every))

    def drain(self):
        for guard, one in self.sent:
            if guard is None:
                one.wait_send()
            else:
                pl.when(guard)(one.wait_send)


def rng(tiles):
    return pl.ds(tiles[0], tiles[1] - tiles[0])


def landed(dst, rsem):
    pltpu.make_async_copy(dst, dst, rsem).wait()


def layer_kernel(
    own_ref, tail_ref, x_ref, c_ref, cos_ref, sin_ref, bias_ref,
    out_ref, gin_ref, red_ref, prev_ref,
    blk, tail_in, tail_out, tail_back, tail_sem, w, pair_buf, b1, b2, b3, q1, q2, z2, xs, go, nrm, qs, kk, vv, prob, mixed, mid, n2p, gate, up, hid, ggu, gq, gqb, spread, acc,
    send, recv, pair_send, pair_recv, own_sem, rs_send, rs_recv, rp_send, rp_recv,
):
    coords, core = place()
    greet(coords, core)
    handed = pltpu.make_async_remote_copy(
        src_ref=tail_ref, dst_ref=tail_in, send_sem=tail_sem.at[0], recv_sem=tail_sem.at[1],
        device_id=(beside(N - 1),), device_id_type=MESH,
    )
    handed.start()
    r = lax.broadcasted_iota(jnp.int32, (640, 80), 0)
    c = lax.broadcasted_iota(jnp.int32, (640, 80), 1)
    last_rows = jnp.where((r // 16 == c // 2) & (r % 16 == 14 + c % 2), 1.0, 0.0).astype(BF)
    for k in range(8):
        r = lax.broadcasted_iota(jnp.int32, (256, 128), 0) + 128 * (k - 1)
        c = lax.broadcasted_iota(jnp.int32, (256, 128), 1) + 128 * k
        spread[k] = jnp.where((r == (c // 16) * 15 + c % 16) & (c % 16 != 15), 1.0, 0.0).astype(BF)

    xs[:, 896:1024] = jnp.zeros((ROWS, 128), BF)
    xs[:, 0:D] = x_ref[...]
    go[:, 896:1024] = jnp.zeros((ROWS, 128), BF)
    live = bias_ref[:, MROWS : MROWS + 1]
    go[:, 0:D] = (c_ref[...].astype(F32) * live).astype(BF)
    x = xs[...].astype(F32)
    inv1 = lax.rsqrt(mean_of(x * x) + EPSILON)
    mixed[:, 896:1024] = jnp.zeros((ROWS, 128), BF)
    gq[12] = jnp.zeros((ROWS, 128), F32)
    handed.wait()
    blk[...] = own_ref[...] + dot(last_rows, tail_in[...].reshape(80, 128)).astype(BF).reshape(TILES, 16, 128)
    sent = gather_into(w, blk, coords, core, send, recv, pair_send, pair_recv, own_sem)
    rs = Reduce(w, pair_buf, (b1, b2, b3, q1, q2, z2), red_ref, coords, core, rs_send, rs_recv, rp_send, rp_recv)

    def join(parts):
        return jnp.concatenate(parts, axis=0)

    def qkv_tiles(c):
        t = slice(3 * c, 3 * c + 3)
        return join([w[0, 0:2, :, :, t].reshape(768, 128), w[0, 2, 0:2, :, t].reshape(192, 128)])

    def put_qkv(c, v):
        t = slice(3 * c, 3 * c + 3)
        w[0, 0:2, :, :, t] = v[:768].reshape(2, 4, 2, 3, 16, 128)
        w[0, 2, 0:2, :, t] = v[768:].reshape(2, 2, 3, 16, 128)

    def out_tiles(c):
        t = slice(5 * c, 5 * c + 5)
        return join([w[0, 2, 2:4, :, t].reshape(320, 128), w[0, 3, :, :, t].reshape(640, 128)])

    def put_out(c, v):
        t = slice(5 * c, 5 * c + 5)
        w[0, 2, 2:4, :, t] = v[:320].reshape(2, 2, 5, 16, 128)
        w[0, 3, :, :, t] = v[320:].reshape(4, 2, 5, 16, 128)

    def in_tiles(c):
        return side([w[1:3, :, :, :, 5 * c + i].reshape(1024, 128) for i in range(5)])

    def down_tiles(c):
        return side([w[3, c, :, :, 5 * i : 5 * i + 5].reshape(640, 128) for i in range(8)])

    def side(parts):
        return jnp.concatenate(parts, axis=1)

    lane = lax.broadcasted_iota(jnp.int32, (MROWS, 128), 1)
    half = (lane < 64, lane >= 64)
    lane_all = lax.broadcasted_iota(jnp.int32, (ROWS, 128), 1)
    low_all = lane_all < 64
    first_all = lane_all % 64 < 32

    def swap(v):
        return jnp.where(first_all, pltpu.roll(v, 96, 1), pltpu.roll(v, 32, 1))

    def both(v, h):
        other = pltpu.roll(v, 64, 1)
        return jnp.where(low_all, v, other) if h == 0 else jnp.where(low_all, other, v)

    gains = w[0, 0, 0, 0, 39].astype(F32)
    gain1 = side([gains[i : i + 1] for i in range(8)])
    gain2 = side([gains[8 + i : 9 + i] for i in range(8)])
    nrm[...] = (xs[...].astype(F32) * inv1 * gain1).astype(BF)

    cos_t, sin_t = cos_ref[...], sin_ref[...]
    for c in range(0, 13, 2):
        group = [qkv_tiles(i) for i in range(c, min(c + 2, 13))]
        y2 = dot(nrm[:, 0:D], side(group))
        for i in range(len(group)):
            y = y2[:, 128 * i : 128 * i + 128]
            if c + i < 10:
                y = y * cos_t + swap(y) * sin_t
            if c + i < 8:
                qs[c + i] = y.astype(BF)
            for h in range(2):
                head = 2 * (c + i) + h
                if 15 <= head < 20:
                    kk[head - 15] = both(y, h).astype(BF)
                if 20 <= head < 25:
                    vv[head - 20] = both(y, h).astype(BF)

    zero_b = jnp.zeros((MROWS, 128), BF)

    def rows_of(m):
        return pl.ds(pl.multiple_of(m * MROWS, MROWS), MROWS)

    def chunk(head):
        return pl.ds(128 * (head // 2), 128)

    def attend(m, _):
        rows = rows_of(m)
        bias = bias_ref[rows, 0:MROWS]
        bias3 = jnp.concatenate([bias, bias, bias], axis=0)
        for g in range(KV):
            heads = [3 * g + i for i in range(3)]
            q = jnp.concatenate([jnp.where(half[h % 2], qs[h // 2, rows, :], zero_b) for h in heads], axis=0)
            s = dot(q, kk[g, rows, :], 1, 1) * 0.125 + bias3
            e = jnp.exp(s - jnp.max(s, axis=-1, keepdims=True))
            p = e / jnp.sum(e, axis=-1, keepdims=True)
            prob[m, g] = p.astype(BF)
            o = dot(p.astype(BF), vv[g, rows, :]).astype(BF)
            for i, h in enumerate(heads):
                mixed[rows, chunk(h)] = jnp.where(half[h % 2], o[MROWS * i : MROWS * i + MROWS], mixed[rows, chunk(h)])
        return 0

    lax.fori_loop(0, MB, attend, 0)

    for c in range(0, 8, 2):
        cols = slice(128 * c, 128 * c + 256)
        mid[:, cols] = xs[:, cols].astype(F32) + dot(mixed[:, 0:D], side([out_tiles(c), out_tiles(c + 1)]))
    middle = mid[...]
    inv2 = lax.rsqrt(mean_of(middle * middle) + EPSILON)
    n2b = (middle * inv2 * gain2).astype(BF)
    n2p[:, 0:128] = dot(n2b[:, 0:128], spread[0, 128:256]).astype(BF)
    for k in range(1, 8):
        n2p[:, 128 * k : 128 * k + 128] = dot(n2b[:, 128 * k - 128 : 128 * k + 128], spread[k]).astype(BF)


    def expand(c, _):
        g = dot(n2p[...], in_tiles(c))
        u = dot(n2p[...], in_tiles(c + 4))
        gate[c] = g.astype(BF)
        up[c] = u.astype(BF)
        hid[c] = (g * jax.nn.sigmoid(g) * u).astype(BF)
        return 0

    lax.fori_loop(0, 4, expand, 0)
    for copy in sent:
        copy.wait_send()
    acc[...] = mid[...]

    def reduce_(c, _):
        tiles = down_tiles(c)
        acc[...] += dot(hid[c], tiles)
        gh = dot(go[...], tiles, 1, 1)
        g, u = gate[c].astype(F32), up[c].astype(F32)
        sg = jax.nn.sigmoid(g)
        ggu[c] = (gh * u * sg * (1.0 + g * (1.0 - sg))).astype(BF)
        ggu[c + 4] = (gh * g * sg).astype(BF)
        for i in range(0, 8, 2):
            term = dot(hid[c], go[:, 128 * i : 128 * i + 256], 0, 0).astype(BF)
            for n in range(2):
                w[3, c, :, :, 5 * (i + n) : 5 * (i + n) + 5] = term[:, 128 * n : 128 * n + 128].reshape(4, 2, 5, 16, 128)
        return 0

    lax.fori_loop(0, 2, reduce_, 0)
    rs.offer(0, 3, xs=(0, 2))
    lax.fori_loop(2, 4, reduce_, 0)
    rs.offer(1, 3, xs=(2, 4))
    out_ref[...] = (acc[:, 0:D] * live).astype(BF)

    acc[...] = jnp.zeros((ROWS, 1024), F32)

    def back(c, _):
        gg = ggu[c]
        acc[...] += dot(gg, in_tiles(c), 1, 1)
        for i in range(0, 5, 2):
            term = dot(n2p[...], gg[:, 128 * i : min(128 * i + 256, 640)], 0, 0).astype(BF)
            for n in range(min(2, 5 - i)):
                w[1:3, :, :, :, 5 * c + i + n] = term[:, 128 * n : 128 * n + 128].reshape(2, 4, 4, 2, 16, 128)
        return 0

    lax.fori_loop(0, 2, back, 0)
    rs.ready(0, 3, xs=(0, 2))
    rs.ready(1, 3, xs=(2, 4))
    rs.open((3, 4), (rs.P1, rs.P2), True)
    lax.fori_loop(2, 5, back, 0)
    rs.offer(2, 1, (0, 25))
    rs.offer(3, 2, (0, 25))
    lax.fori_loop(5, 8, back, 0)
    rs.offer(4, 1, (25, 40))
    rs.offer(5, 2, (25, 40))
    rs.relay((3, 4), (rs.P1, rs.P2), True)
    rs.ready(2, 1, (0, 25))
    rs.ready(3, 2, (0, 25))
    rs.open((1, 3), (rs.P1,), True)
    gn = acc[...]
    hi = gn.astype(BF)
    lo = (gn - hi.astype(F32)).astype(BF)

    def close(k, part):
        cols = slice(128 * k, 128 * k + 128)
        return dot(hi[:, cols], spread[k, part], 1, 1) + dot(lo[:, cols], spread[k, part], 1, 1)

    before, same = slice(0, 128), slice(128, 256)
    gn = side([close(k, same) + close(k + 1, before) if k < 7 else close(k, same) for k in range(8)])
    n2 = mid[...] * inv2
    d_gain2 = jnp.sum(gn * n2, axis=0, keepdims=True)
    u = gn * gain2
    gm = go[...].astype(F32) + inv2 * (u - n2 * mean_of(u * n2))
    mid[...] = gm
    gmb = gm.astype(BF)
    gmix = jnp.zeros((ROWS, D), F32)
    for i in range(0, 8, 2):
        gmix = gmix + dot(gmb[:, 128 * i : 128 * i + 256], side([out_tiles(i), out_tiles(i + 1)]), 1, 1)
    term = dot(mixed[:, 0:D], gmb, 0, 0).astype(BF)
    for i in range(8):
        put_out(i, term[:, 128 * i : 128 * i + 128])
    rs.ready(4, 1, (25, 40))
    rs.ready(5, 2, (25, 40))
    rs.open((1, 3), (rs.P2,))
    rs.offer(8, 0, xs=(3, 4))
    mixed[:, 0:D] = gmix.astype(BF)

    def attend_back(m, _):
        rows = rows_of(m)
        for g in range(KV):
            heads = [3 * g + i for i in range(3)]
            q = jnp.concatenate([jnp.where(half[h % 2], qs[h // 2, rows, :], zero_b) for h in heads], axis=0)
            gmx = jnp.concatenate([jnp.where(half[h % 2], mixed[rows, chunk(h)], zero_b) for h in heads], axis=0)
            gv = dot(prob[m, g], gmx, 0, 0)
            p = prob[m, g].astype(F32)
            gp = dot(gmx, vv[g, rows, :], 1, 1)
            gs = (p * (gp - jnp.sum(p * gp, axis=-1, keepdims=True))).astype(BF)
            gqs = dot(gs, kk[g, rows, :]) * 0.125
            gk = dot(gs, q, 0, 0) * 0.125
            for i, h in enumerate(heads):
                gq[h // 2, rows, :] = jnp.where(half[h % 2], gqs[MROWS * i : MROWS * i + MROWS], gq[h // 2, rows, :])
            for head, value in ((15 + g, gk), (20 + g, gv)):
                value = value + pltpu.roll(value, 64, 1)
                gq[head // 2, rows, :] = jnp.where(half[head % 2], value, gq[head // 2, rows, :])
        return 0

    lax.fori_loop(0, 1, attend_back, 0)
    rs.relay((1, 3), (rs.P1,), True)
    lax.fori_loop(1, 2, attend_back, 0)
    rs.relay((1, 3), (rs.P2,))
    lax.fori_loop(2, MB, attend_back, 0)

    for c in range(13):
        y = gq[c]
        if c < 10:
            y = y * cos_t - swap(y) * sin_t
        gqb[c] = y.astype(BF)
    gn1 = jnp.zeros((ROWS, D), F32)
    for c in range(0, 13, 2):
        group = list(range(c, min(c + 2, 13)))
        gy = side([gqb[i] for i in group])
        gn1 = gn1 + dot(gy, side([qkv_tiles(i) for i in group]), 1, 1)
        term = dot(nrm[:, 0:D], gy, 0, 0).astype(BF)
        for n, i in enumerate(group):
            put_qkv(i, term[:, 128 * n : 128 * n + 128])
    acc[:, 896:1024] = jnp.zeros((ROWS, 128), F32)
    acc[:, 0:D] = gn1
    gn1 = acc[...]
    n1 = xs[...].astype(F32) * inv1
    d_gain1 = jnp.sum(gn1 * n1, axis=0, keepdims=True)
    both_gains = jnp.concatenate([v[:, 128 * i : 128 * i + 128] for v in (d_gain1, d_gain2) for i in range(8)], axis=0)
    w[0, 0, 0, 0, 39] = both_gains.astype(BF)
    rs.offer(6, 0, (0, 20), (0, 3))
    rs.offer(7, 0, (20, 40), (0, 3))
    rs.ready(8, 0, xs=(3, 4))
    u = gn1 * gain1
    res = mid[...] + inv1 * (u - n1 * mean_of(u * n1))
    gin_ref[...] = res[:, 0:D].astype(BF)
    rs.ready(6, 0, (0, 20), (0, 3))
    rs.open((0, 1), (rs.Q1,))
    rs.ready(7, 0, (20, 40), (0, 3))
    rs.open((0, 1), (rs.Q2,))
    rs.finish()
    for n in range(2):
        tail_out[n] = red_ref[pl.ds(14 + n, TILES, stride=16), :]
    handed = pltpu.make_async_remote_copy(
        src_ref=tail_out, dst_ref=tail_back, send_sem=tail_sem.at[2], recv_sem=tail_sem.at[3],
        device_id=(beside(1),), device_id_type=MESH,
    )
    handed.start()
    rs.drain()
    handed.wait()
    prev_ref[...] = tail_back[...]


def layer(block, tail, inputs, cotangent, segments, counts):
    vm = pl.BlockSpec(memory_space=pltpu.VMEM)
    dma = pltpu.SemaphoreType.DMA
    return pl.pallas_call(
        layer_kernel,
        out_shape=(
            jax.ShapeDtypeStruct((ROWS, D), BF),
            jax.ShapeDtypeStruct((ROWS, D), BF),
            jax.ShapeDtypeStruct((TILES * 16, 128), F32),
            jax.ShapeDtypeStruct((2, TILES, 128), F32),
        ),
        in_specs=[vm] * 7,
        out_specs=(vm, vm, vm, vm),
        scratch_shapes=[
            pltpu.VMEM((TILES, 16, 128), BF),
            pltpu.VMEM((5, 16, 128), BF),
            pltpu.VMEM((2, TILES, 128), F32),
            pltpu.VMEM((2, TILES, 128), F32),
            dma((4,)),
            pltpu.VMEM((4, 4, 4, 2, TILES, 16, 128), BF),
            pltpu.VMEM((3, 4, 4, TILES, 16, 128), BF),
            pltpu.VMEM((3, 4, 4, TILES, 16, 128), BF),
            pltpu.VMEM((3, 4, TILES, 16, 128), BF),
            pltpu.VMEM((3, TILES, 16, 128), BF),
            pltpu.VMEM((3, 4, TILES, 16, 128), BF),
            pltpu.VMEM((3, TILES, 16, 128), BF),
            pltpu.VMEM((3, 14, 16, 128), BF),
            pltpu.VMEM((ROWS, 1024), BF),
            pltpu.VMEM((ROWS, 1024), BF),
            pltpu.VMEM((ROWS, 1024), BF),
            pltpu.VMEM((8, ROWS, 128), BF),
            pltpu.VMEM((KV, ROWS, 128), BF),
            pltpu.VMEM((KV, ROWS, 128), BF),
            pltpu.VMEM((MB, KV, ROWS, MROWS), BF),
            pltpu.VMEM((ROWS, 1024), BF),
            pltpu.VMEM((ROWS, 1024), F32),
            pltpu.VMEM((ROWS, 1024), BF),
            pltpu.VMEM((4, ROWS, 640), BF),
            pltpu.VMEM((4, ROWS, 640), BF),
            pltpu.VMEM((4, ROWS, 640), BF),
            pltpu.VMEM((8, ROWS, 640), BF),
            pltpu.VMEM((13, ROWS, 128), F32),
            pltpu.VMEM((13, ROWS, 128), BF),
            pltpu.VMEM((8, 256, 128), BF),
            pltpu.VMEM((ROWS, 1024), F32),
            dma((99,)), dma((99,)), dma((91,)), dma((91,)), dma,
            dma((120,)), dma((120,)), dma((9,)), dma((9,)),
        ],
        compiler_params=pltpu.CompilerParams(collective_id=0, has_side_effects=True, vmem_limit_bytes=VMEM_BYTES),
    )(block, tail, inputs, cotangent, *tables(segments, counts))


def shards(inputs, cotangent, flat_weights, counts, segments):
    d = lax.axis_index("fsdp")
    block, tail = to_block(flat_weights, d)
    block_out, input_grad, rows, prev = layer(block, tail, inputs, cotangent, segments, counts)
    return block_out, input_grad, from_block(rows, prev, d)


def solution(mesh):
    in_specs = (P("fsdp", None), P("fsdp", None), P("fsdp"), P("fsdp"), P("fsdp"))
    out_specs = (P("fsdp", None), P("fsdp", None), P("fsdp"))
    return jax.shard_map(shards, mesh=mesh, in_specs=in_specs, out_specs=out_specs, check_vma=False)
```
